128 devices in a mesh: inl: 8 (over x_hi, z), xl: 16 (over x_lo, y, core).
Axes of the slice: x: 4 (x_hi: 2, x_lo: 2; x = x_hi * 2 + x_lo), y: 4, z: 4, core: 2. Of those that a mesh axis runs over, the one named last changes fastest.
Arguments:
- receiver: bfloat16 [2, 2, 4096, 4096], P(None, None, 'inl', 'xl'), may hold values from -6 to 6
- source: bfloat16 [2, 2, 4096, 4096], P(None, None, 'inl', 'xl'), may hold values from -6 to 6
- weight: int32 [4096, 4096], P('inl', 'xl'), may hold values from 0 to 4096
- omega: float32 [2], replicated, may hold values from 0.6 to 1.4
- slowness: float32 [2], replicated, may hold values from 1 to 2
- wedge_map: int32 [128, 128], replicated, may hold values from 0 to 7
Outputs:
- next_field: bfloat16 [2, 2, 4096, 4096], P(None, None, 'inl', 'xl')
- angle_gather: float32 [8, 4096], replicated
The draws below stay inside these ranges and needn't reach their ends.
Inputs may be any that keep to these rules, and one draw needn't show every extreme that they name: The weight of the first reference velocity is this value divided by 4096. `wedge_map`: tile rows follow the inline wavenumber index, tile columns the crossline one, in unshifted order.
All inputs are finite; a program needn't handle non-finite values.
Results may differ from the reference program's by a relative error of at most 0.0056.
Values may be sent and summed in bfloat16 or wider, within the bound.
No kernel may reach another device: no remote copies, remote signals or barrier semaphores. Data moves between devices by JAX's collectives and lax.ppermute only.
A program may use at most 128 MiB of HBM per device.

```python
import math
import jax
import jax.numpy as jnp
from jax import lax

NX = 4096
NY = 4096
FREQ = 2
REFS = 2
WEDGES = 8
TILE = 32


def shared_rates(key):
    omega_key = jax.random.fold_in(key, 101)
    slow_key = jax.random.fold_in(key, 102)
    omega_draw = jax.random.uniform(omega_key, (FREQ,), jnp.float32)
    slow_draw = jax.random.uniform(slow_key, (REFS,), jnp.float32)
    omega = jnp.exp(math.log(0.6) + omega_draw * (math.log(1.4) - math.log(0.6)))
    slowness = jnp.exp(slow_draw * math.log(2.0))
    return (omega, slowness)


def draw_omega(key, part):
    return shared_rates(key)[0]


def draw_slowness(key, part):
    return shared_rates(key)[1]


def draw_receiver(key, part):
    omega, slowness = shared_rates(key)
    key = jax.random.fold_in(key, 7)
    noise_key, angle_key, phase_key = jax.random.split(key, 3)
    full_shape = (2, FREQ, NX, NY)
    noise_field = jax.random.normal(noise_key, full_shape, jnp.float32)
    radius = omega[:, None] * slowness[None, :]
    angles = jax.random.uniform(angle_key, (FREQ, REFS, 4), jnp.float32, -math.pi, math.pi)
    offset = jax.random.uniform(phase_key, (FREQ, REFS, 4), jnp.float32, -math.pi, math.pi)
    bins_x = jnp.floor(radius[:, :, None] * jnp.cos(angles) * (NX / (2.0 * math.pi)) + 0.5).astype(jnp.int32)
    bins_y = jnp.floor(radius[:, :, None] * jnp.sin(angles) * (NY / (2.0 * math.pi)) + 0.5).astype(jnp.int32)
    row_index = jnp.arange(NX, dtype=jnp.int32)
    col_index = jnp.arange(NY, dtype=jnp.int32)
    real_sum = jnp.zeros((FREQ, NX, NY), jnp.float32)
    imag_sum = jnp.zeros((FREQ, NX, NY), jnp.float32)
    for ref_index in range(REFS):
        for wave_index in range(4):
            turn_x = (bins_x[:, ref_index, wave_index][:, None] * row_index[None, :] % NX).astype(jnp.float32) / NX
            turn_y = (bins_y[:, ref_index, wave_index][:, None] * col_index[None, :] % NY).astype(jnp.float32) / NY
            argument = 2.0 * math.pi * (turn_x[:, :, None] + turn_y[:, None, :]) + offset[:, ref_index, wave_index][:, None, None]
            real_sum = real_sum + 0.5 * jnp.cos(argument)
            imag_sum = imag_sum + 0.5 * jnp.sin(argument)
    waves = jnp.stack([real_sum, imag_sum])
    return jnp.clip(noise_field + waves, -6.0, 6.0).astype(jnp.bfloat16)


def touch_ends(values, stream_key, smallest, largest):
    spot = [jax.random.randint(jax.random.fold_in(stream_key, axis), (), 0, length) for axis, length in enumerate(values.shape)]
    widest = values.shape.index(max(values.shape))
    neighbour = spot[:widest] + [(spot[widest] + 1) % values.shape[widest]] + spot[widest + 1:]
    return values.at[tuple(spot)].set(smallest).at[tuple(neighbour)].set(largest)


def block_scale(key, shape, cuts, least, high):
    def one(dim, parts):
        steps = jax.random.uniform(jax.random.fold_in(jax.random.fold_in(key, 6), dim), (parts,), jnp.float32, least / len(cuts), high / len(cuts))
        return jnp.repeat(jnp.exp(steps), shape[dim] // parts).reshape((-1,) + (1,) * (len(shape) - dim - 1))

    gain = one(*cuts[0])
    for cut in cuts[1:]:
        gain = gain * one(*cut)
    return gain


def centred(stream_key, dims, deviation, most, cuts=(), kind=jnp.bfloat16):
    factor_of = block_scale(stream_key, dims, cuts, -0.22, 0.18) if cuts else 1.0
    array = jax.random.normal(stream_key, dims, jnp.float32) * deviation * factor_of
    return jnp.minimum(jnp.maximum(array, -most), most).astype(kind)


def setup_inputs(seed: int = 0) -> dict:
    streams_of = jax.random.split(jax.random.key(seed), 7)
    receiver = draw_receiver(jax.random.fold_in(streams_of[6], 71), 0)
    source = centred(streams_of[1], (2, FREQ, NX, NY), 1.0, 6.0, ((2, 8), (3, 16)))
    weight = touch_ends(jax.random.randint(streams_of[2], (NX, NY), 0, 4097), jax.random.fold_in(streams_of[2], 1), 0, 4096).astype(jnp.int32)
    omega = draw_omega(jax.random.fold_in(streams_of[6], 71), 0)
    slowness = draw_slowness(jax.random.fold_in(streams_of[6], 71), 0)
    wedge_map = touch_ends(jax.random.randint(streams_of[5], (NX // TILE, NY // TILE), 0, WEDGES), jax.random.fold_in(streams_of[5], 1), 0, WEDGES - 1).astype(jnp.int32)
    return dict(receiver=receiver, source=source, weight=weight, omega=omega, slowness=slowness, wedge_map=wedge_map)


def settle(values):
    return lax.optimization_barrier(values.astype(jnp.bfloat16)).astype(jnp.float32)

def rounded(wave):
    return lax.complex(settle(jnp.real(wave)), settle(jnp.imag(wave)))

def wavenumbers(length):
    index = jnp.arange(length, dtype=jnp.int32)
    index = jnp.where(index >= length // 2, index - length, index)
    return 2.0 * math.pi / length * index.astype(jnp.float32)

def reference(receiver, source, weight, omega, slowness, wedge_map):
    kx = wavenumbers(NX)[:, None]
    ky = wavenumbers(NY)[None, :]
    kx_sq = kx * kx
    ky_sq = ky * ky
    share = weight.astype(jnp.float32) / 4096.0

    def forward(field):
        wave = lax.complex(field[0].astype(jnp.float32), field[1].astype(jnp.float32))
        lines = rounded(jnp.fft.fft(wave, axis=1))
        return jnp.fft.fft(lines, axis=0)

    def one_freq(items):
        rec, src, freq = items
        spec_rec = forward(rec)
        spec_src = forward(src)
        term = jnp.real(jnp.conj(spec_src) * spec_rec)
        continued = []
        for ref in range(REFS):
            number = freq * slowness[ref]
            quad = number * number - kx_sq - ky_sq
            root = jnp.sqrt(jnp.abs(quad))
            real_part = jnp.where(quad >= 0, jnp.cos(root), jnp.exp(-root))
            imag_part = jnp.where(quad >= 0, jnp.sin(root), 0.0)
            phase = lax.complex(real_part, imag_part)
            partial_value = rounded(jnp.fft.ifft(spec_rec * phase, axis=0))
            back = jnp.fft.ifft(partial_value, axis=1)
            continued.append((settle(jnp.real(back)), settle(jnp.imag(back))))
        next_re = share * continued[0][0] + (1.0 - share) * continued[1][0]
        next_im = share * continued[0][1] + (1.0 - share) * continued[1][1]
        tile_sums = term.reshape(NX, NY // TILE, TILE).sum(axis=-1)
        return (jnp.stack([next_re, next_im]).astype(jnp.bfloat16), tile_sums)
    nexts, sums = lax.map(one_freq, (jnp.moveaxis(receiver, 1, 0), jnp.moveaxis(source, 1, 0), omega))
    next_field = jnp.moveaxis(nexts, 0, 1)
    total = lax.optimization_barrier(jnp.sum(sums, axis=0))
    tile_rows = jnp.repeat(wedge_map, TILE, axis=0)
    scale = 1.0 / (NX * NY * math.sqrt(NY))
    angle_gather = jnp.stack([lax.optimization_barrier(jnp.sum(jnp.where(tile_rows == wedge, total, 0.0), axis=1)) for wedge in range(WEDGES)]) * scale
    return (next_field, angle_gather)
```

```python
import functools
import math

import jax
import jax.numpy as jnp
import ml_dtypes
import numpy as np
from jax import lax
from jax.experimental import pallas as pl
from jax.experimental.pallas import tpu as pltpu
from jax.sharding import PartitionSpec as P

SIZE = 4096
DEVICES = 128
GROUP = 16
BF16 = jnp.bfloat16
F32 = jnp.float32
EVERY = ("inl", "xl")
HALF = math.sqrt(0.5)


def roots(rows, cols, length, sign):
    turn = np.outer(np.arange(rows), np.arange(cols)) % length
    return np.exp(sign * 2j * np.pi * turn / length)


def as_block(matrix):
    return np.block([[matrix.real, matrix.imag], [-matrix.imag, matrix.real]])


def two_parts(matrix):
    high = matrix.astype(np.float32).astype(ml_dtypes.bfloat16)
    low = (matrix - high.astype(np.float64)).astype(np.float32).astype(ml_dtypes.bfloat16)
    return high, low


def pair_table(values):
    return np.stack([values.real, values.imag]).astype(np.float32)


@functools.lru_cache(None)
def tables():
    out = {}
    high, low = two_parts(as_block(roots(128, 128, 128, -1)).T)
    out["cross_fwd"] = np.concatenate([high, high, low], axis=1)
    high, low = two_parts(as_block(roots(128, 128, 128, 1)) / SIZE)
    out["cross_inv"] = np.concatenate([high, low], axis=0)
    out["cross_tw_fwd"] = pair_table(roots(32, 128, SIZE, -1))
    out["cross_tw_inv"] = pair_table(roots(32, 128, SIZE, 1))
    for name, sign, scale in (("fwd", -1, 1.0), ("inv", 1, 1.0 / SIZE)):
        lanes = np.kron(np.eye(4), roots(32, 32, 32, sign))
        high, low = two_parts(as_block(lanes) * scale)
        out["inline_" + name] = np.concatenate([high, high, low], axis=0)
        out["inline_tw_" + name] = pair_table(np.tile(roots(128, 32, SIZE, sign), (1, 4)))
    return out


def add(x, y):
    return (x[0] + y[0], x[1] + y[1])


def sub(x, y):
    return (x[0] - y[0], x[1] - y[1])


def times(x, y):
    return (x[0] * y[0] - x[1] * y[1], x[0] * y[1] + x[1] * y[0])


def turn(x, numerator, length, sign):
    eighth = 8 * (numerator % length) * sign % (8 * length)
    if eighth % length:
        angle = sign * 2.0 * math.pi * (numerator % length) / length
        c, s = math.cos(angle), math.sin(angle)
        return (x[0] * c - x[1] * s, x[0] * s + x[1] * c)
    eighth = eighth // length
    r, i = x
    if eighth == 0:
        return x
    if eighth == 1:
        return ((r - i) * HALF, (r + i) * HALF)
    if eighth == 2:
        return (-i, r)
    if eighth == 3:
        return ((r + i) * -HALF, (r - i) * HALF)
    if eighth == 4:
        return (-r, -i)
    if eighth == 5:
        return ((i - r) * HALF, (r + i) * -HALF)
    if eighth == 6:
        return (i, -r)
    return ((r + i) * HALF, (i - r) * HALF)


def dft(x, sign):
    length = len(x)
    if length == 2:
        return [add(x[0], x[1]), sub(x[0], x[1])]
    if length == 4:
        t0, t1 = add(x[0], x[2]), sub(x[0], x[2])
        t2, t3 = add(x[1], x[3]), sub(x[1], x[3])
        r, i = t3
        if sign < 0:
            return [add(t0, t2), (t1[0] + i, t1[1] - r), sub(t0, t2), (t1[0] - i, t1[1] + r)]
        return [add(t0, t2), (t1[0] - i, t1[1] + r), sub(t0, t2), (t1[0] + i, t1[1] - r)]
    first = {8: 2, 16: 4, 32: 8}[length]
    second = length // first
    inner = [dft(x[low::second], sign) for low in range(second)]
    out = [None] * length
    for q in range(first):
        row = [turn(inner[low][q], low * q, length, sign) for low in range(second)]
        for p, value in enumerate(dft(row, sign)):
            out[q + first * p] = value
    return out


def dft128(load, store, work, sign):
    for low in range(8):
        values = dft([load(8 * high + low) for high in range(16)], sign)
        for q in range(16):
            r, i = turn(values[q], low * q, 128, sign)
            work[q * 8 + low, 0] = r
            work[q * 8 + low, 1] = i
    for q in range(16):
        values = dft([(work[q * 8 + low, 0], work[q * 8 + low, 1]) for low in range(8)], sign)
        for p in range(8):
            store(q + 16 * p, values[p])


def split(value):
    high = value.astype(BF16)
    low = (value - high.astype(F32)).astype(BF16)
    return jnp.concatenate([high, low, high], axis=1)


def dot(x, y, dims=((1,), (0,))):
    return lax.dot_general(x, y, (dims, ((), ())), preferred_element_type=F32)


def pack_kernel(receiver, source, weight, out):
    for which, field in enumerate((receiver, source)):
        for part in range(2):
            row = which * 64 + part * 32
            out[:, row : row + 32, :] = field[part, 0]
    value = weight[:, 0]
    high = value >> 7
    code = 1.0 + (value & 127).astype(F32) * (1.0 / 128.0)
    for power in (1, 2, 4, 8, 16, 32):
        code = code * jnp.where((high & power) != 0, 2.0**power, 1.0)
    out[:, 128:144, :] = code.astype(BF16)


def phase_kernel(place, omega, slowness, wedge_map, phase, wedges):
    freq = pl.program_id(0)
    device = place[0]
    step = 2.0 * math.pi / SIZE

    def signed(index):
        index = jnp.where(index >= SIZE // 2, index - SIZE, index)
        return step * index.astype(F32)

    def body(part, carry):
        row = part * 64 + lax.broadcasted_iota(jnp.int32, (64, 128), 0)
        lane = lax.broadcasted_iota(jnp.int32, (64, 128), 1)
        kx = signed((row >> 3) + 128 * (lane & 31))
        ky = signed(device * 32 + 4 * (row & 7) + (lane >> 5))
        kx_sq = kx * kx
        ky_sq = ky * ky
        rows = pl.ds(pl.multiple_of(part * 64, 64), 64)
        for ref in range(2):
            number = omega[freq] * slowness[ref]
            quad = number * number - kx_sq - ky_sq
            root = jnp.sqrt(jnp.abs(quad))
            decay = jnp.exp(-root)
            inside = jnp.maximum(quad, 0.0)
            even = jnp.full_like(quad, 1.0 / math.factorial(22))
            odd = jnp.full_like(quad, 1.0 / math.factorial(23))
            for n in range(10, -1, -1):
                even = 1.0 / math.factorial(2 * n) - inside * even
                odd = 1.0 / math.factorial(2 * n + 1) - inside * odd
            phase[0, ref, 0, rows, :] = jnp.where(quad >= 0, even, decay)
            phase[0, ref, 1, rows, :] = jnp.where(quad >= 0, odd * root, 0.0)
        return carry

    lax.fori_loop(0, 16, body, 0)

    @pl.when(freq == 0)
    def _():
        rows = wedge_map[pl.ds(place[1] // 4, 32, stride=4), :].astype(F32)
        wedges[...] = jnp.concatenate([rows] * 4, axis=0).T


def cross_forward_kernel(lines, twist, matrix, out, mid, turned):
    def field(which, carry):
        for part in range(2):
            values = []
            for a in range(32):
                lanes = pl.ds((a % 2) * 128, 128)
                pair = []
                for side in range(2):
                    row = pl.multiple_of(which * 64 + side * 32 + part * 16, 16)
                    pair.append(lines[a // 2, pl.ds(row, 16), lanes].astype(F32))
                values.append(tuple(pair))
            for k, value in enumerate(dft(values, -1)):
                r, i = times(value, (twist[0, k : k + 1, :], twist[1, k : k + 1, :]))
                row = k * 32 + part * 16
                mid[row : row + 16, 0:128] = r
                mid[row : row + 16, 128:256] = i
        for part in range(4):
            parts = split(mid[part * 256 : part * 256 + 256, :])
            value = dot(matrix[...], parts, ((1,), (1,)))
            for side in range(2):
                for half in range(2):
                    turned[pl.ds(side * 8 + part * 2 + half, 128, stride=16), :] = value[
                        side * 128 : side * 128 + 128, half * 128 : half * 128 + 128
                    ]
        rows = pl.ds(pl.multiple_of(which * 16, 16), 16)
        out[:, rows, :] = turned[...].reshape(128, 16, 128).astype(BF16)
        return carry

    lax.fori_loop(0, 2, field, 0)


def inline_kernel(
    lines, phase, twist, twist_inv, matrix, matrix_inv, out, work, mid, spec, term
):
    freq = pl.program_id(0)

    def forward(which, carry):
        rows = pl.ds(pl.multiple_of(which * 16, 16), 16)

        def load(s):
            value = lines[s, rows, :].astype(F32)
            return (value[0:8], value[8:16])

        def store(k, value):
            r, i = times(value, (twist[0, k : k + 1, :], twist[1, k : k + 1, :]))
            mid[8 * k : 8 * k + 8, 0:128] = r
            mid[8 * k : 8 * k + 8, 128:256] = i

        dft128(load, store, work, -1)
        for part in range(4):
            block = slice(part * 256, part * 256 + 256)
            spec[which, block, :] = dot(split(mid[block, :]), matrix[...])
        return carry

    lax.fori_loop(0, 2, forward, 0)

    @pl.when(freq == 0)
    def _():
        term[...] = jnp.zeros_like(term)

    for part in range(4):
        block = slice(part * 256, part * 256 + 256)
        both = spec[0, block, :] * spec[1, block, :]
        term[block, :] += both[:, 0:128] + both[:, 128:256]

    def inverse(ref, carry):
        for part in range(4):
            block = slice(part * 256, part * 256 + 256)
            value = (spec[0, block, 0:128], spec[0, block, 128:256])
            turned = times(value, (phase[0, ref, 0, block, :], phase[0, ref, 1, block, :]))
            mid[block, :] = dot(split(jnp.concatenate(turned, axis=1)), matrix_inv[...])

        def load(k):
            value = (mid[8 * k : 8 * k + 8, 0:128], mid[8 * k : 8 * k + 8, 128:256])
            return times(value, (twist_inv[0, k : k + 1, :], twist_inv[1, k : k + 1, :]))

        rows = pl.ds(pl.multiple_of(freq * 32 + ref * 16, 16), 16)

        def store(s, value):
            out[s, rows, :] = jnp.concatenate(value, axis=0).astype(BF16)

        dft128(load, store, work, 1)
        return carry

    lax.fori_loop(0, 2, inverse, 0)

    @pl.when(freq == 1)
    def _():
        total = term[...].reshape(128, 8, 128).sum(axis=1)
        total = total + pltpu.roll(total, 64, 1)
        total = total + pltpu.roll(total, 32, 1)
        high = total.astype(BF16).astype(F32)
        rest = total - high
        middle = rest.astype(BF16).astype(F32)
        low = rest - middle
        place = lax.broadcasted_iota(jnp.int32, (128, 128), 1) >> 5
        value = jnp.where(place == 0, high, jnp.where(place == 1, middle, low))
        value = jnp.where(place == 3, 0.0, value).reshape(16, 8, 128).astype(BF16)
        for group in range(8):
            out[group * 16 : group * 16 + 16, 64:72, :] = value


def cross_inverse_kernel(
    lines, sums, wedges, weight_one, weight_two, twist, matrix, out, flat, mid, kept, share
):
    freq = pl.program_id(0)

    @pl.when(freq == 0)
    def _():
        for half, coded in enumerate((weight_one, weight_two)):
            value = coded[...].astype(F32)
            high = jnp.zeros_like(value)
            for power in (32, 16, 8, 4, 2, 1):
                over = value >= 2.0**power
                value = jnp.where(over, value * 2.0**-power, value)
                high = jnp.where(over, high + float(power), high)
            share[:, half * 16 : half * 16 + 16, :] = (high + (value - 1.0)) * (1.0 / 32.0)

        def gather(d, totals):
            value = sums[d].astype(F32)
            where = wedges[pl.ds(d, 1), :]
            return tuple(
                total + jnp.where(where == float(w), value, 0.0) for w, total in enumerate(totals)
            )

        zero = jnp.zeros((8, 128), F32)
        totals = lax.fori_loop(0, 128, gather, (zero,) * 8, unroll=8)
        highs, lows = [], []
        for total in totals:
            total = total + pltpu.roll(total, 64, 1)
            total = total + pltpu.roll(total, 32, 1)
            total = total * (1.0 / (SIZE * SIZE * math.sqrt(SIZE)))
            highs.append(total.astype(BF16).astype(F32))
            lows.append(total - highs[-1])
        place = lax.broadcasted_iota(jnp.int32, (8, 128), 1) >> 5
        for half in range(2):
            rows = []
            for first in (half * 2, half * 2 + 4):
                even = jnp.where(place == 0, highs[first], lows[first])
                odd = jnp.where(place == 2, highs[first + 1], lows[first + 1])
                rows.append(jnp.where(place < 2, even, odd))
            value = jnp.concatenate(rows, axis=0).astype(BF16)
            for group in range(16):
                out[group, 128:144, half * 128 : half * 128 + 128] = value

    for ref in range(2):
        flat[...] = lines[:, ref * 16 : ref * 16 + 16, :].astype(F32).reshape(2048, 128)
        for g in range(8):
            pair = [flat[pl.ds(side * 8 + g, 128, stride=16), :] for side in range(2)]
            value = jnp.concatenate([x.T for x in pair], axis=1).astype(BF16)
            mid[g * 128 : g * 128 + 128, :] = dot(
                jnp.concatenate([value, value], axis=1), matrix[...]
            )

        def rows16(part, carry):
            start = pl.multiple_of(part * 16, 16)
            values = []
            for k in range(32):
                rows = pl.ds(pl.multiple_of(k * 32 + part * 16, 16), 16)
                values.append(
                    times(
                        (mid[rows, 0:128], mid[rows, 128:256]),
                        (twist[0, k : k + 1, :], twist[1, k : k + 1, :]),
                    )
                )
            for a, value in enumerate(dft(values, 1)):
                lanes = slice((a % 2) * 128, (a % 2) * 128 + 128)
                for side in range(2):
                    rounded = value[side].astype(BF16)
                    if ref == 0:
                        kept[a, side, pl.ds(start, 16), :] = rounded
                    else:
                        s = share[a // 2, pl.ds(start, 16), lanes]
                        first = kept[a, side, pl.ds(start, 16), :].astype(F32)
                        mixed = first * s + rounded.astype(F32) * (1.0 - s)
                        row = pl.multiple_of(freq * 64 + side * 32 + part * 16, 16)
                        out[a // 2, pl.ds(row, 16), lanes] = mixed.astype(BF16)
            return carry

        lax.fori_loop(0, 2, rows16, 0)


def unpack_kernel(block, coded, out, angles):
    out[0, 0] = block[...]

    @pl.when(pl.program_id(0) == 0)
    def _():
        value = coded[...].astype(F32)
        for half in range(2):
            for top in range(2):
                part = value[:, top * 8 : top * 8 + 8, half * 128 : half * 128 + 128]
                flipped = part.reshape(128, 128).T
                w = top * 4 + half * 2
                angles[w] = flipped[0:32] + flipped[32:64]
                angles[w + 1] = flipped[64:96] + flipped[96:128]


def whole(shape):
    return pl.BlockSpec(shape, lambda *_: (0,) * len(shape))


def fixed(shape, index):
    return pl.BlockSpec(shape, lambda *_: index)


def params():
    return pltpu.CompilerParams(vmem_limit_bytes=56 * 2**20)


def pack(receiver, source, weight):
    field = pl.BlockSpec((2, 1, GROUP, 32, 256), lambda f: (0, f, 0, 0, 0))
    return pl.pallas_call(
        pack_kernel,
        grid=(2,),
        in_specs=[field, field, pl.BlockSpec((GROUP, 1, 16, 256), lambda f: (0, f, 0, 0))],
        out_specs=pl.BlockSpec((GROUP, 144, 256), lambda f: (0, f, 0)),
        out_shape=jax.ShapeDtypeStruct((GROUP, 288, 256), BF16),
        compiler_params=params(),
        name="pack_fields",
    )(
        receiver.reshape(2, 2, GROUP, 32, 256),
        source.reshape(2, 2, GROUP, 32, 256),
        weight.reshape(GROUP, 2, 16, 256),
    )


def phases(place, omega, slowness, wedge_map):
    scalar = pl.BlockSpec(memory_space=pltpu.SMEM)
    return pl.pallas_call(
        phase_kernel,
        grid=(2,),
        in_specs=[scalar, scalar, scalar, whole((128, 128))],
        out_specs=[
            pl.BlockSpec((1, 2, 2, 1024, 128), lambda f: (f, 0, 0, 0, 0)),
            whole((128, 128)),
        ],
        out_shape=[
            jax.ShapeDtypeStruct((2, 2, 2, 1024, 128), F32),
            jax.ShapeDtypeStruct((128, 128), F32),
        ],
        compiler_params=params(),
        name="phase_table",
    )(place, omega, slowness, wedge_map)


def cross_forward(packed):
    t = tables()
    return pl.pallas_call(
        cross_forward_kernel,
        grid=(2,),
        in_specs=[
            pl.BlockSpec((GROUP, 144, 256), lambda f: (0, f, 0)),
            whole((2, 32, 128)),
            whole((256, 768)),
        ],
        out_specs=pl.BlockSpec((DEVICES, 32, 128), lambda f: (0, f, 0)),
        out_shape=jax.ShapeDtypeStruct((DEVICES, 64, 128), BF16),
        scratch_shapes=[pltpu.VMEM((1024, 256), F32), pltpu.VMEM((2048, 128), F32)],
        compiler_params=params(),
        name="crossline_forward",
    )(packed, jnp.asarray(t["cross_tw_fwd"]), jnp.asarray(t["cross_fwd"]))


def inline_step(lines, phase):
    t = tables()
    return pl.pallas_call(
        inline_kernel,
        grid=(2,),
        in_specs=[
            pl.BlockSpec((DEVICES, 32, 128), lambda f: (0, f, 0)),
            pl.BlockSpec((1, 2, 2, 1024, 128), lambda f: (f, 0, 0, 0, 0)),
            whole((2, 128, 128)),
            whole((2, 128, 128)),
            whole((768, 256)),
            whole((768, 256)),
        ],
        out_specs=whole((DEVICES, 72, 128)),
        out_shape=jax.ShapeDtypeStruct((DEVICES, 72, 128), BF16),
        scratch_shapes=[
            pltpu.VMEM((128, 2, 8, 128), F32),
            pltpu.VMEM((1024, 256), F32),
            pltpu.VMEM((2, 1024, 256), F32),
            pltpu.VMEM((1024, 128), F32),
        ],
        compiler_params=params(),
        name="inline_step",
    )(
        lines,
        phase,
        jnp.asarray(t["inline_tw_fwd"]),
        jnp.asarray(t["inline_tw_inv"]),
        jnp.asarray(t["inline_fwd"]),
        jnp.asarray(t["inline_inv"]),
    )


def cross_inverse(partial, wedges, packed):
    t = tables()
    return pl.pallas_call(
        cross_inverse_kernel,
        grid=(2,),
        in_specs=[
            pl.BlockSpec((DEVICES, 32, 128), lambda f: (0, f, 0)),
            fixed((DEVICES, 8, 128), (0, 8, 0)),
            whole((128, 128)),
            fixed((GROUP, 16, 256), (0, 8, 0)),
            fixed((GROUP, 16, 256), (0, 17, 0)),
            whole((2, 32, 128)),
            whole((512, 256)),
        ],
        out_specs=whole((GROUP, 144, 256)),
        out_shape=jax.ShapeDtypeStruct((GROUP, 144, 256), BF16),
        scratch_shapes=[
            pltpu.VMEM((2048, 128), F32),
            pltpu.VMEM((1024, 256), F32),
            pltpu.VMEM((32, 2, 32, 128), BF16),
            pltpu.VMEM((GROUP, 32, 256), F32),
        ],
        compiler_params=params(),
        name="crossline_inverse",
    )(
        partial,
        partial,
        wedges,
        packed,
        packed,
        jnp.asarray(t["cross_tw_inv"]),
        jnp.asarray(t["cross_inv"]),
    )


def unpack(home):
    return pl.pallas_call(
        unpack_kernel,
        grid=(4,),
        in_specs=[
            pl.BlockSpec((GROUP, 32, 256), lambda c: (0, c, 0)),
            fixed((GROUP, 16, 256), (0, 8, 0)),
        ],
        out_specs=[
            pl.BlockSpec((1, 1, GROUP, 32, 256), lambda c: (c % 2, c // 2, 0, 0, 0)),
            whole((8, 32, 128)),
        ],
        out_shape=[
            jax.ShapeDtypeStruct((2, 2, GROUP, 32, 256), BF16),
            jax.ShapeDtypeStruct((8, 32, 128), F32),
        ],
        compiler_params=params(),
        name="unpack_fields",
    )(home, home)


def exchange(value, axes):
    return lax.all_to_all(value, axes, 0, 0, tiled=True)


def per_device(receiver, source, weight, omega, slowness, wedge_map):
    line = lax.axis_index("xl")
    place = jnp.stack([lax.axis_index("inl") * GROUP + line, line]).astype(jnp.int32)
    packed = exchange(pack(receiver, source, weight), "xl")
    phase, wedges = phases(place, omega, slowness, wedge_map)
    lines = exchange(cross_forward(packed), EVERY)
    partial = exchange(inline_step(lines, phase), EVERY)
    home = exchange(cross_inverse(partial, wedges, packed), "xl")
    mixed, angles = unpack(home)
    return (mixed.reshape(2, 2, 512, 256), angles.reshape(8, SIZE))


def solution(mesh):
    return jax.shard_map(
        per_device,
        mesh=mesh,
        in_specs=(
            P(None, None, "inl", "xl"),
            P(None, None, "inl", "xl"),
            P("inl", "xl"),
            P(),
            P(),
            P(),
        ),
        out_specs=(P(None, None, "inl", "xl"), P()),
        check_vma=False,
    )
```

```python
import functools
import math

import jax
import jax.numpy as jnp
import ml_dtypes
import numpy as np
from jax import lax
from jax.experimental import pallas as pl
from jax.experimental.pallas import tpu as pltpu
from jax.sharding import Mesh
from jax.sharding import PartitionSpec as P

SIZE = 4096
DEVICES = 128
GROUP = 16
BF16 = jnp.bfloat16
F32 = jnp.float32
NAMES = ("x_hi", "z", "x_lo", "y", "core")
LINE = ("y", "x_lo", "core")
EVERY = ("x_lo", "x_hi", "z", "y", "core")
HALF = math.sqrt(0.5)


def line_rank(block):
    high, rest = divmod(block, 8)
    return rest // 2 * 4 + high * 2 + rest % 2


def every_rank(block):
    group, line = divmod(block, GROUP)
    return line // 2 % 2 * 64 + group * 8 + line // 4 * 2 + line % 2


def roots(rows, cols, length, sign):
    turn = np.outer(np.arange(rows), np.arange(cols)) % length
    return np.exp(sign * 2j * np.pi * turn / length)


def as_block(matrix):
    return np.block([[matrix.real, matrix.imag], [-matrix.imag, matrix.real]])


def two_parts(matrix):
    high = matrix.astype(np.float32).astype(ml_dtypes.bfloat16)
    low = (matrix - high.astype(np.float64)).astype(np.float32).astype(ml_dtypes.bfloat16)
    return high, low


def pair_table(values):
    return np.stack([values.real, values.imag]).astype(np.float32)


@functools.lru_cache(None)
def tables():
    out = {}
    high, low = two_parts(as_block(roots(128, 128, 128, -1)).T)
    out["cross_fwd"] = np.concatenate([high, high, low], axis=1)
    high, low = two_parts(as_block(roots(128, 128, 128, 1)) / SIZE)
    out["cross_inv"] = np.concatenate([high, low], axis=0)
    out["cross_tw_fwd"] = pair_table(roots(32, 128, SIZE, -1))
    out["cross_tw_inv"] = pair_table(roots(32, 128, SIZE, 1))
    for name, sign, scale in (("fwd", -1, 1.0), ("inv", 1, 1.0 / SIZE)):
        lanes = np.kron(np.eye(4), roots(32, 32, 32, sign))
        high, low = two_parts(as_block(lanes) * scale)
        out["inline_" + name] = np.concatenate([high, high, low], axis=0)
        out["inline_tw_" + name] = pair_table(np.tile(roots(128, 32, SIZE, sign), (1, 4)))
    return out


def add(x, y):
    return (x[0] + y[0], x[1] + y[1])


def sub(x, y):
    return (x[0] - y[0], x[1] - y[1])


def times(x, y):
    return (x[0] * y[0] - x[1] * y[1], x[0] * y[1] + x[1] * y[0])


def turn(x, numerator, length, sign):
    eighth = 8 * (numerator % length) * sign % (8 * length)
    if eighth % length:
        angle = sign * 2.0 * math.pi * (numerator % length) / length
        c, s = math.cos(angle), math.sin(angle)
        return (x[0] * c - x[1] * s, x[0] * s + x[1] * c)
    eighth = eighth // length
    r, i = x
    if eighth == 0:
        return x
    if eighth == 1:
        return ((r - i) * HALF, (r + i) * HALF)
    if eighth == 2:
        return (-i, r)
    if eighth == 3:
        return ((r + i) * -HALF, (r - i) * HALF)
    if eighth == 4:
        return (-r, -i)
    if eighth == 5:
        return ((i - r) * HALF, (r + i) * -HALF)
    if eighth == 6:
        return (i, -r)
    return ((r + i) * HALF, (i - r) * HALF)


def dft(x, sign):
    length = len(x)
    if length == 2:
        return [add(x[0], x[1]), sub(x[0], x[1])]
    if length == 4:
        t0, t1 = add(x[0], x[2]), sub(x[0], x[2])
        t2, t3 = add(x[1], x[3]), sub(x[1], x[3])
        r, i = t3
        if sign < 0:
            return [add(t0, t2), (t1[0] + i, t1[1] - r), sub(t0, t2), (t1[0] - i, t1[1] + r)]
        return [add(t0, t2), (t1[0] - i, t1[1] + r), sub(t0, t2), (t1[0] + i, t1[1] - r)]
    first = {8: 2, 16: 4, 32: 8}[length]
    second = length // first
    inner = [dft(x[low::second], sign) for low in range(second)]
    out = [None] * length
    for q in range(first):
        row = [turn(inner[low][q], low * q, length, sign) for low in range(second)]
        for p, value in enumerate(dft(row, sign)):
            out[q + first * p] = value
    return out


def split(value):
    high = value.astype(BF16)
    low = (value - high.astype(F32)).astype(BF16)
    return jnp.concatenate([high, low, high], axis=1)


def dot(x, y, dims=((1,), (0,))):
    return lax.dot_general(x, y, (dims, ((), ())), preferred_element_type=F32)


def pack_kernel(receiver, source, weight, out, raw, sems):
    copies = [pltpu.make_async_copy(weight, raw, sems.at[8])]
    for which, field in enumerate((receiver, source)):
        for part in range(2):
            for freq in range(2):
                rows = pl.ds(freq * 144 + which * 64 + part * 32, 32)
                sem = sems.at[which * 4 + part * 2 + freq]
                copies.append(
                    pltpu.make_async_copy(field.at[part, freq], out.at[:, rows, :], sem)
                )
    for copy in copies:
        copy.start()
    copies[0].wait()
    for freq in range(2):
        value = raw[:, freq]
        high = value >> 7
        code = 1.0 + (value & 127).astype(F32) * (1.0 / 128.0)
        for power in (1, 2, 4, 8, 16, 32):
            code = code * jnp.where((high & power) != 0, 2.0**power, 1.0)
        out[:, freq * 144 + 128 : freq * 144 + 144, :] = code.astype(BF16)
    for copy in copies[1:]:
        copy.wait()


def phase_kernel(omega, slowness, wedge_map, phase, wedges):
    x_hi, z, x_lo, y, core = (lax.axis_index(name) for name in NAMES)
    device = ((x_lo * 2 + x_hi) * 4 + z) * 8 + y * 2 + core
    step = 2.0 * math.pi / SIZE

    def signed(index):
        index = jnp.where(index >= SIZE // 2, index - SIZE, index)
        return step * index.astype(F32)

    def body(part, carry):
        row = part * 64 + lax.broadcasted_iota(jnp.int32, (64, 128), 0)
        lane = lax.broadcasted_iota(jnp.int32, (64, 128), 1)
        kx = signed((row >> 6) + 16 * ((row >> 3) & 7) + 128 * (lane & 31))
        ky = signed(device * 32 + (row & 7) + 8 * (lane >> 5))
        kx_sq = kx * kx
        ky_sq = ky * ky
        rows = pl.ds(pl.multiple_of(part * 64, 64), 64)
        for freq in range(2):
            for ref in range(2):
                number = omega[freq] * slowness[ref]
                quad = number * number - kx_sq - ky_sq
                root = jnp.sqrt(jnp.abs(quad))
                decay = jnp.exp(-root)
                inside = jnp.maximum(quad, 0.0)
                even = jnp.full_like(quad, 1.0 / math.factorial(22))
                odd = jnp.full_like(quad, 1.0 / math.factorial(23))
                for n in range(10, -1, -1):
                    even = 1.0 / math.factorial(2 * n) - inside * even
                    odd = 1.0 / math.factorial(2 * n + 1) - inside * odd
                phase[freq, ref, 0, rows, :] = jnp.where(quad >= 0, even, decay)
                phase[freq, ref, 1, rows, :] = jnp.where(quad >= 0, odd * root, 0.0)
        return carry

    lax.fori_loop(0, 16, body, 0)
    rows = wedge_map[pl.ds(y, 32, stride=4), :].astype(F32)
    wedges[...] = jnp.concatenate([rows] * 4, axis=0).T


def cross_forward_kernel(lines, twist, table, out, matrix, work, turned, ready, sem, sems):
    fetch = pltpu.make_async_copy(table, matrix, sem)
    fetch.start()

    def send(index):
        rows = pl.ds(pl.multiple_of(index * 16, 16), 16)
        return pltpu.make_async_copy(ready.at[index], out.at[:, rows, :], sems.at[index])

    def field(index, carry):
        start = index // 2 * 144 + index % 2 * 64
        for part in range(2):
            for low in range(4):
                values = []
                for high in range(8):
                    a = 4 * high + low
                    lanes = pl.ds((a % 2) * 128, 128)
                    pair = []
                    for side in range(2):
                        row = pl.multiple_of(start + side * 32 + part * 16, 16)
                        value = lines[line_rank(a // 2), pl.ds(row, 16), lanes]
                        pair.append(value.astype(F32))
                    values.append(tuple(pair))
                for q, value in enumerate(dft(values, -1)):
                    r, i = turn(value, low * q, 32, -1)
                    work[q, low, 0, part * 16 : part * 16 + 16, :] = r
                    work[q, low, 1, part * 16 : part * 16 + 16, :] = i

        @pl.when(index == 0)
        def _():
            fetch.wait()

        for pair in range(4):
            real, imag = [], []
            for q in (2 * pair, 2 * pair + 1):
                values = dft([(work[q, low, 0], work[q, low, 1]) for low in range(4)], -1)
                for p, value in enumerate(values):
                    k = q + 8 * p
                    r, i = times(value, (twist[0, k : k + 1, :], twist[1, k : k + 1, :]))
                    real.append(r)
                    imag.append(i)
            both = [jnp.concatenate(real, axis=0), jnp.concatenate(imag, axis=0)]
            value = dot(matrix[...], split(jnp.concatenate(both, axis=1)), ((1,), (1,)))
            for side in range(2):
                for half in range(2):
                    turned[pl.ds(side * 8 + pair * 2 + half, 128, stride=16), :] = value[
                        side * 128 : side * 128 + 128, half * 128 : half * 128 + 128
                    ]
        ready[index] = turned[...].reshape(128, 16, 128).astype(BF16)
        send(index).start()
        return carry

    lax.fori_loop(0, 4, field, 0)
    for index in range(4):
        send(index).wait()


def inline_kernel(
    lines,
    phase,
    twist,
    twist_inv,
    table,
    table_inv,
    out,
    held,
    matrix,
    matrix_inv,
    shifts,
    work,
    spec,
    term,
    sums,
    sems,
):
    fetch = pltpu.make_async_copy(table, matrix, sems.at[2])
    fetch_inv = pltpu.make_async_copy(table_inv, matrix_inv, sems.at[3])

    def fetch_phase(freq):
        return pltpu.make_async_copy(phase.at[freq], shifts.at[freq], sems.at[freq])

    def fetch_lines(index):
        rows = pl.ds(pl.multiple_of(index * 16, 16), 16)
        return pltpu.make_async_copy(lines.at[:, rows, :], held.at[index], sems.at[4 + index])

    order = [fetch_lines(0), fetch, fetch_lines(1), fetch_phase(0), fetch_inv]
    for copy in order + [fetch_lines(2), fetch_lines(3), fetch_phase(1)]:
        copy.start()
    term[...] = jnp.zeros_like(term)

    def one_freq(freq, carry):
        def forward(which, carry):
            index = freq * 2 + which
            fetch_lines(index).wait()
            for low in range(8):
                values = []
                for high in range(16):
                    value = held[index, every_rank(8 * high + low)].astype(F32)
                    values.append((value[0:8], value[8:16]))
                for q, value in enumerate(dft(values, -1)):
                    r, i = turn(value, low * q, 128, -1)
                    work[q * 8 + low, 0] = r
                    work[q * 8 + low, 1] = i

            @pl.when(index == 0)
            def _():
                fetch.wait()

            for part in range(4):
                real, imag = [], []
                for q in range(4 * part, 4 * part + 4):
                    values = [(work[q * 8 + low, 0], work[q * 8 + low, 1]) for low in range(8)]
                    for p, value in enumerate(dft(values, -1)):
                        k = q + 16 * p
                        r, i = times(value, (twist[0, k : k + 1, :], twist[1, k : k + 1, :]))
                        real.append(r)
                        imag.append(i)
                both = [jnp.concatenate(real, axis=0), jnp.concatenate(imag, axis=0)]
                block = slice(part * 256, part * 256 + 256)
                spec[which, block, :] = dot(split(jnp.concatenate(both, axis=1)), matrix[...])
            return carry

        lax.fori_loop(0, 2, forward, 0)
        for part in range(4):
            block = slice(part * 256, part * 256 + 256)
            both = spec[0, block, :] * spec[1, block, :]
            term[block, :] += both[:, 0:128] + both[:, 128:256]

        fetch_phase(freq).wait()

        @pl.when(freq == 0)
        def _():
            fetch_inv.wait()

        def inverse(ref, carry):
            for part in range(4):
                block = slice(part * 256, part * 256 + 256)
                value = (spec[0, block, 0:128], spec[0, block, 128:256])
                shift = (shifts[freq, ref, 0, block, :], shifts[freq, ref, 1, block, :])
                turned = jnp.concatenate(times(value, shift), axis=1)
                turned = dot(split(turned), matrix_inv[...])
                for j in range(4):
                    q = 4 * part + j
                    values = []
                    for p in range(8):
                        k = q + 16 * p
                        row = 64 * j + 8 * p
                        value = (turned[row : row + 8, 0:128], turned[row : row + 8, 128:256])
                        values.append(
                            times(value, (twist_inv[0, k : k + 1, :], twist_inv[1, k : k + 1, :]))
                        )
                    for low, value in enumerate(dft(values, 1)):
                        r, i = turn(value, low * q, 128, 1)
                        work[low * 16 + q, 0] = r
                        work[low * 16 + q, 1] = i
            rows = pl.ds(pl.multiple_of(freq * 32 + ref * 16, 16), 16)
            for low in range(8):
                values = [(work[low * 16 + q, 0], work[low * 16 + q, 1]) for q in range(16)]
                for high, value in enumerate(dft(values, 1)):
                    value = jnp.concatenate(value, axis=0).astype(BF16)
                    out[every_rank(8 * high + low), rows, :] = value
            return carry

        lax.fori_loop(0, 2, inverse, 0)
        return carry

    lax.fori_loop(0, 2, one_freq, 0)
    total = term[...].reshape(128, 8, 128).sum(axis=1)
    for q in range(16):
        sums[pl.ds(q, 8, stride=16), :] = total[8 * q : 8 * q + 8, :]
    total = sums[...]
    total = total + pltpu.roll(total, 64, 1)
    total = total + pltpu.roll(total, 32, 1)
    high = total.astype(BF16).astype(F32)
    rest = total - high
    middle = rest.astype(BF16).astype(F32)
    low = rest - middle
    place = lax.broadcasted_iota(jnp.int32, (128, 128), 1) >> 5
    value = jnp.where(place == 0, high, jnp.where(place == 1, middle, low))
    value = jnp.where(place == 3, 0.0, value).reshape(16, 8, 128).astype(BF16)
    for block in range(DEVICES):
        out[every_rank(block), 64:72, :] = value[block % GROUP]


def cross_inverse_kernel(
    lines, wedges, packed, twist, table, out, matrix, flat, work, kept, share, sem
):
    fetch = pltpu.make_async_copy(table, matrix, sem)
    fetch.start()
    for half in range(2):
        value = packed[:, half * 144 + 128 : half * 144 + 144, :].astype(F32)
        high = jnp.zeros_like(value)
        for power in (32, 16, 8, 4, 2, 1):
            over = value >= 2.0**power
            value = jnp.where(over, value * 2.0**-power, value)
            high = jnp.where(over, high + float(power), high)
        share[:, half * 16 : half * 16 + 16, :] = (high + (value - 1.0)) * (1.0 / 32.0)

    def gather(d, totals):
        value = lines[d, 64:72, :].astype(F32)
        where = wedges[pl.ds(d, 1), :]
        return tuple(
            total + jnp.where(where == float(w), value, 0.0) for w, total in enumerate(totals)
        )

    zero = jnp.zeros((8, 128), F32)
    totals = lax.fori_loop(0, 128, gather, (zero,) * 8, unroll=8)
    highs, lows = [], []
    for total in totals:
        total = total + pltpu.roll(total, 64, 1)
        total = total + pltpu.roll(total, 32, 1)
        total = total * (1.0 / (SIZE * SIZE * math.sqrt(SIZE)))
        highs.append(total.astype(BF16).astype(F32))
        lows.append(total - highs[-1])
    place = lax.broadcasted_iota(jnp.int32, (8, 128), 1) >> 5
    for half in range(2):
        rows = []
        for first in (half * 2, half * 2 + 4):
            even = jnp.where(place == 0, highs[first], lows[first])
            odd = jnp.where(place == 2, highs[first + 1], lows[first + 1])
            rows.append(jnp.where(place < 2, even, odd))
        value = jnp.concatenate(rows, axis=0).astype(BF16)
        for group in range(16):
            out[group, 128:144, half * 128 : half * 128 + 128] = value

    fetch.wait()

    def one_freq(freq, carry):
        for ref in range(2):
            rows = pl.ds(pl.multiple_of(freq * 32 + ref * 16, 16), 16)
            flat[...] = lines[:, rows, :].astype(F32).reshape(2048, 128)
            for g in range(8):
                pair = [flat[pl.ds(side * 8 + g, 128, stride=16), :] for side in range(2)]
                value = jnp.concatenate([x.T for x in pair], axis=1).astype(BF16)
                value = dot(jnp.concatenate([value, value], axis=1), matrix[...])
                values = []
                for p in range(4):
                    k = g + 8 * p
                    block = value[32 * p : 32 * p + 32, :]
                    block = (block[:, 0:128], block[:, 128:256])
                    values.append(times(block, (twist[0, k : k + 1, :], twist[1, k : k + 1, :])))
                for low, value in enumerate(dft(values, 1)):
                    r, i = turn(value, low * g, 32, 1)
                    work[low, g, 0] = r
                    work[low, g, 1] = i

            def rows16(part, carry):
                start = pl.multiple_of(part * 16, 16)
                rows = pl.ds(start, 16)
                for low in range(4):
                    values = [(work[low, g, 0, rows, :], work[low, g, 1, rows, :]) for g in range(8)]
                    for high, value in enumerate(dft(values, 1)):
                        a = 4 * high + low
                        lanes = slice((a % 2) * 128, (a % 2) * 128 + 128)
                        for side in range(2):
                            rounded = value[side].astype(BF16)
                            if ref == 0:
                                kept[a, side, rows, :] = rounded
                            else:
                                s = share[line_rank(a // 2), rows, lanes]
                                first = kept[a, side, rows, :].astype(F32)
                                mixed = first * s + rounded.astype(F32) * (1.0 - s)
                                row = pl.multiple_of(freq * 64 + side * 32 + part * 16, 16)
                                out[line_rank(a // 2), pl.ds(row, 16), lanes] = mixed.astype(BF16)
                return carry

            lax.fori_loop(0, 2, rows16, 0)
        return carry

    lax.fori_loop(0, 2, one_freq, 0)


def unpack_kernel(home, out, angles, turned, sems):
    copies = []
    for part in range(4):
        block = home.at[:, pl.ds(part * 32, 32), :]
        copies.append(pltpu.make_async_copy(block, out.at[part % 2, part // 2], sems.at[part]))
    for copy in copies:
        copy.start()
    value = home[:, 128:144, :].astype(F32)
    for half in range(2):
        for top in range(2):
            part = value[:, top * 8 : top * 8 + 8, half * 128 : half * 128 + 128]
            flipped = part.reshape(128, 128).T
            w = top * 4 + half * 2
            turned[pl.ds(w, 32, stride=8), :] = flipped[0:32] + flipped[32:64]
            turned[pl.ds(w + 1, 32, stride=8), :] = flipped[64:96] + flipped[96:128]
    for k in range(32):
        angles[:, k * 128 : k * 128 + 128] = turned[k * 8 : k * 8 + 8, :]
    for copy in copies:
        copy.wait()


FAR = pl.BlockSpec(memory_space=pltpu.HBM)
LOCAL = pl.BlockSpec(memory_space=pltpu.VMEM)
SCALAR = pl.BlockSpec(memory_space=pltpu.SMEM)


def near(value):
    return pltpu.with_memory_space_constraint(value, pltpu.VMEM)


def far(value):
    return pltpu.with_memory_space_constraint(value, pltpu.HBM)


def call(kernel, name, outs, out_specs, in_specs, scratch, mebibytes, args):
    return pl.pallas_call(
        kernel,
        in_specs=in_specs,
        out_specs=out_specs,
        out_shape=outs,
        scratch_shapes=scratch,
        compiler_params=pltpu.CompilerParams(vmem_limit_bytes=mebibytes * 2**20),
        name=name,
    )(*args)


def pack(receiver, source, weight):
    args = (
        far(receiver.reshape(2, 2, GROUP, 32, 256)),
        far(source.reshape(2, 2, GROUP, 32, 256)),
        far(weight.reshape(GROUP, 2, 16, 256)),
    )
    scratch = [pltpu.VMEM((GROUP, 2, 16, 256), jnp.int32), pltpu.SemaphoreType.DMA((9,))]
    outs = pltpu.VMEM((GROUP, 288, 256), BF16)
    return call(pack_kernel, "pack_fields", outs, LOCAL, [FAR] * 3, scratch, 12, args)


def phases(omega, slowness, wedge_map):
    outs = [
        jax.ShapeDtypeStruct((2, 2, 2, 1024, 128), F32),
        jax.ShapeDtypeStruct((128, 128), F32),
    ]
    args = (omega, slowness, wedge_map)
    specs = [SCALAR] * 2 + [LOCAL]
    return call(phase_kernel, "phase_table", outs, [LOCAL] * 2, specs, [], 12, args)


def cross_forward(packed):
    t = tables()
    args = [near(packed), near(jnp.asarray(t["cross_tw_fwd"])), jnp.asarray(t["cross_fwd"])]
    outs = pltpu.HBM((DEVICES, 64, 128), BF16)
    scratch = [
        pltpu.VMEM((256, 768), BF16),
        pltpu.VMEM((8, 4, 2, 32, 128), F32),
        pltpu.VMEM((2048, 128), F32),
        pltpu.VMEM((4, DEVICES, 16, 128), BF16),
        pltpu.SemaphoreType.DMA,
        pltpu.SemaphoreType.DMA((4,)),
    ]
    return call(
        cross_forward_kernel, "crossline_forward", outs, FAR, [LOCAL] * 2 + [FAR], scratch, 16, args
    )


def inline_step(lines, phase):
    t = tables()
    args = [far(lines), far(phase)]
    args += [near(jnp.asarray(t[n])) for n in ("inline_tw_fwd", "inline_tw_inv")]
    args += [jnp.asarray(t[n]) for n in ("inline_fwd", "inline_inv")]
    outs = pltpu.VMEM((DEVICES, 72, 128), BF16)
    scratch = [
        pltpu.VMEM((4, DEVICES, 16, 128), BF16),
        pltpu.VMEM((768, 256), BF16),
        pltpu.VMEM((768, 256), BF16),
        pltpu.VMEM((2, 2, 2, 1024, 128), F32),
        pltpu.VMEM((128, 2, 8, 128), F32),
        pltpu.VMEM((2, 1024, 256), F32),
        pltpu.VMEM((1024, 128), F32),
        pltpu.VMEM((128, 128), F32),
        pltpu.SemaphoreType.DMA((8,)),
    ]
    specs = [FAR, FAR, LOCAL, LOCAL, FAR, FAR]
    return call(inline_kernel, "inline_step", outs, LOCAL, specs, scratch, 20, args)


def cross_inverse(partial, wedges, packed):
    t = tables()
    args = [near(partial), near(wedges), near(packed), near(jnp.asarray(t["cross_tw_inv"]))]
    args.append(jnp.asarray(t["cross_inv"]))
    outs = pltpu.VMEM((GROUP, 144, 256), BF16)
    scratch = [
        pltpu.VMEM((512, 256), BF16),
        pltpu.VMEM((2048, 128), F32),
        pltpu.VMEM((4, 8, 2, 32, 128), F32),
        pltpu.VMEM((32, 2, 32, 128), BF16),
        pltpu.VMEM((GROUP, 32, 256), F32),
        pltpu.SemaphoreType.DMA,
    ]
    return call(
        cross_inverse_kernel, "crossline_inverse", outs, LOCAL, [LOCAL] * 4 + [FAR], scratch, 16, args
    )


def unpack(home):
    outs = [
        jax.ShapeDtypeStruct((2, 2, GROUP, 32, 256), BF16),
        jax.ShapeDtypeStruct((8, SIZE), F32),
    ]
    scratch = [pltpu.VMEM((256, 128), F32), pltpu.SemaphoreType.DMA((4,))]
    specs = [FAR, LOCAL]
    return call(unpack_kernel, "unpack_fields", outs, specs, [LOCAL], scratch, 12, [near(home)])


def exchange(value, axes):
    return lax.all_to_all(value, axes, 0, 0, tiled=True)


def per_device(receiver, source, weight, omega, slowness, wedge_map):
    packed = exchange(pack(receiver, source, weight), LINE)
    phase, wedges = phases(omega, slowness, wedge_map)
    lines = exchange(cross_forward(packed), EVERY)
    partial = exchange(inline_step(lines, phase), EVERY)
    home = exchange(cross_inverse(partial, wedges, packed), LINE)
    mixed, angles = unpack(home)
    return (mixed.reshape(2, 2, 512, 256), angles)


def solution(mesh):
    fine = Mesh(mesh.devices.reshape(2, 4, 2, 4, 2), NAMES)
    rows, columns = ("x_hi", "z"), ("x_lo", "y", "core")
    return jax.shard_map(
        per_device,
        mesh=fine,
        in_specs=(
            P(None, None, rows, columns),
            P(None, None, rows, columns),
            P(rows, columns),
            P(),
            P(),
            P(),
        ),
        out_specs=(P(None, None, rows, columns), P()),
        check_vma=False,
    )
```

```python
import functools
import math

import jax
import jax.numpy as jnp
import ml_dtypes
import numpy as np
from jax import lax
from jax.experimental import pallas as pl
from jax.experimental.pallas import tpu as pltpu
from jax.sharding import Mesh
from jax.sharding import PartitionSpec as P

SIZE = 4096
DEVICES = 128
GROUP = 16
BF16 = jnp.bfloat16
F32 = jnp.float32
NAMES = ("x_hi", "z", "x_lo", "y", "core")
LINE = ("y", "x_lo", "core")
EVERY = ("x_lo", "x_hi", "z", "y", "core")
HALF = math.sqrt(0.5)


def line_rank(block):
    high, rest = divmod(block, 8)
    return rest // 2 * 4 + high * 2 + rest % 2


def every_rank(block):
    group, line = divmod(block, GROUP)
    return line // 2 % 2 * 64 + group * 8 + line // 4 * 2 + line % 2


def roots(rows, cols, length, sign):
    turn = np.outer(np.arange(rows), np.arange(cols)) % length
    return np.exp(sign * 2j * np.pi * turn / length)


def as_block(matrix):
    return np.block([[matrix.real, matrix.imag], [-matrix.imag, matrix.real]])


def two_parts(matrix):
    high = matrix.astype(np.float32).astype(ml_dtypes.bfloat16)
    low = (matrix - high.astype(np.float64)).astype(np.float32).astype(ml_dtypes.bfloat16)
    return high, low


def gains(length):
    turns = np.exp(2j * np.pi * np.arange(length) / length)
    factors = np.exp2(np.arange(4096) / 4096)
    best = []
    for row in range(length):
        entries = turns[row * np.arange(length) % length]
        entries = np.concatenate([entries.real, entries.imag])
        scaled = factors[:, None] * entries
        rounded = scaled.astype(np.float32).astype(ml_dtypes.bfloat16).astype(np.float64)
        best.append(factors[(np.square(rounded - scaled).sum(axis=1) / factors**2).argmin()])
    return np.array(best)


def pair_table(values):
    return np.stack([values.real, values.imag]).astype(np.float32)


@functools.lru_cache(None)
def tables():
    out = {}
    high, low = two_parts(as_block(roots(128, 128, 128, -1)).T)
    out["cross_fwd"] = np.concatenate([high, high, low], axis=1)
    high, low = two_parts(as_block(roots(128, 128, 128, 1)) / SIZE)
    out["cross_inv"] = np.concatenate([high, low], axis=0)
    out["cross_tw_fwd"] = pair_table(roots(32, 128, SIZE, -1))
    out["cross_tw_inv"] = pair_table(roots(32, 128, SIZE, 1))
    gain = np.tile(gains(32), 4)
    out["phase_scale"] = (1.0 / gain).astype(np.float32)[None, :]
    for name, sign, scale in (("fwd", -1, 1.0), ("inv", 1, 1.0 / SIZE)):
        lanes = np.kron(np.eye(4), roots(32, 32, 32, sign))
        high, _ = two_parts(np.tile(gain, 2)[:, None] * as_block(lanes) * scale)
        out["inline_" + name] = high
    out["inline_tw_fwd"] = pair_table(np.tile(roots(128, 32, SIZE, -1), (1, 4)) / gain)
    out["inline_tw_inv"] = pair_table(np.tile(roots(128, 32, SIZE, 1), (1, 4)))
    return out


def add(x, y):
    return (x[0] + y[0], x[1] + y[1])


def sub(x, y):
    return (x[0] - y[0], x[1] - y[1])


def times(x, y):
    return (x[0] * y[0] - x[1] * y[1], x[0] * y[1] + x[1] * y[0])


def turn(x, numerator, length, sign):
    eighth = 8 * (numerator % length) * sign % (8 * length)
    if eighth % length:
        angle = sign * 2.0 * math.pi * (numerator % length) / length
        c, s = math.cos(angle), math.sin(angle)
        return (x[0] * c - x[1] * s, x[0] * s + x[1] * c)
    eighth = eighth // length
    r, i = x
    if eighth == 0:
        return x
    if eighth == 1:
        return ((r - i) * HALF, (r + i) * HALF)
    if eighth == 2:
        return (-i, r)
    if eighth == 3:
        return ((r + i) * -HALF, (r - i) * HALF)
    if eighth == 4:
        return (-r, -i)
    if eighth == 5:
        return ((i - r) * HALF, (r + i) * -HALF)
    if eighth == 6:
        return (i, -r)
    return ((r + i) * HALF, (i - r) * HALF)


def dft(x, sign):
    length = len(x)
    if length == 2:
        return [add(x[0], x[1]), sub(x[0], x[1])]
    if length == 4:
        t0, t1 = add(x[0], x[2]), sub(x[0], x[2])
        t2, t3 = add(x[1], x[3]), sub(x[1], x[3])
        r, i = t3
        if sign < 0:
            return [add(t0, t2), (t1[0] + i, t1[1] - r), sub(t0, t2), (t1[0] - i, t1[1] + r)]
        return [add(t0, t2), (t1[0] - i, t1[1] + r), sub(t0, t2), (t1[0] + i, t1[1] - r)]
    first = {8: 2, 16: 4, 32: 8}[length]
    second = length // first
    inner = [dft(x[low::second], sign) for low in range(second)]
    out = [None] * length
    for q in range(first):
        row = [turn(inner[low][q], low * q, length, sign) for low in range(second)]
        for p, value in enumerate(dft(row, sign)):
            out[q + first * p] = value
    return out


def split(value):
    high = value.astype(BF16)
    return high, (value - high.astype(F32)).astype(BF16)


def dot(x, y, dims=((1,), (0,))):
    return lax.dot_general(x, y, (dims, ((), ())), preferred_element_type=F32)


def dot2(value, matrix):
    high, low = split(value)
    return dot(high, matrix[...]) + dot(low, matrix[...])


def pack_kernel(receiver, source, weight, out, raw, sems):
    copies = [pltpu.make_async_copy(weight, raw, sems.at[8])]
    for which, field in enumerate((receiver, source)):
        for part in range(2):
            for freq in range(2):
                rows = pl.ds(freq * 144 + which * 64 + part * 32, 32)
                sem = sems.at[which * 4 + part * 2 + freq]
                copies.append(
                    pltpu.make_async_copy(field.at[part, freq], out.at[:, rows, :], sem)
                )
    for copy in copies:
        copy.start()
    copies[0].wait()
    for freq in range(2):
        value = raw[:, freq]
        high = value >> 7
        code = 1.0 + (value & 127).astype(F32) * (1.0 / 128.0)
        for power in (1, 2, 4, 8, 16, 32):
            code = code * jnp.where((high & power) != 0, 2.0**power, 1.0)
        out[:, freq * 144 + 128 : freq * 144 + 144, :] = code.astype(BF16)
    for copy in copies[1:]:
        copy.wait()


def prepare_kernel(omega, slowness, scale, wedge_map, packed, phase, wedges, share):
    x_hi, z, x_lo, y, core = (lax.axis_index(name) for name in NAMES)
    device = ((x_lo * 2 + x_hi) * 4 + z) * 8 + y * 2 + core
    step = 2.0 * math.pi / SIZE

    def signed(index):
        index = jnp.where(index >= SIZE // 2, index - SIZE, index)
        return step * index.astype(F32)

    def body(part, carry):
        row = part * 64 + lax.broadcasted_iota(jnp.int32, (64, 128), 0)
        lane = lax.broadcasted_iota(jnp.int32, (64, 128), 1)
        kx = signed((row >> 6) + 16 * ((row >> 3) & 7) + 128 * (lane & 31))
        ky = signed(device * 32 + (row & 7) + 8 * (lane >> 5))
        kx_sq = kx * kx
        ky_sq = ky * ky
        rows = pl.ds(pl.multiple_of(part * 64, 64), 64)
        for freq in range(2):
            for ref in range(2):
                number = omega[freq] * slowness[ref]
                quad = number * number - kx_sq - ky_sq
                root = jnp.sqrt(jnp.abs(quad))
                decay = jnp.exp(-root)
                inside = jnp.maximum(quad, 0.0)
                even = jnp.full_like(quad, 1.0 / math.factorial(22))
                odd = jnp.full_like(quad, 1.0 / math.factorial(23))
                for n in range(10, -1, -1):
                    even = 1.0 / math.factorial(2 * n) - inside * even
                    odd = 1.0 / math.factorial(2 * n + 1) - inside * odd
                real = jnp.where(quad >= 0, even, decay)
                imag = jnp.where(quad >= 0, odd * root, 0.0)
                phase[freq, ref, 0, rows, :] = real * scale[...]
                phase[freq, ref, 1, rows, :] = imag * scale[...]
        return carry

    lax.fori_loop(0, 16, body, 0)
    rows = wedge_map[pl.ds(y, 32, stride=4), :].astype(F32)
    wedges[...] = jnp.concatenate([rows] * 4, axis=0).T
    for half in range(2):
        for a in range(32):
            lanes = slice((a % 2) * 128, (a % 2) * 128 + 128)
            block = packed[line_rank(a // 2), half * 144 + 128 : half * 144 + 144, lanes]
            value = block.astype(F32)
            high = jnp.zeros_like(value)
            for power in (32, 16, 8, 4, 2, 1):
                over = value >= 2.0**power
                value = jnp.where(over, value * 2.0**-power, value)
                high = jnp.where(over, high + float(power), high)
            share[a, half * 16 : half * 16 + 16, :] = (high + (value - 1.0)) * (1.0 / 32.0)


def cross_forward_kernel(lines, twist, table, out, matrix, work, turned, ready, sem, sems):
    fetch = pltpu.make_async_copy(table, matrix, sem)
    fetch.start()

    def send(index):
        rows = pl.ds(pl.multiple_of(index * 16, 16), 16)
        return pltpu.make_async_copy(ready.at[index], out.at[:, rows, :], sems.at[index])

    def field(index, carry):
        start = index // 2 * 144 + index % 2 * 64
        for part in range(2):
            for low in range(4):
                values = []
                for high in range(8):
                    a = 4 * high + low
                    lanes = pl.ds((a % 2) * 128, 128)
                    pair = []
                    for side in range(2):
                        row = pl.multiple_of(start + side * 32 + part * 16, 16)
                        value = lines[line_rank(a // 2), pl.ds(row, 16), lanes]
                        pair.append(value.astype(F32))
                    values.append(tuple(pair))
                for q, value in enumerate(dft(values, -1)):
                    r, i = turn(value, low * q, 32, -1)
                    work[q, low, 0, part * 16 : part * 16 + 16, :] = r
                    work[q, low, 1, part * 16 : part * 16 + 16, :] = i

        @pl.when(index == 0)
        def _():
            fetch.wait()

        for pair in range(4):
            real, imag = [], []
            for q in (2 * pair, 2 * pair + 1):
                values = dft([(work[q, low, 0], work[q, low, 1]) for low in range(4)], -1)
                for p, value in enumerate(values):
                    k = q + 8 * p
                    r, i = times(value, (twist[0, k : k + 1, :], twist[1, k : k + 1, :]))
                    real.append(r)
                    imag.append(i)
            both = [jnp.concatenate(real, axis=0), jnp.concatenate(imag, axis=0)]
            high, low = split(jnp.concatenate(both, axis=1))
            parts = jnp.concatenate([high, low, high], axis=1)
            value = dot(matrix[...], parts, ((1,), (1,)))
            for side in range(2):
                for half in range(2):
                    turned[pl.ds(side * 8 + pair * 2 + half, 128, stride=24), :] = value[
                        side * 128 : side * 128 + 128, half * 128 : half * 128 + 128
                    ]
        ready[index] = turned[...].reshape(128, 24, 128)[:, :16].astype(BF16)
        send(index).start()
        return carry

    lax.fori_loop(0, 4, field, 0, unroll=True)
    for index in range(4):
        send(index).wait()


def inline_kernel(
    lines,
    phase,
    twist,
    twist_inv,
    table,
    table_inv,
    out,
    held,
    matrix,
    matrix_inv,
    shifts,
    work,
    spec,
    term,
    sums,
    sems,
):
    fetch = pltpu.make_async_copy(table, matrix, sems.at[2])
    fetch_inv = pltpu.make_async_copy(table_inv, matrix_inv, sems.at[3])

    def fetch_phase(freq):
        return pltpu.make_async_copy(phase.at[freq], shifts.at[freq], sems.at[freq])

    def fetch_lines(index):
        rows = pl.ds(pl.multiple_of(index * 16, 16), 16)
        return pltpu.make_async_copy(lines.at[:, rows, :], held.at[index], sems.at[4 + index])

    order = [fetch_lines(0), fetch, fetch_lines(1), fetch_phase(0), fetch_inv]
    for copy in order + [fetch_lines(2), fetch_lines(3), fetch_phase(1)]:
        copy.start()
    term[...] = jnp.zeros_like(term)

    def one_freq(freq, carry):
        def forward(which, carry):
            index = freq * 2 + which
            fetch_lines(index).wait()
            for low in range(8):
                values = []
                for high in range(16):
                    value = held[index, every_rank(8 * high + low)].astype(F32)
                    values.append((value[0:8], value[8:16]))
                for q, value in enumerate(dft(values, -1)):
                    r, i = turn(value, low * q, 128, -1)
                    work[q * 8 + low, 0] = r
                    work[q * 8 + low, 1] = i

            @pl.when(index == 0)
            def _():
                fetch.wait()

            for part in range(4):
                real, imag = [], []
                for q in range(4 * part, 4 * part + 4):
                    values = [(work[q * 8 + low, 0], work[q * 8 + low, 1]) for low in range(8)]
                    for p, value in enumerate(dft(values, -1)):
                        k = q + 16 * p
                        r, i = times(value, (twist[0, k : k + 1, :], twist[1, k : k + 1, :]))
                        real.append(r)
                        imag.append(i)
                both = [jnp.concatenate(real, axis=0), jnp.concatenate(imag, axis=0)]
                block = slice(part * 256, part * 256 + 256)
                spec[which, block, :] = dot2(jnp.concatenate(both, axis=1), matrix)
            return carry

        lax.fori_loop(0, 2, forward, 0, unroll=True)
        for part in range(4):
            block = slice(part * 256, part * 256 + 256)
            both = spec[0, block, :] * spec[1, block, :]
            term[block, :] += both[:, 0:128] + both[:, 128:256]

        fetch_phase(freq).wait()

        @pl.when(freq == 0)
        def _():
            fetch_inv.wait()

        def inverse(ref, carry):
            for part in range(4):
                block = slice(part * 256, part * 256 + 256)
                value = (spec[0, block, 0:128], spec[0, block, 128:256])
                shift = (shifts[freq, ref, 0, block, :], shifts[freq, ref, 1, block, :])
                turned = jnp.concatenate(times(value, shift), axis=1)
                turned = dot2(turned, matrix_inv)
                for j in range(4):
                    q = 4 * part + j
                    values = []
                    for p in range(8):
                        k = q + 16 * p
                        row = 64 * j + 8 * p
                        value = (turned[row : row + 8, 0:128], turned[row : row + 8, 128:256])
                        values.append(
                            times(value, (twist_inv[0, k : k + 1, :], twist_inv[1, k : k + 1, :]))
                        )
                    for low, value in enumerate(dft(values, 1)):
                        r, i = turn(value, low * q, 128, 1)
                        work[low * 16 + q, 0] = r
                        work[low * 16 + q, 1] = i
            rows = pl.ds(pl.multiple_of(freq * 32 + ref * 16, 16), 16)
            for low in range(8):
                values = [(work[low * 16 + q, 0], work[low * 16 + q, 1]) for q in range(16)]
                for high, value in enumerate(dft(values, 1)):
                    value = jnp.concatenate(value, axis=0).astype(BF16)
                    out[every_rank(8 * high + low), rows, :] = value
            return carry

        lax.fori_loop(0, 2, inverse, 0, unroll=True)
        return carry

    lax.fori_loop(0, 2, one_freq, 0)
    total = term[...].reshape(128, 8, 128).sum(axis=1)
    for q in range(16):
        sums[pl.ds(q, 8, stride=16), :] = total[8 * q : 8 * q + 8, :]
    total = sums[...]
    total = total + pltpu.roll(total, 64, 1)
    total = total + pltpu.roll(total, 32, 1)
    high = total.astype(BF16).astype(F32)
    rest = total - high
    middle = rest.astype(BF16).astype(F32)
    low = rest - middle
    place = lax.broadcasted_iota(jnp.int32, (128, 128), 1) >> 5
    value = jnp.where(place == 0, high, jnp.where(place == 1, middle, low))
    value = jnp.where(place == 3, 0.0, value).reshape(16, 8, 128).astype(BF16)
    for block in range(DEVICES):
        out[every_rank(block), 64:72, :] = value[block % GROUP]


def cross_inverse_kernel(
    lines, wedges, shares, twist, table, out, matrix, flat, work, kept, share, sems
):
    fetch = pltpu.make_async_copy(table, matrix, sems.at[0])
    fetch.start()
    fetch_share = pltpu.make_async_copy(shares, share, sems.at[1])
    fetch_share.start()
    def gather(d, totals):
        value = lines[d, 64:72, :].astype(F32)
        where = wedges[pl.ds(d, 1), :]
        return tuple(
            total + jnp.where(where == float(w), value, 0.0) for w, total in enumerate(totals)
        )

    zero = jnp.zeros((8, 128), F32)
    totals = lax.fori_loop(0, 128, gather, (zero,) * 8, unroll=8)
    highs, lows = [], []
    for total in totals:
        total = total + pltpu.roll(total, 64, 1)
        total = total + pltpu.roll(total, 32, 1)
        total = total * (1.0 / (SIZE * SIZE * math.sqrt(SIZE)))
        highs.append(total.astype(BF16).astype(F32))
        lows.append(total - highs[-1])
    place = lax.broadcasted_iota(jnp.int32, (8, 128), 1) >> 5
    for half in range(2):
        rows = []
        for first in (half * 2, half * 2 + 4):
            even = jnp.where(place == 0, highs[first], lows[first])
            odd = jnp.where(place == 2, highs[first + 1], lows[first + 1])
            rows.append(jnp.where(place < 2, even, odd))
        value = jnp.concatenate(rows, axis=0).astype(BF16)
        for group in range(16):
            out[group, 128:144, half * 128 : half * 128 + 128] = value

    fetch.wait()
    fetch_share.wait()

    def one_freq(freq, carry):
        for ref in range(2):
            rows = pl.ds(pl.multiple_of(freq * 32 + ref * 16, 16), 16)
            for d in range(128):
                flat[24 * d : 24 * d + 16, :] = lines[d, rows, :].astype(F32)
            for g in range(8):
                pair = [flat[pl.ds(side * 8 + g, 128, stride=24), :] for side in range(2)]
                value = jnp.concatenate([x.T for x in pair], axis=1).astype(BF16)
                value = dot(jnp.concatenate([value, value], axis=1), matrix[...])
                values = []
                for p in range(4):
                    k = g + 8 * p
                    block = value[32 * p : 32 * p + 32, :]
                    block = (block[:, 0:128], block[:, 128:256])
                    values.append(times(block, (twist[0, k : k + 1, :], twist[1, k : k + 1, :])))
                for low, value in enumerate(dft(values, 1)):
                    r, i = turn(value, low * g, 32, 1)
                    work[low, g, 0] = r
                    work[low, g, 1] = i

            def rows16(part, carry):
                start = pl.multiple_of(part * 16, 16)
                rows = pl.ds(start, 16)
                for low in range(4):
                    values = [(work[low, g, 0, rows, :], work[low, g, 1, rows, :]) for g in range(8)]
                    for high, value in enumerate(dft(values, 1)):
                        a = 4 * high + low
                        lanes = slice((a % 2) * 128, (a % 2) * 128 + 128)
                        for side in range(2):
                            rounded = value[side].astype(BF16)
                            if ref == 0:
                                kept[a, side, rows, :] = rounded
                            else:
                                s = share[a, rows, :]
                                first = kept[a, side, rows, :].astype(F32)
                                mixed = first * s + rounded.astype(F32) * (1.0 - s)
                                row = pl.multiple_of(freq * 64 + side * 32 + part * 16, 16)
                                out[line_rank(a // 2), pl.ds(row, 16), lanes] = mixed.astype(BF16)
                return carry

            lax.fori_loop(0, 2, rows16, 0, unroll=True)
        return carry

    lax.fori_loop(0, 2, one_freq, 0)


def unpack_kernel(home, out, angles, turned, sems):
    copies = []
    for part in range(4):
        block = home.at[:, pl.ds(part * 32, 32), :]
        copies.append(pltpu.make_async_copy(block, out.at[part % 2, part // 2], sems.at[part]))
    for copy in copies:
        copy.start()
    value = home[:, 128:144, :].astype(F32)
    for half in range(2):
        for top in range(2):
            part = value[:, top * 8 : top * 8 + 8, half * 128 : half * 128 + 128]
            flipped = part.reshape(128, 128).T
            w = top * 4 + half * 2
            turned[pl.ds(w, 32, stride=8), :] = flipped[0:32] + flipped[32:64]
            turned[pl.ds(w + 1, 32, stride=8), :] = flipped[64:96] + flipped[96:128]
    for k in range(32):
        angles[:, k * 128 : k * 128 + 128] = turned[k * 8 : k * 8 + 8, :]
    for copy in copies:
        copy.wait()


FAR = pl.BlockSpec(memory_space=pltpu.HBM)
LOCAL = pl.BlockSpec(memory_space=pltpu.VMEM)
SCALAR = pl.BlockSpec(memory_space=pltpu.SMEM)


def near(value):
    return pltpu.with_memory_space_constraint(value, pltpu.VMEM)


def far(value):
    return pltpu.with_memory_space_constraint(value, pltpu.HBM)


def call(kernel, name, outs, out_specs, in_specs, scratch, mebibytes, args):
    return pl.pallas_call(
        kernel,
        in_specs=in_specs,
        out_specs=out_specs,
        out_shape=outs,
        scratch_shapes=scratch,
        compiler_params=pltpu.CompilerParams(vmem_limit_bytes=mebibytes * 2**20),
        name=name,
    )(*args)


def pack(receiver, source, weight):
    args = (
        far(receiver.reshape(2, 2, GROUP, 32, 256)),
        far(source.reshape(2, 2, GROUP, 32, 256)),
        far(weight.reshape(GROUP, 2, 16, 256)),
    )
    scratch = [pltpu.VMEM((GROUP, 2, 16, 256), jnp.int32), pltpu.SemaphoreType.DMA((9,))]
    outs = pltpu.VMEM((GROUP, 288, 256), BF16)
    return call(pack_kernel, "pack_fields", outs, LOCAL, [FAR] * 3, scratch, 12, args)


def prepare(omega, slowness, wedge_map, packed):
    outs = [
        pltpu.HBM((2, 2, 2, 1024, 128), F32),
        pltpu.VMEM((128, 128), F32),
        pltpu.HBM((32, 32, 128), F32),
    ]
    scale = jnp.asarray(tables()["phase_scale"])
    args = (omega, slowness, scale, wedge_map, near(packed))
    specs = [SCALAR] * 2 + [LOCAL] * 3
    return call(prepare_kernel, "prepare", outs, [LOCAL] * 3, specs, [], 16, args)


def cross_forward(packed):
    t = tables()
    args = [near(packed), near(jnp.asarray(t["cross_tw_fwd"])), jnp.asarray(t["cross_fwd"])]
    outs = pltpu.HBM((DEVICES, 64, 128), BF16)
    scratch = [
        pltpu.VMEM((256, 768), BF16),
        pltpu.VMEM((8, 4, 2, 32, 128), F32),
        pltpu.VMEM((3072, 128), F32),
        pltpu.VMEM((4, DEVICES, 16, 128), BF16),
        pltpu.SemaphoreType.DMA,
        pltpu.SemaphoreType.DMA((4,)),
    ]
    return call(
        cross_forward_kernel, "crossline_forward", outs, FAR, [LOCAL] * 2 + [FAR], scratch, 16, args
    )


def inline_step(lines, phase):
    t = tables()
    args = [far(lines), far(phase)]
    args += [near(jnp.asarray(t[n])) for n in ("inline_tw_fwd", "inline_tw_inv")]
    args += [jnp.asarray(t[n]) for n in ("inline_fwd", "inline_inv")]
    outs = pltpu.VMEM((DEVICES, 72, 128), BF16)
    scratch = [
        pltpu.VMEM((4, DEVICES, 16, 128), BF16),
        pltpu.VMEM((256, 256), BF16),
        pltpu.VMEM((256, 256), BF16),
        pltpu.VMEM((2, 2, 2, 1024, 128), F32),
        pltpu.VMEM((128, 2, 8, 128), F32),
        pltpu.VMEM((2, 1024, 256), F32),
        pltpu.VMEM((1024, 128), F32),
        pltpu.VMEM((128, 128), F32),
        pltpu.SemaphoreType.DMA((8,)),
    ]
    specs = [FAR, FAR, LOCAL, LOCAL, FAR, FAR]
    return call(inline_kernel, "inline_step", outs, LOCAL, specs, scratch, 20, args)


def cross_inverse(partial, wedges, share):
    t = tables()
    args = [near(partial), near(wedges), far(share), near(jnp.asarray(t["cross_tw_inv"]))]
    args.append(jnp.asarray(t["cross_inv"]))
    outs = pltpu.VMEM((GROUP, 144, 256), BF16)
    scratch = [
        pltpu.VMEM((512, 256), BF16),
        pltpu.VMEM((3072, 128), F32),
        pltpu.VMEM((4, 8, 2, 32, 128), F32),
        pltpu.VMEM((32, 2, 32, 128), BF16),
        pltpu.VMEM((32, 32, 128), F32),
        pltpu.SemaphoreType.DMA((2,)),
    ]
    return call(
        cross_inverse_kernel, "crossline_inverse", outs, LOCAL, [LOCAL, LOCAL, FAR, LOCAL, FAR], scratch, 16, args
    )


def unpack(home):
    outs = [
        jax.ShapeDtypeStruct((2, 2, GROUP, 32, 256), BF16),
        jax.ShapeDtypeStruct((8, SIZE), F32),
    ]
    scratch = [pltpu.VMEM((256, 128), F32), pltpu.SemaphoreType.DMA((4,))]
    specs = [FAR, LOCAL]
    return call(unpack_kernel, "unpack_fields", outs, specs, [LOCAL], scratch, 12, [near(home)])


def exchange(value, axes):
    return lax.all_to_all(value, axes, 0, 0, tiled=True)


def per_device(receiver, source, weight, omega, slowness, wedge_map):
    packed = exchange(pack(receiver, source, weight), LINE)
    phase, wedges, share = prepare(omega, slowness, wedge_map, packed)
    lines = exchange(cross_forward(packed), EVERY)
    partial = exchange(inline_step(lines, phase), EVERY)
    home = exchange(cross_inverse(partial, wedges, share), LINE)
    mixed, angles = unpack(home)
    return (mixed.reshape(2, 2, 512, 256), angles)


def solution(mesh):
    fine = Mesh(mesh.devices.reshape(2, 4, 2, 4, 2), NAMES)
    rows, columns = ("x_hi", "z"), ("x_lo", "y", "core")
    return jax.shard_map(
        per_device,
        mesh=fine,
        in_specs=(
            P(None, None, rows, columns),
            P(None, None, rows, columns),
            P(rows, columns),
            P(),
            P(),
            P(),
        ),
        out_specs=(P(None, None, rows, columns), P()),
        check_vma=False,
    )
```

```python
import functools
import math

import jax
import jax.numpy as jnp
import ml_dtypes
import numpy as np
from jax import lax
from jax.experimental import pallas as pl
from jax.experimental.pallas import tpu as pltpu
from jax.sharding import Mesh
from jax.sharding import PartitionSpec as P

SIZE = 4096
DEVICES = 128
GROUP = 16
ROWS = ("x_hi", "z_hi", "z_lo")
COLUMNS = ("x_lo", "y_hi", "y_lo", "core")
NAMES = ROWS + COLUMNS
LINE = ("core", "y_lo", "y_hi", "x_lo")
EVERY = ("z_lo", "z_hi", "y_lo", "y_hi", "x_lo", "x_hi", "core")
BF16 = jnp.bfloat16
F32 = jnp.float32
HALF = math.sqrt(0.5)


def reorder(value, old, new):
    bits = {name: value >> place & 1 for place, name in enumerate(reversed(old))}
    return sum(bits[name] << place for place, name in enumerate(reversed(new)))


def line_rank(block):
    return reorder(block, COLUMNS, LINE)


def every_rank(block):
    return reorder(block, ROWS + LINE, EVERY)


def roots(rows, cols, length, sign):
    turn = np.outer(np.arange(rows), np.arange(cols)) % length
    return np.exp(sign * 2j * np.pi * turn / length)


def as_block(matrix):
    return np.block([[matrix.real, matrix.imag], [-matrix.imag, matrix.real]])


def two_parts(matrix):
    high = matrix.astype(np.float32).astype(ml_dtypes.bfloat16)
    low = (matrix - high.astype(np.float64)).astype(np.float32).astype(ml_dtypes.bfloat16)
    return high, low


def gains(length):
    turns = np.exp(2j * np.pi * np.arange(length) / length)
    factors = np.exp2(np.arange(4096) / 4096)
    best = []
    for row in range(length):
        entries = turns[row * np.arange(length) % length]
        entries = np.concatenate([entries.real, entries.imag])
        scaled = factors[:, None] * entries
        rounded = scaled.astype(np.float32).astype(ml_dtypes.bfloat16).astype(np.float64)
        best.append(factors[(np.square(rounded - scaled).sum(axis=1) / factors**2).argmin()])
    return np.array(best)


def pair_table(values):
    return np.stack([values.real, values.imag]).astype(np.float32)


@functools.lru_cache(None)
def tables():
    out = {}
    high, low = two_parts(as_block(roots(128, 128, 128, -1)).T)
    out["cross_fwd"] = np.concatenate([high, high, low], axis=1)
    high, low = two_parts(as_block(roots(128, 128, 128, 1)) / SIZE)
    out["cross_inv"] = np.concatenate([high, low], axis=0)
    out["cross_tw_fwd"] = pair_table(roots(32, 128, SIZE, -1))
    out["cross_tw_inv"] = pair_table(roots(32, 128, SIZE, 1))
    gain = np.tile(gains(32), 4)
    out["phase_scale"] = (1.0 / gain).astype(np.float32)[None, :]
    for name, sign, scale in (("fwd", -1, 1.0), ("inv", 1, 1.0 / SIZE)):
        lanes = np.kron(np.eye(4), roots(32, 32, 32, sign))
        high, _ = two_parts(np.tile(gain, 2)[:, None] * as_block(lanes) * scale)
        out["inline_" + name] = high
    out["inline_tw_fwd"] = pair_table(np.tile(roots(128, 32, SIZE, -1), (1, 4)) / gain)
    out["inline_tw_inv"] = pair_table(np.tile(roots(128, 32, SIZE, 1), (1, 4)))
    return out


def add(x, y):
    return (x[0] + y[0], x[1] + y[1])


def sub(x, y):
    return (x[0] - y[0], x[1] - y[1])


def times(x, y):
    return (x[0] * y[0] - x[1] * y[1], x[0] * y[1] + x[1] * y[0])


def turn(x, numerator, length, sign):
    eighth = 8 * (numerator % length) * sign % (8 * length)
    if eighth % length:
        angle = sign * 2.0 * math.pi * (numerator % length) / length
        c, s = math.cos(angle), math.sin(angle)
        return (x[0] * c - x[1] * s, x[0] * s + x[1] * c)
    eighth = eighth // length
    r, i = x
    if eighth == 0:
        return x
    if eighth == 1:
        return ((r - i) * HALF, (r + i) * HALF)
    if eighth == 2:
        return (-i, r)
    if eighth == 3:
        return ((r + i) * -HALF, (r - i) * HALF)
    if eighth == 4:
        return (-r, -i)
    if eighth == 5:
        return ((i - r) * HALF, (r + i) * -HALF)
    if eighth == 6:
        return (i, -r)
    return ((r + i) * HALF, (i - r) * HALF)


def dft(x, sign):
    length = len(x)
    if length == 2:
        return [add(x[0], x[1]), sub(x[0], x[1])]
    if length == 4:
        t0, t1 = add(x[0], x[2]), sub(x[0], x[2])
        t2, t3 = add(x[1], x[3]), sub(x[1], x[3])
        r, i = t3
        if sign < 0:
            return [add(t0, t2), (t1[0] + i, t1[1] - r), sub(t0, t2), (t1[0] - i, t1[1] + r)]
        return [add(t0, t2), (t1[0] - i, t1[1] + r), sub(t0, t2), (t1[0] + i, t1[1] - r)]
    first = {8: 2, 16: 4, 32: 8}[length]
    second = length // first
    inner = [dft(x[low::second], sign) for low in range(second)]
    out = [None] * length
    for q in range(first):
        row = [turn(inner[low][q], low * q, length, sign) for low in range(second)]
        for p, value in enumerate(dft(row, sign)):
            out[q + first * p] = value
    return out


def split(value):
    high = value.astype(BF16)
    return high, (value - high.astype(F32)).astype(BF16)


def dot(x, y, dims=((1,), (0,))):
    return lax.dot_general(x, y, (dims, ((), ())), preferred_element_type=F32)


def dot2(value, matrix):
    high, low = split(value)
    return dot(high, matrix[...]) + dot(low, matrix[...])


def pack_kernel(receiver, source, weight, out, raw, sems):
    copies = [pltpu.make_async_copy(weight, raw, sems.at[8])]
    for which, field in enumerate((receiver, source)):
        for part in range(2):
            for freq in range(2):
                rows = pl.ds(freq * 144 + which * 64 + part * 32, 32)
                sem = sems.at[which * 4 + part * 2 + freq]
                copies.append(
                    pltpu.make_async_copy(field.at[part, freq], out.at[:, rows, :], sem)
                )
    for copy in copies:
        copy.start()
    copies[0].wait()
    for freq in range(2):
        value = raw[:, freq]
        high = value >> 7
        code = 1.0 + (value & 127).astype(F32) * (1.0 / 128.0)
        for power in (1, 2, 4, 8, 16, 32):
            code = code * jnp.where((high & power) != 0, 2.0**power, 1.0)
        out[:, freq * 144 + 128 : freq * 144 + 144, :] = code.astype(BF16)
    for copy in copies[1:]:
        copy.wait()


def prepare_kernel(omega, slowness, scale, wedge_map, packed, phase, wedges, share):
    place = {name: lax.axis_index(name) for name in NAMES}
    device = 0
    for name in EVERY:
        device = device * 2 + place[name]
    step = 2.0 * math.pi / SIZE

    def signed(index):
        index = jnp.where(index >= SIZE // 2, index - SIZE, index)
        return step * index.astype(F32)

    def body(part, carry):
        row = part * 64 + lax.broadcasted_iota(jnp.int32, (64, 128), 0)
        lane = lax.broadcasted_iota(jnp.int32, (64, 128), 1)
        kx = signed((row >> 6) + 16 * ((row >> 3) & 7) + 128 * (lane & 31))
        ky = signed(device * 32 + (row & 7) + 8 * (lane >> 5))
        kx_sq = kx * kx
        ky_sq = ky * ky
        rows = pl.ds(pl.multiple_of(part * 64, 64), 64)
        for freq in range(2):
            for ref in range(2):
                number = omega[freq] * slowness[ref]
                quad = number * number - kx_sq - ky_sq
                root = jnp.sqrt(jnp.abs(quad))
                decay = jnp.exp(-root)
                inside = jnp.maximum(quad, 0.0)
                even = jnp.full_like(quad, 1.0 / math.factorial(22))
                odd = jnp.full_like(quad, 1.0 / math.factorial(23))
                for n in range(10, -1, -1):
                    even = 1.0 / math.factorial(2 * n) - inside * even
                    odd = 1.0 / math.factorial(2 * n + 1) - inside * odd
                real = jnp.where(quad >= 0, even, decay)
                imag = jnp.where(quad >= 0, odd * root, 0.0)
                phase[freq, ref, 0, rows, :] = real * scale[...]
                phase[freq, ref, 1, rows, :] = imag * scale[...]
        return carry

    lax.fori_loop(0, 16, body, 0)
    rows = wedge_map[pl.ds(place["core"] * 2 + place["y_lo"], 32, stride=4), :].astype(F32)
    wedges[...] = jnp.concatenate([rows] * 4, axis=0).T
    for half in range(2):
        for a in range(32):
            lanes = slice((a % 2) * 128, (a % 2) * 128 + 128)
            block = packed[line_rank(a // 2), half * 144 + 128 : half * 144 + 144, lanes]
            value = block.astype(F32)
            high = jnp.zeros_like(value)
            for power in (32, 16, 8, 4, 2, 1):
                over = value >= 2.0**power
                value = jnp.where(over, value * 2.0**-power, value)
                high = jnp.where(over, high + float(power), high)
            share[a, half * 16 : half * 16 + 16, :] = (high + (value - 1.0)) * (1.0 / 32.0)


def cross_forward_kernel(lines, twist, table, out, matrix, work, turned, ready, sem, sems):
    fetch = pltpu.make_async_copy(table, matrix, sem)
    fetch.start()

    def send(index):
        rows = pl.ds(pl.multiple_of(index * 16, 16), 16)
        return pltpu.make_async_copy(ready.at[index], out.at[:, rows, :], sems.at[index])

    def field(index, carry):
        start = index // 2 * 144 + index % 2 * 64
        for part in range(2):
            for low in range(4):
                values = []
                for high in range(8):
                    a = 4 * high + low
                    lanes = pl.ds((a % 2) * 128, 128)
                    pair = []
                    for side in range(2):
                        row = pl.multiple_of(start + side * 32 + part * 16, 16)
                        value = lines[line_rank(a // 2), pl.ds(row, 16), lanes]
                        pair.append(value.astype(F32))
                    values.append(tuple(pair))
                for q, value in enumerate(dft(values, -1)):
                    r, i = turn(value, low * q, 32, -1)
                    work[q, low, 0, part * 16 : part * 16 + 16, :] = r
                    work[q, low, 1, part * 16 : part * 16 + 16, :] = i

        @pl.when(index == 0)
        def _():
            fetch.wait()

        for pair in range(4):
            real, imag = [], []
            for q in (2 * pair, 2 * pair + 1):
                values = dft([(work[q, low, 0], work[q, low, 1]) for low in range(4)], -1)
                for p, value in enumerate(values):
                    k = q + 8 * p
                    r, i = times(value, (twist[0, k : k + 1, :], twist[1, k : k + 1, :]))
                    real.append(r)
                    imag.append(i)
            both = [jnp.concatenate(real, axis=0), jnp.concatenate(imag, axis=0)]
            high, low = split(jnp.concatenate(both, axis=1))
            parts = jnp.concatenate([high, low, high], axis=1)
            value = dot(matrix[...], parts, ((1,), (1,)))
            for side in range(2):
                for half in range(2):
                    turned[pl.ds(side * 8 + pair * 2 + half, 128, stride=24), :] = value[
                        side * 128 : side * 128 + 128, half * 128 : half * 128 + 128
                    ]
        ready[index] = turned[...].reshape(128, 24, 128)[:, :16].astype(BF16)
        send(index).start()
        return carry

    lax.fori_loop(0, 4, field, 0, unroll=True)
    for index in range(4):
        send(index).wait()


def inline_kernel(
    lines,
    phase,
    twist,
    twist_inv,
    table,
    table_inv,
    out,
    held,
    matrix,
    matrix_inv,
    shifts,
    work,
    spec,
    term,
    sums,
    sems,
):
    fetch = pltpu.make_async_copy(table, matrix, sems.at[2])
    fetch_inv = pltpu.make_async_copy(table_inv, matrix_inv, sems.at[3])

    def fetch_phase(freq):
        return pltpu.make_async_copy(phase.at[freq], shifts.at[freq], sems.at[freq])

    def fetch_lines(index):
        rows = pl.ds(pl.multiple_of(index * 16, 16), 16)
        return pltpu.make_async_copy(lines.at[:, rows, :], held.at[index], sems.at[4 + index])

    order = [fetch_lines(0), fetch, fetch_lines(1), fetch_phase(0), fetch_inv]
    for copy in order + [fetch_lines(2), fetch_lines(3), fetch_phase(1)]:
        copy.start()
    term[...] = jnp.zeros_like(term)

    def one_freq(freq, carry):
        def forward(which, carry):
            index = freq * 2 + which
            fetch_lines(index).wait()
            for low in range(8):
                values = []
                for high in range(16):
                    value = held[index, every_rank(8 * high + low)].astype(F32)
                    values.append((value[0:8], value[8:16]))
                for q, value in enumerate(dft(values, -1)):
                    r, i = turn(value, low * q, 128, -1)
                    work[q * 8 + low, 0] = r
                    work[q * 8 + low, 1] = i

            @pl.when(index == 0)
            def _():
                fetch.wait()

            for part in range(4):
                real, imag = [], []
                for q in range(4 * part, 4 * part + 4):
                    values = [(work[q * 8 + low, 0], work[q * 8 + low, 1]) for low in range(8)]
                    for p, value in enumerate(dft(values, -1)):
                        k = q + 16 * p
                        r, i = times(value, (twist[0, k : k + 1, :], twist[1, k : k + 1, :]))
                        real.append(r)
                        imag.append(i)
                both = [jnp.concatenate(real, axis=0), jnp.concatenate(imag, axis=0)]
                block = slice(part * 256, part * 256 + 256)
                spec[which, block, :] = dot2(jnp.concatenate(both, axis=1), matrix)
            return carry

        lax.fori_loop(0, 2, forward, 0, unroll=True)
        for part in range(4):
            block = slice(part * 256, part * 256 + 256)
            both = spec[0, block, :] * spec[1, block, :]
            term[block, :] += both[:, 0:128] + both[:, 128:256]

        fetch_phase(freq).wait()

        @pl.when(freq == 0)
        def _():
            fetch_inv.wait()

        def inverse(ref, carry):
            for part in range(4):
                block = slice(part * 256, part * 256 + 256)
                value = (spec[0, block, 0:128], spec[0, block, 128:256])
                shift = (shifts[freq, ref, 0, block, :], shifts[freq, ref, 1, block, :])
                turned = jnp.concatenate(times(value, shift), axis=1)
                turned = dot2(turned, matrix_inv)
                for j in range(4):
                    q = 4 * part + j
                    values = []
                    for p in range(8):
                        k = q + 16 * p
                        row = 64 * j + 8 * p
                        value = (turned[row : row + 8, 0:128], turned[row : row + 8, 128:256])
                        values.append(
                            times(value, (twist_inv[0, k : k + 1, :], twist_inv[1, k : k + 1, :]))
                        )
                    for low, value in enumerate(dft(values, 1)):
                        r, i = turn(value, low * q, 128, 1)
                        work[low * 16 + q, 0] = r
                        work[low * 16 + q, 1] = i
            rows = pl.ds(pl.multiple_of(freq * 32 + ref * 16, 16), 16)
            for low in range(8):
                values = [(work[low * 16 + q, 0], work[low * 16 + q, 1]) for q in range(16)]
                for high, value in enumerate(dft(values, 1)):
                    value = jnp.concatenate(value, axis=0).astype(BF16)
                    out[every_rank(8 * high + low), rows, :] = value
            return carry

        lax.fori_loop(0, 2, inverse, 0, unroll=True)
        return carry

    lax.fori_loop(0, 2, one_freq, 0)
    total = term[...].reshape(128, 8, 128).sum(axis=1)
    for q in range(16):
        sums[pl.ds(q, 8, stride=16), :] = total[8 * q : 8 * q + 8, :]
    total = sums[...]
    total = total + pltpu.roll(total, 64, 1)
    total = total + pltpu.roll(total, 32, 1)
    high = total.astype(BF16).astype(F32)
    place = lax.broadcasted_iota(jnp.int32, (128, 128), 1) >> 5
    value = jnp.where(place % 2 == 0, high, total - high).reshape(16, 8, 128).astype(BF16)
    for block in range(DEVICES):
        out[every_rank(block), 64:72, :] = value[block % GROUP]


def cross_inverse_kernel(
    lines, wedges, shares, twist, table, out, matrix, flat, work, kept, share, sems
):
    fetch = pltpu.make_async_copy(table, matrix, sems.at[0])
    fetch.start()
    fetch_share = pltpu.make_async_copy(shares, share, sems.at[1])
    fetch_share.start()
    place = lax.broadcasted_iota(jnp.int32, (8, 128), 1) >> 5
    odd = (place >> 1).astype(F32)

    def gather(d, totals):
        value = lines[d, 64:72, :].astype(F32)
        where = wedges[pl.ds(d, 1), :] - odd
        return tuple(
            total + jnp.where(where == 2.0 * j, value, 0.0) for j, total in enumerate(totals)
        )

    zero = jnp.zeros((8, 128), F32)
    totals = lax.fori_loop(0, 128, gather, (zero,) * 4, unroll=16)
    totals = [total + pltpu.roll(total, 96, 1) for total in totals]
    for half in range(2):
        value = jnp.where(place % 2 == 0, totals[2 * half], pltpu.roll(totals[2 * half + 1], 32, 1))
        value = (value * (1.0 / (SIZE * SIZE * math.sqrt(SIZE)))).astype(BF16)
        for group in range(16):
            out[group, 128:136, half * 128 : half * 128 + 128] = value

    fetch.wait()

    def one_freq(freq, carry):
        for ref in range(2):
            if ref == 1:

                @pl.when(freq == 0)
                def _():
                    fetch_share.wait()

            rows = pl.ds(pl.multiple_of(freq * 32 + ref * 16, 16), 16)
            for d in range(128):
                flat[24 * d : 24 * d + 16, :] = lines[d, rows, :].astype(F32)
            for g in range(8):
                pair = [flat[pl.ds(side * 8 + g, 128, stride=24), :] for side in range(2)]
                value = jnp.concatenate([x.T for x in pair], axis=1).astype(BF16)
                value = dot(jnp.concatenate([value, value], axis=1), matrix[...])
                values = []
                for p in range(4):
                    k = g + 8 * p
                    block = value[32 * p : 32 * p + 32, :]
                    block = (block[:, 0:128], block[:, 128:256])
                    values.append(times(block, (twist[0, k : k + 1, :], twist[1, k : k + 1, :])))
                for low, value in enumerate(dft(values, 1)):
                    r, i = turn(value, low * g, 32, 1)
                    work[low, g, 0] = r
                    work[low, g, 1] = i

            def rows16(part, carry):
                start = pl.multiple_of(part * 16, 16)
                rows = pl.ds(start, 16)
                for low in range(4):
                    values = [(work[low, g, 0, rows, :], work[low, g, 1, rows, :]) for g in range(8)]
                    for high, value in enumerate(dft(values, 1)):
                        a = 4 * high + low
                        lanes = slice((a % 2) * 128, (a % 2) * 128 + 128)
                        for side in range(2):
                            rounded = value[side].astype(BF16)
                            if ref == 0:
                                kept[a, side, rows, :] = rounded
                            else:
                                s = share[a, rows, :]
                                first = kept[a, side, rows, :].astype(F32)
                                mixed = first * s + rounded.astype(F32) * (1.0 - s)
                                row = pl.multiple_of(freq * 64 + side * 32 + part * 16, 16)
                                out[line_rank(a // 2), pl.ds(row, 16), lanes] = mixed.astype(BF16)
                return carry

            lax.fori_loop(0, 2, rows16, 0, unroll=True)
        return carry

    lax.fori_loop(0, 2, one_freq, 0)


def unpack_kernel(home, out, angles, turned, sems):
    copies = []
    for part in range(4):
        block = home.at[:, pl.ds(part * 32, 32), :]
        copies.append(pltpu.make_async_copy(block, out.at[part % 2, part // 2], sems.at[part]))
    for copy in copies:
        copy.start()
    value = home[:, 128:136, :].astype(F32)
    for half in range(2):
        flipped = value[:, :, half * 128 : half * 128 + 128].reshape(128, 128).T
        for group, wedge in enumerate((0, 2, 1, 3)):
            rows = pl.ds(half * 4 + wedge, 32, stride=8)
            turned[rows, :] = flipped[group * 32 : group * 32 + 32]
    for k in range(32):
        angles[:, k * 128 : k * 128 + 128] = turned[k * 8 : k * 8 + 8, :]
    for copy in copies:
        copy.wait()


FAR = pl.BlockSpec(memory_space=pltpu.HBM)
LOCAL = pl.BlockSpec(memory_space=pltpu.VMEM)
SCALAR = pl.BlockSpec(memory_space=pltpu.SMEM)


def near(value):
    return pltpu.with_memory_space_constraint(value, pltpu.VMEM)


def far(value):
    return pltpu.with_memory_space_constraint(value, pltpu.HBM)


def call(kernel, name, outs, out_specs, in_specs, scratch, mebibytes, args):
    return pl.pallas_call(
        kernel,
        in_specs=in_specs,
        out_specs=out_specs,
        out_shape=outs,
        scratch_shapes=scratch,
        compiler_params=pltpu.CompilerParams(vmem_limit_bytes=mebibytes * 2**20),
        name=name,
    )(*args)


def pack(receiver, source, weight):
    args = (
        far(receiver.reshape(2, 2, GROUP, 32, 256)),
        far(source.reshape(2, 2, GROUP, 32, 256)),
        far(weight.reshape(GROUP, 2, 16, 256)),
    )
    scratch = [pltpu.VMEM((GROUP, 2, 16, 256), jnp.int32), pltpu.SemaphoreType.DMA((9,))]
    outs = pltpu.VMEM((GROUP, 288, 256), BF16)
    return call(pack_kernel, "pack_fields", outs, LOCAL, [FAR] * 3, scratch, 12, args)


def prepare(omega, slowness, wedge_map, packed):
    outs = [
        pltpu.HBM((2, 2, 2, 1024, 128), F32),
        pltpu.VMEM((128, 128), F32),
        pltpu.HBM((32, 32, 128), F32),
    ]
    scale = jnp.asarray(tables()["phase_scale"])
    args = (omega, slowness, scale, wedge_map, near(packed))
    specs = [SCALAR] * 2 + [LOCAL] * 3
    return call(prepare_kernel, "prepare", outs, [LOCAL] * 3, specs, [], 16, args)


def cross_forward(packed):
    t = tables()
    args = [near(packed), near(jnp.asarray(t["cross_tw_fwd"])), jnp.asarray(t["cross_fwd"])]
    outs = pltpu.HBM((DEVICES, 64, 128), BF16)
    scratch = [
        pltpu.VMEM((256, 768), BF16),
        pltpu.VMEM((8, 4, 2, 32, 128), F32),
        pltpu.VMEM((3072, 128), F32),
        pltpu.VMEM((4, DEVICES, 16, 128), BF16),
        pltpu.SemaphoreType.DMA,
        pltpu.SemaphoreType.DMA((4,)),
    ]
    return call(
        cross_forward_kernel, "crossline_forward", outs, FAR, [LOCAL] * 2 + [FAR], scratch, 16, args
    )


def inline_step(lines, phase):
    t = tables()
    args = [far(lines), far(phase)]
    args += [near(jnp.asarray(t[n])) for n in ("inline_tw_fwd", "inline_tw_inv")]
    args += [jnp.asarray(t[n]) for n in ("inline_fwd", "inline_inv")]
    outs = pltpu.VMEM((DEVICES, 72, 128), BF16)
    scratch = [
        pltpu.VMEM((4, DEVICES, 16, 128), BF16),
        pltpu.VMEM((256, 256), BF16),
        pltpu.VMEM((256, 256), BF16),
        pltpu.VMEM((2, 2, 2, 1024, 128), F32),
        pltpu.VMEM((128, 2, 8, 128), F32),
        pltpu.VMEM((2, 1024, 256), F32),
        pltpu.VMEM((1024, 128), F32),
        pltpu.VMEM((128, 128), F32),
        pltpu.SemaphoreType.DMA((8,)),
    ]
    specs = [FAR, FAR, LOCAL, LOCAL, FAR, FAR]
    return call(inline_kernel, "inline_step", outs, LOCAL, specs, scratch, 20, args)


def cross_inverse(partial, wedges, share):
    t = tables()
    args = [near(partial), near(wedges), far(share), near(jnp.asarray(t["cross_tw_inv"]))]
    args.append(jnp.asarray(t["cross_inv"]))
    outs = pltpu.VMEM((GROUP, 136, 256), BF16)
    scratch = [
        pltpu.VMEM((512, 256), BF16),
        pltpu.VMEM((3072, 128), F32),
        pltpu.VMEM((4, 8, 2, 32, 128), F32),
        pltpu.VMEM((32, 2, 32, 128), BF16),
        pltpu.VMEM((32, 32, 128), F32),
        pltpu.SemaphoreType.DMA((2,)),
    ]
    return call(
        cross_inverse_kernel, "crossline_inverse", outs, LOCAL, [LOCAL, LOCAL, FAR, LOCAL, FAR], scratch, 16, args
    )


def unpack(home):
    outs = [
        jax.ShapeDtypeStruct((2, 2, GROUP, 32, 256), BF16),
        jax.ShapeDtypeStruct((8, SIZE), F32),
    ]
    scratch = [pltpu.VMEM((256, 128), F32), pltpu.SemaphoreType.DMA((4,))]
    specs = [FAR, LOCAL]
    return call(unpack_kernel, "unpack_fields", outs, specs, [LOCAL], scratch, 12, [near(home)])


def exchange(value, axes):
    return lax.all_to_all(value, axes, 0, 0, tiled=True)


def per_device(receiver, source, weight, omega, slowness, wedge_map):
    packed = exchange(pack(receiver, source, weight), LINE)
    phase, wedges, share = prepare(omega, slowness, wedge_map, packed)
    lines = exchange(cross_forward(packed), EVERY)
    partial = exchange(inline_step(lines, phase), EVERY)
    home = exchange(cross_inverse(partial, wedges, share), LINE)
    mixed, angles = unpack(home)
    return (mixed.reshape(2, 2, 512, 256), angles)


def solution(mesh):
    fine = Mesh(mesh.devices.reshape((2,) * 7), NAMES)
    return jax.shard_map(
        per_device,
        mesh=fine,
        in_specs=(
            P(None, None, ROWS, COLUMNS),
            P(None, None, ROWS, COLUMNS),
            P(ROWS, COLUMNS),
            P(),
            P(),
            P(),
        ),
        out_specs=(P(None, None, ROWS, COLUMNS), P()),
        check_vma=False,
    )
```

```python
import functools
import math

import jax
import jax.numpy as jnp
import ml_dtypes
import numpy as np
from jax import lax
from jax.experimental import pallas as pl
from jax.experimental.pallas import tpu as pltpu
from jax.sharding import Mesh
from jax.sharding import PartitionSpec as P

SIZE = 4096
DEVICES = 128
GROUP = 16
ROWS = ("x_hi", "z_hi", "z_lo")
COLUMNS = ("x_lo", "y_hi", "y_lo", "core")
NAMES = ROWS + COLUMNS
LINE = ("core", "y_lo", "y_hi", "x_lo")
EVERY = ("z_lo", "z_hi", "y_lo", "y_hi", "x_lo", "x_hi", "core")
BF16 = jnp.bfloat16
F32 = jnp.float32
HALF = math.sqrt(0.5)


def reorder(value, old, new):
    bits = {name: value >> place & 1 for place, name in enumerate(reversed(old))}
    return sum(bits[name] << place for place, name in enumerate(reversed(new)))


def line_rank(block):
    return reorder(block, COLUMNS, LINE)


def every_rank(block):
    return reorder(block, ROWS + LINE, EVERY)


def roots(rows, cols, length, sign):
    turn = np.outer(np.arange(rows), np.arange(cols)) % length
    return np.exp(sign * 2j * np.pi * turn / length)


def as_block(matrix):
    return np.block([[matrix.real, matrix.imag], [-matrix.imag, matrix.real]])


def two_parts(matrix):
    high = matrix.astype(np.float32).astype(ml_dtypes.bfloat16)
    low = (matrix - high.astype(np.float64)).astype(np.float32).astype(ml_dtypes.bfloat16)
    return high, low


def gains(length):
    turns = np.exp(2j * np.pi * np.arange(length) / length)
    factors = np.exp2(np.arange(4096) / 4096)
    best = []
    for row in range(length):
        entries = turns[row * np.arange(length) % length]
        entries = np.concatenate([entries.real, entries.imag])
        scaled = factors[:, None] * entries
        rounded = scaled.astype(np.float32).astype(ml_dtypes.bfloat16).astype(np.float64)
        best.append(factors[(np.square(rounded - scaled).sum(axis=1) / factors**2).argmin()])
    return np.array(best)


def pair_table(values):
    return np.stack([values.real, values.imag]).astype(np.float32)


@functools.lru_cache(None)
def tables():
    out = {}
    high, low = two_parts(as_block(roots(128, 128, 128, -1)).T)
    out["cross_fwd"] = np.concatenate([high, high, low], axis=1)
    high, low = two_parts(as_block(roots(128, 128, 128, 1)) / SIZE)
    out["cross_inv"] = np.concatenate([high, low], axis=0)
    out["cross_tw_fwd"] = pair_table(roots(32, 128, SIZE, -1))
    out["cross_tw_inv"] = pair_table(roots(32, 128, SIZE, 1))
    gain = np.tile(gains(32), 4)
    out["phase_scale"] = (1.0 / gain).astype(np.float32)[None, :]
    for name, sign, scale in (("fwd", -1, 1.0), ("inv", 1, 1.0 / SIZE)):
        lanes = np.kron(np.eye(4), roots(32, 32, 32, sign))
        high, _ = two_parts(np.tile(gain, 2)[:, None] * as_block(lanes) * scale)
        out["inline_" + name] = high
    out["inline_tw_fwd"] = pair_table(np.tile(roots(128, 32, SIZE, -1), (1, 4)) / gain)
    out["inline_tw_inv"] = pair_table(np.tile(roots(128, 32, SIZE, 1), (1, 4)))
    return out


def add(x, y):
    return (x[0] + y[0], x[1] + y[1])


def sub(x, y):
    return (x[0] - y[0], x[1] - y[1])


def times(x, y):
    return (x[0] * y[0] - x[1] * y[1], x[0] * y[1] + x[1] * y[0])


def turn(x, numerator, length, sign):
    eighth = 8 * (numerator % length) * sign % (8 * length)
    if eighth % length:
        angle = sign * 2.0 * math.pi * (numerator % length) / length
        c, s = math.cos(angle), math.sin(angle)
        return (x[0] * c - x[1] * s, x[0] * s + x[1] * c)
    eighth = eighth // length
    r, i = x
    if eighth == 0:
        return x
    if eighth == 1:
        return ((r - i) * HALF, (r + i) * HALF)
    if eighth == 2:
        return (-i, r)
    if eighth == 3:
        return ((r + i) * -HALF, (r - i) * HALF)
    if eighth == 4:
        return (-r, -i)
    if eighth == 5:
        return ((i - r) * HALF, (r + i) * -HALF)
    if eighth == 6:
        return (i, -r)
    return ((r + i) * HALF, (i - r) * HALF)


def dft(x, sign):
    length = len(x)
    if length == 2:
        return [add(x[0], x[1]), sub(x[0], x[1])]
    if length == 4:
        t0, t1 = add(x[0], x[2]), sub(x[0], x[2])
        t2, t3 = add(x[1], x[3]), sub(x[1], x[3])
        r, i = t3
        if sign < 0:
            return [add(t0, t2), (t1[0] + i, t1[1] - r), sub(t0, t2), (t1[0] - i, t1[1] + r)]
        return [add(t0, t2), (t1[0] - i, t1[1] + r), sub(t0, t2), (t1[0] + i, t1[1] - r)]
    first = {8: 2, 16: 4, 32: 8}[length]
    second = length // first
    inner = [dft(x[low::second], sign) for low in range(second)]
    out = [None] * length
    for q in range(first):
        row = [turn(inner[low][q], low * q, length, sign) for low in range(second)]
        for p, value in enumerate(dft(row, sign)):
            out[q + first * p] = value
    return out


def split(value):
    high = value.astype(BF16)
    return high, (value - high.astype(F32)).astype(BF16)


def dot(x, y, dims=((1,), (0,))):
    return lax.dot_general(x, y, (dims, ((), ())), preferred_element_type=F32)


def dot2(value, matrix):
    high, low = split(value)
    return dot(high, matrix[...]) + dot(low, matrix[...])


def pack_kernel(receiver, source, weight, out, raw, sems):
    copies = [pltpu.make_async_copy(weight, raw, sems.at[8])]
    for which, field in enumerate((receiver, source)):
        for part in range(2):
            for freq in range(2):
                rows = pl.ds(freq * 144 + which * 64 + part * 32, 32)
                sem = sems.at[which * 4 + part * 2 + freq]
                copies.append(
                    pltpu.make_async_copy(field.at[part, freq], out.at[:, rows, :], sem)
                )
    for copy in copies:
        copy.start()
    copies[0].wait()
    for freq in range(2):
        value = raw[:, freq]
        high = value >> 7
        code = 1.0 + (value & 127).astype(F32) * (1.0 / 128.0)
        for power in (1, 2, 4, 8, 16, 32):
            code = code * jnp.where((high & power) != 0, 2.0**power, 1.0)
        out[:, freq * 144 + 128 : freq * 144 + 144, :] = code.astype(BF16)
    for copy in copies[1:]:
        copy.wait()


def prepare_kernel(omega, slowness, scale, wedge_map, packed, phase, wedges, share):
    place = {name: lax.axis_index(name) for name in NAMES}
    device = 0
    for name in EVERY:
        device = device * 2 + place[name]
    step = 2.0 * math.pi / SIZE

    def signed(index):
        index = jnp.where(index >= SIZE // 2, index - SIZE, index)
        return step * index.astype(F32)

    def body(part, carry):
        row = part * 64 + lax.broadcasted_iota(jnp.int32, (64, 128), 0)
        lane = lax.broadcasted_iota(jnp.int32, (64, 128), 1)
        kx = signed((row >> 6) + 16 * ((row >> 3) & 7) + 128 * (lane & 31))
        ky = signed(device * 32 + (row & 7) + 8 * (lane >> 5))
        kx_sq = kx * kx
        ky_sq = ky * ky
        rows = pl.ds(pl.multiple_of(part * 64, 64), 64)
        for freq in range(2):
            for ref in range(2):
                number = omega[freq] * slowness[ref]
                quad = number * number - kx_sq - ky_sq
                root = jnp.sqrt(jnp.abs(quad))
                decay = jnp.exp(-root)
                inside = jnp.maximum(quad, 0.0)
                even = jnp.full_like(quad, 1.0 / math.factorial(22))
                odd = jnp.full_like(quad, 1.0 / math.factorial(23))
                for n in range(10, -1, -1):
                    even = 1.0 / math.factorial(2 * n) - inside * even
                    odd = 1.0 / math.factorial(2 * n + 1) - inside * odd
                real = jnp.where(quad >= 0, even, decay)
                imag = jnp.where(quad >= 0, odd * root, 0.0)
                phase[freq, ref, 0, rows, :] = real * scale[...]
                phase[freq, ref, 1, rows, :] = imag * scale[...]
        return carry

    lax.fori_loop(0, 16, body, 0)
    rows = wedge_map[pl.ds(place["core"] * 2 + place["y_lo"], 32, stride=4), :].astype(F32)
    wedges[...] = jnp.concatenate([rows] * 4, axis=0).T
    for half in range(2):
        for a in range(32):
            lanes = slice((a % 2) * 128, (a % 2) * 128 + 128)
            block = packed[line_rank(a // 2), half * 144 + 128 : half * 144 + 144, lanes]
            value = block.astype(F32)
            high = jnp.zeros_like(value)
            for power in (32, 16, 8, 4, 2, 1):
                over = value >= 2.0**power
                value = jnp.where(over, value * 2.0**-power, value)
                high = jnp.where(over, high + float(power), high)
            share[a, half * 16 : half * 16 + 16, :] = (high + (value - 1.0)) * (1.0 / 32.0)


def cross_forward_kernel(lines, twist, table, out, matrix, work, turned, ready, sem, sems):
    fetch = pltpu.make_async_copy(table, matrix, sem)
    fetch.start()

    def send(index):
        rows = pl.ds(pl.multiple_of(index * 16, 16), 16)
        return pltpu.make_async_copy(ready.at[index], out.at[:, rows, :], sems.at[index])

    def field(index, carry):
        start = index // 2 * 144 + index % 2 * 64
        for part in range(2):
            for low in range(4):
                values = []
                for high in range(8):
                    a = 4 * high + low
                    lanes = pl.ds((a % 2) * 128, 128)
                    pair = []
                    for side in range(2):
                        row = pl.multiple_of(start + side * 32 + part * 16, 16)
                        value = lines[line_rank(a // 2), pl.ds(row, 16), lanes]
                        pair.append(value.astype(F32))
                    values.append(tuple(pair))
                for q, value in enumerate(dft(values, -1)):
                    r, i = turn(value, low * q, 32, -1)
                    work[q, low, 0, part * 16 : part * 16 + 16, :] = r
                    work[q, low, 1, part * 16 : part * 16 + 16, :] = i

        @pl.when(index == 0)
        def _():
            fetch.wait()

        for pair in range(4):
            real, imag = [], []
            for q in (2 * pair, 2 * pair + 1):
                values = dft([(work[q, low, 0], work[q, low, 1]) for low in range(4)], -1)
                for p, value in enumerate(values):
                    k = q + 8 * p
                    r, i = times(value, (twist[0, k : k + 1, :], twist[1, k : k + 1, :]))
                    real.append(r)
                    imag.append(i)
            both = [jnp.concatenate(real, axis=0), jnp.concatenate(imag, axis=0)]
            high, low = split(jnp.concatenate(both, axis=1))
            parts = jnp.concatenate([high, low, high], axis=1)
            value = dot(matrix[...], parts, ((1,), (1,)))
            for side in range(2):
                for half in range(2):
                    turned[pl.ds(side * 8 + pair * 2 + half, 128, stride=24), :] = value[
                        side * 128 : side * 128 + 128, half * 128 : half * 128 + 128
                    ]
        ready[index] = turned[...].reshape(128, 24, 128)[:, :16].astype(BF16)
        send(index).start()
        return carry

    lax.fori_loop(0, 4, field, 0, unroll=True)
    for index in range(4):
        send(index).wait()


def inline_kernel(
    lines,
    phase,
    twist,
    twist_inv,
    table,
    table_inv,
    out,
    held,
    matrix,
    matrix_inv,
    shifts,
    work,
    spec,
    term,
    sums,
    sems,
):
    fetch = pltpu.make_async_copy(table, matrix, sems.at[2])
    fetch_inv = pltpu.make_async_copy(table_inv, matrix_inv, sems.at[3])

    def fetch_phase(freq):
        return pltpu.make_async_copy(phase.at[freq], shifts.at[freq], sems.at[freq])

    def fetch_lines(index):
        rows = pl.ds(pl.multiple_of(index * 16, 16), 16)
        return pltpu.make_async_copy(lines.at[:, rows, :], held.at[index], sems.at[4 + index])

    order = [fetch_lines(0), fetch, fetch_lines(1), fetch_phase(0), fetch_inv]
    for copy in order + [fetch_lines(2), fetch_lines(3), fetch_phase(1)]:
        copy.start()
    term[...] = jnp.zeros_like(term)

    def one_freq(freq, carry):
        def forward(which, carry):
            index = freq * 2 + which
            fetch_lines(index).wait()
            for low in range(8):
                values = []
                for high in range(16):
                    value = held[index, every_rank(8 * high + low)].astype(F32)
                    values.append((value[0:8], value[8:16]))
                for q, value in enumerate(dft(values, -1)):
                    r, i = turn(value, low * q, 128, -1)
                    work[q * 8 + low, 0] = r
                    work[q * 8 + low, 1] = i

            @pl.when(index == 0)
            def _():
                fetch.wait()

            for part in range(4):
                real, imag = [], []
                for q in range(4 * part, 4 * part + 4):
                    values = [(work[q * 8 + low, 0], work[q * 8 + low, 1]) for low in range(8)]
                    for p, value in enumerate(dft(values, -1)):
                        k = q + 16 * p
                        r, i = times(value, (twist[0, k : k + 1, :], twist[1, k : k + 1, :]))
                        real.append(r)
                        imag.append(i)
                both = [jnp.concatenate(real, axis=0), jnp.concatenate(imag, axis=0)]
                block = slice(part * 256, part * 256 + 256)
                spec[which, block, :] = dot2(jnp.concatenate(both, axis=1), matrix)
            return carry

        lax.fori_loop(0, 2, forward, 0, unroll=True)
        for part in range(4):
            block = slice(part * 256, part * 256 + 256)
            both = spec[0, block, :] * spec[1, block, :]
            term[block, :] += both[:, 0:128] + both[:, 128:256]

        fetch_phase(freq).wait()

        @pl.when(freq == 0)
        def _():
            fetch_inv.wait()

        def inverse(ref, carry):
            for part in range(4):
                block = slice(part * 256, part * 256 + 256)
                value = (spec[0, block, 0:128], spec[0, block, 128:256])
                shift = (shifts[freq, ref, 0, block, :], shifts[freq, ref, 1, block, :])
                turned = jnp.concatenate(times(value, shift), axis=1)
                turned = dot2(turned, matrix_inv)
                for j in range(4):
                    q = 4 * part + j
                    values = []
                    for p in range(8):
                        k = q + 16 * p
                        row = 64 * j + 8 * p
                        value = (turned[row : row + 8, 0:128], turned[row : row + 8, 128:256])
                        values.append(
                            times(value, (twist_inv[0, k : k + 1, :], twist_inv[1, k : k + 1, :]))
                        )
                    for low, value in enumerate(dft(values, 1)):
                        r, i = turn(value, low * q, 128, 1)
                        work[low * 16 + q, 0] = r
                        work[low * 16 + q, 1] = i
            rows = pl.ds(pl.multiple_of(freq * 32 + ref * 16, 16), 16)
            for low in range(8):
                values = [(work[low * 16 + q, 0], work[low * 16 + q, 1]) for q in range(16)]
                for high, value in enumerate(dft(values, 1)):
                    value = jnp.concatenate(value, axis=0).astype(BF16)
                    out[every_rank(8 * high + low), rows, :] = value
            return carry

        lax.fori_loop(0, 2, inverse, 0, unroll=True)
        return carry

    lax.fori_loop(0, 2, one_freq, 0)
    total = term[...].reshape(128, 8, 128).sum(axis=1)
    for q in range(16):
        sums[pl.ds(q, 8, stride=16), :] = total[8 * q : 8 * q + 8, :]
    total = sums[...]
    total = total + pltpu.roll(total, 64, 1)
    total = total + pltpu.roll(total, 32, 1)
    high = total.astype(BF16).astype(F32)
    place = lax.broadcasted_iota(jnp.int32, (128, 128), 1) >> 5
    value = jnp.where(place % 2 == 0, high, total - high).reshape(16, 8, 128).astype(BF16)
    for block in range(DEVICES):
        out[every_rank(block), 64:72, :] = value[block % GROUP]


def cross_inverse_kernel(
    lines, wedges, shares, twist, table, out, matrix, flat, work, kept, share, sems
):
    fetch = pltpu.make_async_copy(table, matrix, sems.at[0])
    fetch.start()
    fetch_share = pltpu.make_async_copy(shares, share, sems.at[1])
    fetch_share.start()
    place = lax.broadcasted_iota(jnp.int32, (8, 128), 1) >> 5
    odd = (place >> 1).astype(F32)

    def gather(d, totals):
        value = lines[d, 64:72, :].astype(F32)
        where = wedges[pl.ds(d, 1), :] - odd
        return tuple(
            total + jnp.where(where == 2.0 * j, value, 0.0) for j, total in enumerate(totals)
        )

    zero = jnp.zeros((8, 128), F32)
    totals = lax.fori_loop(0, 128, gather, (zero,) * 4, unroll=16)
    totals = [total + pltpu.roll(total, 96, 1) for total in totals]
    for half in range(2):
        value = jnp.where(place % 2 == 0, totals[2 * half], pltpu.roll(totals[2 * half + 1], 32, 1))
        value = (value * (1.0 / (SIZE * SIZE * math.sqrt(SIZE)))).astype(BF16)
        for group in range(16):
            out[group, 128:136, half * 128 : half * 128 + 128] = value

    fetch.wait()

    def one_freq(freq, carry):
        for ref in range(2):
            if ref == 1:

                @pl.when(freq == 0)
                def _():
                    fetch_share.wait()

            rows = pl.ds(pl.multiple_of(freq * 32 + ref * 16, 16), 16)
            for d in range(128):
                flat[24 * d : 24 * d + 16, :] = lines[d, rows, :].astype(F32)
            for g in range(8):
                pair = [flat[pl.ds(side * 8 + g, 128, stride=24), :] for side in range(2)]
                value = jnp.concatenate([x.T for x in pair], axis=1).astype(BF16)
                value = dot(jnp.concatenate([value, value], axis=1), matrix[...])
                values = []
                for p in range(4):
                    k = g + 8 * p
                    block = value[32 * p : 32 * p + 32, :]
                    block = (block[:, 0:128], block[:, 128:256])
                    values.append(times(block, (twist[0, k : k + 1, :], twist[1, k : k + 1, :])))
                for low, value in enumerate(dft(values, 1)):
                    r, i = turn(value, low * g, 32, 1)
                    work[low, g, 0] = r
                    work[low, g, 1] = i

            def rows16(part, carry):
                start = pl.multiple_of(part * 16, 16)
                rows = pl.ds(start, 16)
                for low in range(4):
                    values = [(work[low, g, 0, rows, :], work[low, g, 1, rows, :]) for g in range(8)]
                    for high, value in enumerate(dft(values, 1)):
                        a = 4 * high + low
                        lanes = slice((a % 2) * 128, (a % 2) * 128 + 128)
                        for side in range(2):
                            rounded = value[side].astype(BF16)
                            if ref == 0:
                                kept[a, side, rows, :] = rounded
                            else:
                                s = share[a, rows, :]
                                first = kept[a, side, rows, :].astype(F32)
                                mixed = first * s + rounded.astype(F32) * (1.0 - s)
                                row = pl.multiple_of(freq * 64 + side * 32 + part * 16, 16)
                                out[line_rank(a // 2), pl.ds(row, 16), lanes] = mixed.astype(BF16)
                return carry

            lax.fori_loop(0, 2, rows16, 0, unroll=True)
        return carry

    lax.fori_loop(0, 2, one_freq, 0)


def unpack_kernel(home, out, angles, turned, wide, sems):
    copies = []
    for part in range(4):
        block = home.at[:, pl.ds(part * 32, 32), :]
        copies.append(pltpu.make_async_copy(block, out.at[part % 2, part // 2], sems.at[part]))
    for copy in copies:
        copy.start()
    value = home[:, 128:136, :].astype(F32)
    for half in range(2):
        flipped = value[:, :, half * 128 : half * 128 + 128].reshape(128, 128).T
        for group, wedge in enumerate((0, 2, 1, 3)):
            rows = pl.ds(half * 4 + wedge, 32, stride=8)
            turned[rows, :] = flipped[group * 32 : group * 32 + 32]
    for k in range(32):
        wide[:, k * 128 : k * 128 + 128] = turned[k * 8 : k * 8 + 8, :]
    copies.append(pltpu.make_async_copy(wide, angles, sems.at[4]))
    copies[4].start()
    for copy in copies:
        copy.wait()


FAR = pl.BlockSpec(memory_space=pltpu.HBM)
LOCAL = pl.BlockSpec(memory_space=pltpu.VMEM)
SCALAR = pl.BlockSpec(memory_space=pltpu.SMEM)


def near(value):
    return pltpu.with_memory_space_constraint(value, pltpu.VMEM)


def far(value):
    return pltpu.with_memory_space_constraint(value, pltpu.HBM)


def call(kernel, name, outs, out_specs, in_specs, scratch, mebibytes, args):
    return pl.pallas_call(
        kernel,
        in_specs=in_specs,
        out_specs=out_specs,
        out_shape=outs,
        scratch_shapes=scratch,
        compiler_params=pltpu.CompilerParams(vmem_limit_bytes=mebibytes * 2**20),
        name=name,
    )(*args)


def pack(receiver, source, weight):
    args = (
        far(receiver.reshape(2, 2, GROUP, 32, 256)),
        far(source.reshape(2, 2, GROUP, 32, 256)),
        far(weight.reshape(GROUP, 2, 16, 256)),
    )
    scratch = [pltpu.VMEM((GROUP, 2, 16, 256), jnp.int32), pltpu.SemaphoreType.DMA((9,))]
    outs = pltpu.VMEM((GROUP, 288, 256), BF16)
    return call(pack_kernel, "pack_fields", outs, LOCAL, [FAR] * 3, scratch, 12, args)


def prepare(omega, slowness, wedge_map, packed):
    outs = [
        pltpu.HBM((2, 2, 2, 1024, 128), F32),
        pltpu.VMEM((128, 128), F32),
        pltpu.HBM((32, 32, 128), F32),
    ]
    scale = jnp.asarray(tables()["phase_scale"])
    args = (omega, slowness, scale, wedge_map, near(packed))
    specs = [SCALAR] * 2 + [LOCAL] * 3
    return call(prepare_kernel, "prepare", outs, [LOCAL] * 3, specs, [], 16, args)


def cross_forward(packed):
    t = tables()
    args = [near(packed), near(jnp.asarray(t["cross_tw_fwd"])), jnp.asarray(t["cross_fwd"])]
    outs = pltpu.HBM((DEVICES, 64, 128), BF16)
    scratch = [
        pltpu.VMEM((256, 768), BF16),
        pltpu.VMEM((8, 4, 2, 32, 128), F32),
        pltpu.VMEM((3072, 128), F32),
        pltpu.VMEM((4, DEVICES, 16, 128), BF16),
        pltpu.SemaphoreType.DMA,
        pltpu.SemaphoreType.DMA((4,)),
    ]
    return call(
        cross_forward_kernel, "crossline_forward", outs, FAR, [LOCAL] * 2 + [FAR], scratch, 16, args
    )


def inline_step(lines, phase):
    t = tables()
    args = [far(lines), far(phase)]
    args += [near(jnp.asarray(t[n])) for n in ("inline_tw_fwd", "inline_tw_inv")]
    args += [jnp.asarray(t[n]) for n in ("inline_fwd", "inline_inv")]
    outs = pltpu.VMEM((DEVICES, 72, 128), BF16)
    scratch = [
        pltpu.VMEM((4, DEVICES, 16, 128), BF16),
        pltpu.VMEM((256, 256), BF16),
        pltpu.VMEM((256, 256), BF16),
        pltpu.VMEM((2, 2, 2, 1024, 128), F32),
        pltpu.VMEM((128, 2, 8, 128), F32),
        pltpu.VMEM((2, 1024, 256), F32),
        pltpu.VMEM((1024, 128), F32),
        pltpu.VMEM((128, 128), F32),
        pltpu.SemaphoreType.DMA((8,)),
    ]
    specs = [FAR, FAR, LOCAL, LOCAL, FAR, FAR]
    return call(inline_kernel, "inline_step", outs, LOCAL, specs, scratch, 20, args)


def cross_inverse(partial, wedges, share):
    t = tables()
    args = [near(partial), near(wedges), far(share), near(jnp.asarray(t["cross_tw_inv"]))]
    args.append(jnp.asarray(t["cross_inv"]))
    outs = pltpu.VMEM((GROUP, 136, 256), BF16)
    scratch = [
        pltpu.VMEM((512, 256), BF16),
        pltpu.VMEM((3072, 128), F32),
        pltpu.VMEM((4, 8, 2, 32, 128), F32),
        pltpu.VMEM((32, 2, 32, 128), BF16),
        pltpu.VMEM((32, 32, 128), F32),
        pltpu.SemaphoreType.DMA((2,)),
    ]
    return call(
        cross_inverse_kernel, "crossline_inverse", outs, LOCAL, [LOCAL, LOCAL, FAR, LOCAL, FAR], scratch, 16, args
    )


def unpack(home):
    outs = [
        pltpu.HBM((2, 2, GROUP, 32, 256), BF16),
        pltpu.HBM((8, SIZE), F32),
    ]
    scratch = [
        pltpu.VMEM((256, 128), F32),
        pltpu.VMEM((8, SIZE), F32),
        pltpu.SemaphoreType.DMA((5,)),
    ]
    specs = [FAR, FAR]
    return call(unpack_kernel, "unpack_fields", outs, specs, [LOCAL], scratch, 12, [near(home)])


def exchange(value, axes):
    return lax.all_to_all(value, axes, 0, 0, tiled=True)


def per_device(receiver, source, weight, omega, slowness, wedge_map):
    packed = exchange(pack(receiver, source, weight), LINE)
    phase, wedges, share = prepare(omega, slowness, wedge_map, packed)
    lines = exchange(cross_forward(packed), EVERY)
    partial = exchange(inline_step(lines, phase), EVERY)
    home = exchange(cross_inverse(partial, wedges, share), LINE)
    mixed, angles = unpack(home)
    return (mixed.reshape(2, 2, 512, 256), angles)


def solution(mesh):
    fine = Mesh(mesh.devices.reshape((2,) * 7), NAMES)
    return jax.shard_map(
        per_device,
        mesh=fine,
        in_specs=(
            P(None, None, ROWS, COLUMNS),
            P(None, None, ROWS, COLUMNS),
            P(ROWS, COLUMNS),
            P(),
            P(),
            P(),
        ),
        out_specs=(P(None, None, ROWS, COLUMNS), P()),
        check_vma=False,
    )
```

```python
import functools
import math

import jax
import jax.numpy as jnp
import ml_dtypes
import numpy as np
from jax import lax
from jax.experimental import pallas as pl
from jax.experimental.pallas import tpu as pltpu
from jax.sharding import Mesh
from jax.sharding import PartitionSpec as P

SIZE = 4096
DEVICES = 128
GROUP = 16
ROWS = ("x_hi", "z_hi", "z_lo")
COLUMNS = ("x_lo", "y_hi", "y_lo", "core")
NAMES = ROWS + COLUMNS
LINE = ("core", "y_lo", "y_hi", "x_lo")
EVERY = ("z_lo", "z_hi", "y_lo", "y_hi", "x_lo", "x_hi", "core")
MESSAGE = 66
BF16 = jnp.bfloat16
F32 = jnp.float32
HALF = math.sqrt(0.5)


def reorder(value, old, new):
    bits = {name: value >> place & 1 for place, name in enumerate(reversed(old))}
    return sum(bits[name] << place for place, name in enumerate(reversed(new)))


def line_rank(block):
    return reorder(block, COLUMNS, LINE)


def every_rank(block):
    return reorder(block, ROWS + LINE, EVERY)


def roots(rows, cols, length, sign):
    turn = np.outer(np.arange(rows), np.arange(cols)) % length
    return np.exp(sign * 2j * np.pi * turn / length)


def as_block(matrix):
    return np.block([[matrix.real, matrix.imag], [-matrix.imag, matrix.real]])


def two_parts(matrix):
    high = matrix.astype(np.float32).astype(ml_dtypes.bfloat16)
    low = (matrix - high.astype(np.float64)).astype(np.float32).astype(ml_dtypes.bfloat16)
    return high, low


def gains(length):
    turns = np.exp(2j * np.pi * np.arange(length) / length)
    factors = np.exp2(np.arange(4096) / 4096)
    best = []
    for row in range(length):
        entries = turns[row * np.arange(length) % length]
        entries = np.concatenate([entries.real, entries.imag])
        scaled = factors[:, None] * entries
        rounded = scaled.astype(np.float32).astype(ml_dtypes.bfloat16).astype(np.float64)
        best.append(factors[(np.square(rounded - scaled).sum(axis=1) / factors**2).argmin()])
    return np.array(best)


def pair_table(values):
    return np.stack([values.real, values.imag]).astype(np.float32)


@functools.lru_cache(None)
def tables():
    out = {}
    high, low = two_parts(as_block(roots(128, 128, 128, -1)).T)
    out["cross_fwd"] = np.concatenate([high, high, low], axis=1)
    high, low = two_parts(as_block(roots(128, 128, 128, 1)) / SIZE)
    out["cross_inv"] = np.concatenate([high, low], axis=0)
    out["cross_tw_fwd"] = pair_table(roots(32, 128, SIZE, -1))
    out["cross_tw_inv"] = pair_table(roots(32, 128, SIZE, 1))
    gain = np.tile(gains(32), 4)
    out["phase_scale"] = (1.0 / gain).astype(np.float32)[None, :]
    for name, sign, scale in (("fwd", -1, 1.0), ("inv", 1, 1.0 / SIZE)):
        lanes = np.kron(np.eye(4), roots(32, 32, 32, sign))
        high, _ = two_parts(np.tile(gain, 2)[:, None] * as_block(lanes) * scale)
        out["inline_" + name] = high
    out["inline_tw_fwd"] = pair_table(np.tile(roots(128, 32, SIZE, -1), (1, 4)) / gain)
    out["inline_tw_inv"] = pair_table(np.tile(roots(128, 32, SIZE, 1), (1, 4)))
    return out


def add(x, y):
    return (x[0] + y[0], x[1] + y[1])


def sub(x, y):
    return (x[0] - y[0], x[1] - y[1])


def times(x, y):
    return (x[0] * y[0] - x[1] * y[1], x[0] * y[1] + x[1] * y[0])


def turn(x, numerator, length, sign):
    eighth = 8 * (numerator % length) * sign % (8 * length)
    if eighth % length:
        angle = sign * 2.0 * math.pi * (numerator % length) / length
        c, s = math.cos(angle), math.sin(angle)
        return (x[0] * c - x[1] * s, x[0] * s + x[1] * c)
    eighth = eighth // length
    r, i = x
    if eighth == 0:
        return x
    if eighth == 1:
        return ((r - i) * HALF, (r + i) * HALF)
    if eighth == 2:
        return (-i, r)
    if eighth == 3:
        return ((r + i) * -HALF, (r - i) * HALF)
    if eighth == 4:
        return (-r, -i)
    if eighth == 5:
        return ((i - r) * HALF, (r + i) * -HALF)
    if eighth == 6:
        return (i, -r)
    return ((r + i) * HALF, (i - r) * HALF)


def dft(x, sign):
    length = len(x)
    if length == 2:
        return [add(x[0], x[1]), sub(x[0], x[1])]
    if length == 4:
        t0, t1 = add(x[0], x[2]), sub(x[0], x[2])
        t2, t3 = add(x[1], x[3]), sub(x[1], x[3])
        r, i = t3
        if sign < 0:
            return [add(t0, t2), (t1[0] + i, t1[1] - r), sub(t0, t2), (t1[0] - i, t1[1] + r)]
        return [add(t0, t2), (t1[0] - i, t1[1] + r), sub(t0, t2), (t1[0] + i, t1[1] - r)]
    first = {8: 2, 16: 4, 32: 8}[length]
    second = length // first
    inner = [dft(x[low::second], sign) for low in range(second)]
    out = [None] * length
    for q in range(first):
        row = [turn(inner[low][q], low * q, length, sign) for low in range(second)]
        for p, value in enumerate(dft(row, sign)):
            out[q + first * p] = value
    return out


def split(value):
    high = value.astype(BF16)
    return high, (value - high.astype(F32)).astype(BF16)


def dot(x, y, dims=((1,), (0,))):
    return lax.dot_general(x, y, (dims, ((), ())), preferred_element_type=F32)


def dot2(value, matrix):
    high, low = split(value)
    return dot(high, matrix[...]) + dot(low, matrix[...])


def pack_kernel(receiver, source, weight, out, raw, sems):
    copies = [pltpu.make_async_copy(weight, raw, sems.at[8])]
    for which, field in enumerate((receiver, source)):
        for part in range(2):
            for freq in range(2):
                rows = pl.ds(freq * 144 + which * 64 + part * 32, 32)
                sem = sems.at[which * 4 + part * 2 + freq]
                copies.append(
                    pltpu.make_async_copy(field.at[part, freq], out.at[:, rows, :], sem)
                )
    for copy in copies:
        copy.start()
    copies[0].wait()
    for freq in range(2):
        value = raw[:, freq]
        high = value >> 7
        code = 1.0 + (value & 127).astype(F32) * (1.0 / 128.0)
        for power in (1, 2, 4, 8, 16, 32):
            code = code * jnp.where((high & power) != 0, 2.0**power, 1.0)
        out[:, freq * 144 + 128 : freq * 144 + 144, :] = code.astype(BF16)
    for copy in copies[1:]:
        copy.wait()


def prepare_kernel(
    omega, slowness, scale, wedge_map, packed, phase, wedges, share, tiles
):
    place = {name: lax.axis_index(name) for name in NAMES}
    device = 0
    for name in EVERY:
        device = device * 2 + place[name]
    step = 2.0 * math.pi / SIZE

    def signed(index):
        index = jnp.where(index >= SIZE // 2, index - SIZE, index)
        return step * index.astype(F32)

    def body(part, carry):
        row = part * 64 + lax.broadcasted_iota(jnp.int32, (64, 128), 0)
        lane = lax.broadcasted_iota(jnp.int32, (64, 128), 1)
        kx = signed((row >> 6) + 16 * ((row >> 3) & 7) + 128 * (lane & 31))
        ky = signed(device * 32 + (row & 7) + 8 * (lane >> 5))
        kx_sq = kx * kx
        ky_sq = ky * ky
        rows = pl.ds(pl.multiple_of(part * 64, 64), 64)
        for freq in range(2):
            for ref in range(2):
                number = omega[freq] * slowness[ref]
                quad = number * number - kx_sq - ky_sq
                root = jnp.sqrt(jnp.abs(quad))
                decay = jnp.exp(-root)
                inside = jnp.maximum(quad, 0.0)
                even = jnp.full_like(quad, 1.0 / math.factorial(22))
                odd = jnp.full_like(quad, 1.0 / math.factorial(23))
                for n in range(10, -1, -1):
                    even = 1.0 / math.factorial(2 * n) - inside * even
                    odd = 1.0 / math.factorial(2 * n + 1) - inside * odd
                real = jnp.where(quad >= 0, even, decay)
                imag = jnp.where(quad >= 0, odd * root, 0.0)
                phase[freq, ref, 0, rows, :] = real * scale[...]
                phase[freq, ref, 1, rows, :] = imag * scale[...]
        return carry

    lax.fori_loop(0, 16, body, 0)
    tiles[0:128, :] = wedge_map[...].astype(F32)
    rows = [tiles[pl.ds(high, 32, stride=4), :] for high in range(4)]
    rows = jnp.concatenate(rows, axis=0).T
    wedges[pl.ds(0, 128, stride=2), :] = rows
    wedges[pl.ds(1, 128, stride=2), :] = rows
    for half in range(2):
        for a in range(32):
            lanes = slice((a % 2) * 128, (a % 2) * 128 + 128)
            block = packed[line_rank(a // 2), half * 144 + 128 : half * 144 + 144, lanes]
            value = block.astype(F32)
            high = jnp.zeros_like(value)
            for power in (32, 16, 8, 4, 2, 1):
                over = value >= 2.0**power
                value = jnp.where(over, value * 2.0**-power, value)
                high = jnp.where(over, high + float(power), high)
            share[a, half * 16 : half * 16 + 16, :] = (high + (value - 1.0)) * (1.0 / 32.0)


def cross_forward_kernel(lines, twist, table, out, matrix, work, turned, ready, sem, sems):
    fetch = pltpu.make_async_copy(table, matrix, sem)
    fetch.start()

    def send(index):
        rows = pl.ds(pl.multiple_of(index * 16, 16), 16)
        return pltpu.make_async_copy(ready.at[index], out.at[:, rows, :], sems.at[index])

    def field(index, carry):
        start = index // 2 * 144 + index % 2 * 64
        for part in range(2):
            for low in range(4):
                values = []
                for high in range(8):
                    a = 4 * high + low
                    lanes = pl.ds((a % 2) * 128, 128)
                    pair = []
                    for side in range(2):
                        row = pl.multiple_of(start + side * 32 + part * 16, 16)
                        value = lines[line_rank(a // 2), pl.ds(row, 16), lanes]
                        pair.append(value.astype(F32))
                    values.append(tuple(pair))
                for q, value in enumerate(dft(values, -1)):
                    r, i = turn(value, low * q, 32, -1)
                    work[q, low, 0, part * 16 : part * 16 + 16, :] = r
                    work[q, low, 1, part * 16 : part * 16 + 16, :] = i

        @pl.when(index == 0)
        def _():
            fetch.wait()

        for pair in range(4):
            real, imag = [], []
            for q in (2 * pair, 2 * pair + 1):
                values = dft([(work[q, low, 0], work[q, low, 1]) for low in range(4)], -1)
                for p, value in enumerate(values):
                    k = q + 8 * p
                    r, i = times(value, (twist[0, k : k + 1, :], twist[1, k : k + 1, :]))
                    real.append(r)
                    imag.append(i)
            both = [jnp.concatenate(real, axis=0), jnp.concatenate(imag, axis=0)]
            high, low = split(jnp.concatenate(both, axis=1))
            parts = jnp.concatenate([high, low, high], axis=1)
            value = dot(matrix[...], parts, ((1,), (1,)))
            for side in range(2):
                for half in range(2):
                    turned[pl.ds(side * 8 + pair * 2 + half, 128, stride=24), :] = value[
                        side * 128 : side * 128 + 128, half * 128 : half * 128 + 128
                    ]
        ready[index] = turned[0:3072, :].reshape(128, 24, 128)[:, :16].astype(BF16)
        send(index).start()
        return carry

    lax.fori_loop(0, 4, field, 0, unroll=True)
    for index in range(4):
        send(index).wait()


def inline_kernel(
    lines,
    phase,
    twist,
    twist_inv,
    table,
    table_inv,
    out,
    held,
    matrix,
    matrix_inv,
    shifts,
    work,
    spec,
    term,
    sums,
    sems,
):
    fetch = pltpu.make_async_copy(table, matrix, sems.at[2])
    fetch_inv = pltpu.make_async_copy(table_inv, matrix_inv, sems.at[3])

    def fetch_phase(freq):
        return pltpu.make_async_copy(phase.at[freq], shifts.at[freq], sems.at[freq])

    def fetch_lines(index):
        rows = pl.ds(index * 16, 16)
        return pltpu.make_async_copy(lines.at[:, rows, :], held.at[index], sems.at[4 + index])

    order = [fetch_lines(0), fetch, fetch_lines(1), fetch_phase(0), fetch_inv]
    for copy in order + [fetch_lines(2), fetch_lines(3), fetch_phase(1)]:
        copy.start()
    term[...] = jnp.zeros_like(term)

    def one_freq(freq):
        def forward(which):
            index = freq * 2 + which
            fetch_lines(index).wait()
            for low in range(8):
                values = []
                for high in range(16):
                    value = held[index, every_rank(8 * high + low)].astype(F32)
                    values.append((value[0:8], value[8:16]))
                for q, value in enumerate(dft(values, -1)):
                    r, i = turn(value, low * q, 128, -1)
                    work[q * 8 + low, 0] = r
                    work[q * 8 + low, 1] = i

            if index == 0:
                fetch.wait()
            for part in range(4):
                real, imag = [], []
                for q in range(4 * part, 4 * part + 4):
                    values = [(work[q * 8 + low, 0], work[q * 8 + low, 1]) for low in range(8)]
                    for p, value in enumerate(dft(values, -1)):
                        k = q + 16 * p
                        r, i = times(value, (twist[0, k : k + 1, :], twist[1, k : k + 1, :]))
                        real.append(r)
                        imag.append(i)
                both = [jnp.concatenate(real, axis=0), jnp.concatenate(imag, axis=0)]
                block = slice(part * 256, part * 256 + 256)
                spec[which, block, :] = dot2(jnp.concatenate(both, axis=1), matrix)

        for which in range(2):
            forward(which)
        for part in range(4):
            block = slice(part * 256, part * 256 + 256)
            both = spec[0, block, :] * spec[1, block, :]
            term[block, :] += both[:, 0:128] + both[:, 128:256]

        fetch_phase(freq).wait()

        if freq == 0:
            fetch_inv.wait()

        def inverse(ref):
            for part in range(4):
                block = slice(part * 256, part * 256 + 256)
                value = (spec[0, block, 0:128], spec[0, block, 128:256])
                shift = (shifts[freq, ref, 0, block, :], shifts[freq, ref, 1, block, :])
                turned = jnp.concatenate(times(value, shift), axis=1)
                turned = dot2(turned, matrix_inv)
                for j in range(4):
                    q = 4 * part + j
                    values = []
                    for p in range(8):
                        k = q + 16 * p
                        row = 64 * j + 8 * p
                        value = (turned[row : row + 8, 0:128], turned[row : row + 8, 128:256])
                        values.append(
                            times(value, (twist_inv[0, k : k + 1, :], twist_inv[1, k : k + 1, :]))
                        )
                    for low, value in enumerate(dft(values, 1)):
                        r, i = turn(value, low * q, 128, 1)
                        work[low * 16 + q, 0] = r
                        work[low * 16 + q, 1] = i
            for low in range(8):
                values = [(work[low * 16 + q, 0], work[low * 16 + q, 1]) for q in range(16)]
                for high, value in enumerate(dft(values, 1)):
                    value = jnp.concatenate(value, axis=0).astype(BF16)
                    start = every_rank(8 * high + low) * MESSAGE + freq * 32 + ref * 16
                    out[start : start + 16, :] = value

        for ref in range(2):
            inverse(ref)

    for freq in range(2):
        one_freq(freq)
    total = term[...].reshape(128, 8, 128).sum(axis=1)
    for q in range(16):
        sums[pl.ds(q, 8, stride=16), :] = total[8 * q : 8 * q + 8, :]
    total = sums[0:128, :]
    total = total + pltpu.roll(total, 64, 1)
    total = total + pltpu.roll(total, 32, 1)
    place = lax.broadcasted_iota(jnp.int32, (32, 128), 1) >> 5
    value = total[0:32, :]
    for u in range(1, 4):
        value = jnp.where(place == u, total[32 * u : 32 * u + 32, :], value)
    for v in range(2):
        sums[pl.ds(v, 16, stride=2), :] = value[16 * v : 16 * v + 16, :]
    value = sums[0:32, :].astype(BF16)
    for block in range(DEVICES):
        start = every_rank(block) * MESSAGE + 64
        line = block % GROUP
        out[start : start + 2, :] = value[2 * line : 2 * line + 2, :]


def cross_inverse_kernel(
    lines, wedges, shares, twist, table, out, matrix, flat, work, kept, share, sems
):
    fetch = pltpu.make_async_copy(table, matrix, sems.at[0])
    fetch.start()
    fetch_share = pltpu.make_async_copy(shares, share, sems.at[1])
    fetch_share.start()
    for d in range(DEVICES):
        flat[2 * d : 2 * d + 2, :] = lines[d * MESSAGE + 64 : d * MESSAGE + 66, :].astype(F32)

    def gather(step, totals):
        rows = pl.ds(pl.multiple_of(step * 8, 8), 8)
        value, where = flat[rows, :], wedges[rows, :]
        return tuple(
            total + jnp.where(where == float(w), value, 0.0) for w, total in enumerate(totals)
        )

    zero = jnp.zeros((8, 128), F32)
    totals = lax.fori_loop(0, 32, gather, (zero,) * 8, unroll=8)
    totals = [t[0:2] + t[2:4] + (t[4:6] + t[6:8]) for t in totals]
    for half in range(2):
        value = jnp.concatenate(totals[4 * half : 4 * half + 4], axis=0)
        value = (value * (1.0 / (SIZE * SIZE * math.sqrt(SIZE)))).astype(BF16)
        for group in range(16):
            out[group, 128:136, half * 128 : half * 128 + 128] = value

    fetch.wait()

    def one_freq(freq):
        for ref in range(2):
            if freq == 0 and ref == 1:
                fetch_share.wait()

            for d in range(128):
                rows = pl.ds(d * MESSAGE + freq * 32 + ref * 16, 16)
                flat[24 * d : 24 * d + 16, :] = lines[rows, :].astype(F32)
            for g in range(8):
                pair = [flat[pl.ds(side * 8 + g, 128, stride=24), :] for side in range(2)]
                value = jnp.concatenate([x.T for x in pair], axis=1).astype(BF16)
                value = dot(jnp.concatenate([value, value], axis=1), matrix[...])
                values = []
                for p in range(4):
                    k = g + 8 * p
                    block = value[32 * p : 32 * p + 32, :]
                    block = (block[:, 0:128], block[:, 128:256])
                    values.append(times(block, (twist[0, k : k + 1, :], twist[1, k : k + 1, :])))
                for low, value in enumerate(dft(values, 1)):
                    r, i = turn(value, low * g, 32, 1)
                    work[low, g, 0] = r
                    work[low, g, 1] = i

            def rows16(part, carry):
                start = pl.multiple_of(part * 16, 16)
                rows = pl.ds(start, 16)
                for low in range(4):
                    values = [(work[low, g, 0, rows, :], work[low, g, 1, rows, :]) for g in range(8)]
                    for high, value in enumerate(dft(values, 1)):
                        a = 4 * high + low
                        lanes = slice((a % 2) * 128, (a % 2) * 128 + 128)
                        for side in range(2):
                            rounded = value[side].astype(BF16)
                            if ref == 0:
                                kept[a, side, rows, :] = rounded
                            else:
                                s = share[a, rows, :]
                                first = kept[a, side, rows, :].astype(F32)
                                mixed = first * s + rounded.astype(F32) * (1.0 - s)
                                row = pl.multiple_of(freq * 64 + side * 32 + part * 16, 16)
                                out[line_rank(a // 2), pl.ds(row, 16), lanes] = mixed.astype(BF16)
                return carry

            lax.fori_loop(0, 2, rows16, 0, unroll=True)

    for freq in range(2):
        one_freq(freq)


def unpack_kernel(home, out, angles, coded, turned, wide, sems):
    copies = []
    for part in range(4):
        block = home.at[:, pl.ds(part * 32, 32), :]
        copies.append(pltpu.make_async_copy(block, out.at[part % 2, part // 2], sems.at[part]))
    for copy in copies:
        copy.start()
    place = lax.broadcasted_iota(jnp.int32, (32, 128), 1) >> 5
    for half in range(2):
        rows = home[:, 128:136, half * 128 : half * 128 + 128].astype(F32)
        coded[0:128, :] = rows.reshape(128, 128)
        rows = [coded[pl.ds(r, 16, stride=8), :] for r in range(8)]
        flipped = jnp.concatenate(rows, axis=0).T
        for w in range(4):
            value = pltpu.roll(flipped[0:32], (4 - w) * 32 % 128, 1)
            for u in range(1, 4):
                part = pltpu.roll(flipped[32 * u : 32 * u + 32], (4 + u - w) * 32 % 128, 1)
                value = jnp.where(place == u, part, value)
            turned[pl.ds(half * 4 + w, 32, stride=8), :] = value
    for k in range(32):
        wide[:, k * 128 : k * 128 + 128] = turned[k * 8 : k * 8 + 8, :]
    copies.append(pltpu.make_async_copy(wide, angles, sems.at[4]))
    copies[4].start()
    for copy in copies:
        copy.wait()


FAR = pl.BlockSpec(memory_space=pltpu.HBM)
LOCAL = pl.BlockSpec(memory_space=pltpu.VMEM)
SCALAR = pl.BlockSpec(memory_space=pltpu.SMEM)


def near(value):
    return pltpu.with_memory_space_constraint(value, pltpu.VMEM)


def far(value):
    return pltpu.with_memory_space_constraint(value, pltpu.HBM)


def call(kernel, name, outs, out_specs, in_specs, scratch, mebibytes, args):
    return pl.pallas_call(
        kernel,
        in_specs=in_specs,
        out_specs=out_specs,
        out_shape=outs,
        scratch_shapes=scratch,
        compiler_params=pltpu.CompilerParams(vmem_limit_bytes=mebibytes * 2**20),
        name=name,
    )(*args)


def pack(receiver, source, weight):
    args = (
        far(receiver.reshape(2, 2, GROUP, 32, 256)),
        far(source.reshape(2, 2, GROUP, 32, 256)),
        far(weight.reshape(GROUP, 2, 16, 256)),
    )
    scratch = [pltpu.VMEM((GROUP, 2, 16, 256), jnp.int32), pltpu.SemaphoreType.DMA((9,))]
    outs = pltpu.VMEM((GROUP, 288, 256), BF16)
    return call(pack_kernel, "pack_fields", outs, LOCAL, [FAR] * 3, scratch, 12, args)


def prepare(omega, slowness, wedge_map, packed):
    outs = [
        pltpu.HBM((2, 2, 2, 1024, 128), F32),
        pltpu.VMEM((264, 128), F32),
        pltpu.HBM((32, 32, 128), F32),
    ]
    scale = jnp.asarray(tables()["phase_scale"])
    args = (omega, slowness, scale, wedge_map, near(packed))
    specs = [SCALAR] * 2 + [LOCAL] * 3
    scratch = [pltpu.VMEM((136, 128), F32)]
    return call(prepare_kernel, "prepare", outs, [LOCAL] * 3, specs, scratch, 16, args)


def cross_forward(packed):
    t = tables()
    args = [near(packed), near(jnp.asarray(t["cross_tw_fwd"])), jnp.asarray(t["cross_fwd"])]
    outs = pltpu.HBM((DEVICES, 64, 128), BF16)
    scratch = [
        pltpu.VMEM((256, 768), BF16),
        pltpu.VMEM((8, 4, 2, 32, 128), F32),
        pltpu.VMEM((3096, 128), F32),
        pltpu.VMEM((4, DEVICES, 16, 128), BF16),
        pltpu.SemaphoreType.DMA,
        pltpu.SemaphoreType.DMA((4,)),
    ]
    return call(
        cross_forward_kernel, "crossline_forward", outs, FAR, [LOCAL] * 2 + [FAR], scratch, 16, args
    )


def inline_step(lines, phase):
    t = tables()
    args = [far(lines), far(phase)]
    args += [near(jnp.asarray(t[n])) for n in ("inline_tw_fwd", "inline_tw_inv")]
    args += [jnp.asarray(t[n]) for n in ("inline_fwd", "inline_inv")]
    outs = pltpu.VMEM((DEVICES * MESSAGE, 128), BF16)
    scratch = [
        pltpu.VMEM((4, DEVICES, 16, 128), BF16),
        pltpu.VMEM((256, 256), BF16),
        pltpu.VMEM((256, 256), BF16),
        pltpu.VMEM((2, 2, 2, 1024, 128), F32),
        pltpu.VMEM((128, 2, 8, 128), F32),
        pltpu.VMEM((2, 1024, 256), F32),
        pltpu.VMEM((1024, 128), F32),
        pltpu.VMEM((144, 128), F32),
        pltpu.SemaphoreType.DMA((8,)),
    ]
    specs = [FAR, FAR, LOCAL, LOCAL, FAR, FAR]
    return call(inline_kernel, "inline_step", outs, LOCAL, specs, scratch, 20, args)


def cross_inverse(partial, wedges, share):
    t = tables()
    args = [near(partial), near(wedges), far(share), near(jnp.asarray(t["cross_tw_inv"]))]
    args.append(jnp.asarray(t["cross_inv"]))
    outs = pltpu.VMEM((GROUP, 136, 256), BF16)
    scratch = [
        pltpu.VMEM((512, 256), BF16),
        pltpu.VMEM((3096, 128), F32),
        pltpu.VMEM((4, 8, 2, 32, 128), F32),
        pltpu.VMEM((32, 2, 32, 128), BF16),
        pltpu.VMEM((32, 32, 128), F32),
        pltpu.SemaphoreType.DMA((2,)),
    ]
    return call(
        cross_inverse_kernel, "crossline_inverse", outs, LOCAL, [LOCAL, LOCAL, FAR, LOCAL, FAR], scratch, 16, args
    )


def unpack(home):
    outs = [
        pltpu.HBM((2, 2, GROUP, 32, 256), BF16),
        pltpu.HBM((8, SIZE), F32),
    ]
    scratch = [
        pltpu.VMEM((136, 128), F32),
        pltpu.VMEM((264, 128), F32),
        pltpu.VMEM((8, SIZE), F32),
        pltpu.SemaphoreType.DMA((5,)),
    ]
    specs = [FAR, FAR]
    return call(unpack_kernel, "unpack_fields", outs, specs, [LOCAL], scratch, 12, [near(home)])


def exchange(value, axes):
    return lax.all_to_all(value, axes, 0, 0, tiled=True)


def per_device(receiver, source, weight, omega, slowness, wedge_map):
    packed = exchange(pack(receiver, source, weight), LINE)
    phase, wedges, share = prepare(omega, slowness, wedge_map, packed)
    lines = exchange(cross_forward(packed), EVERY)
    partial = inline_step(lines, phase).reshape(DEVICES, MESSAGE // 2, 2, 128)
    partial = exchange(partial, EVERY).reshape(DEVICES * MESSAGE, 128)
    home = exchange(cross_inverse(partial, wedges, share), LINE)
    mixed, angles = unpack(home)
    return (mixed.reshape(2, 2, 512, 256), angles)


def solution(mesh):
    fine = Mesh(mesh.devices.reshape((2,) * 7), NAMES)
    return jax.shard_map(
        per_device,
        mesh=fine,
        in_specs=(
            P(None, None, ROWS, COLUMNS),
            P(None, None, ROWS, COLUMNS),
            P(ROWS, COLUMNS),
            P(),
            P(),
            P(),
        ),
        out_specs=(P(None, None, ROWS, COLUMNS), P()),
        check_vma=False,
    )
```

```python
import functools
import math

import jax
import jax.numpy as jnp
import ml_dtypes
import numpy as np
from jax import lax
from jax.experimental import pallas as pl
from jax.experimental.pallas import tpu as pltpu
from jax.sharding import Mesh
from jax.sharding import PartitionSpec as P

SIZE = 4096
DEVICES = 128
GROUP = 16
ROWS = ("x_hi", "z_hi", "z_lo")
COLUMNS = ("x_lo", "y_hi", "y_lo", "core")
NAMES = ROWS + COLUMNS
LINE = ("core", "y_lo", "y_hi", "x_lo")
EVERY = ("z_lo", "z_hi", "y_lo", "y_hi", "x_lo", "x_hi", "core")
MESSAGE = 66
BF16 = jnp.bfloat16
F32 = jnp.float32
HALF = math.sqrt(0.5)


def reorder(value, old, new):
    bits = {name: value >> place & 1 for place, name in enumerate(reversed(old))}
    return sum(bits[name] << place for place, name in enumerate(reversed(new)))


def line_rank(block):
    return reorder(block, COLUMNS, LINE)


def every_rank(block):
    return reorder(block, ROWS + LINE, EVERY)


def roots(rows, cols, length, sign):
    turn = np.outer(np.arange(rows), np.arange(cols)) % length
    return np.exp(sign * 2j * np.pi * turn / length)


def as_block(matrix):
    return np.block([[matrix.real, matrix.imag], [-matrix.imag, matrix.real]])


def two_parts(matrix):
    high = matrix.astype(np.float32).astype(ml_dtypes.bfloat16)
    low = (matrix - high.astype(np.float64)).astype(np.float32).astype(ml_dtypes.bfloat16)
    return high, low


def gains(length):
    turns = np.exp(2j * np.pi * np.arange(length) / length)
    factors = np.exp2(np.arange(4096) / 4096)
    best = []
    for row in range(length):
        entries = turns[row * np.arange(length) % length]
        entries = np.concatenate([entries.real, entries.imag])
        scaled = factors[:, None] * entries
        rounded = scaled.astype(np.float32).astype(ml_dtypes.bfloat16).astype(np.float64)
        best.append(factors[(np.square(rounded - scaled).sum(axis=1) / factors**2).argmin()])
    return np.array(best)


def pair_table(values):
    return np.stack([values.real, values.imag]).astype(np.float32)


@functools.lru_cache(None)
def tables():
    out = {}
    gain = gains(128)
    high, _ = two_parts((np.tile(gain, 2)[:, None] * as_block(roots(128, 128, 128, -1))).T)
    out["cross_fwd"] = high
    high, low = two_parts(as_block(roots(128, 128, 128, 1)) / SIZE)
    out["cross_inv"] = np.concatenate([high, low], axis=0)
    out["cross_tw_fwd"] = pair_table(roots(32, 128, SIZE, -1) / gain)
    out["cross_tw_inv"] = pair_table(roots(32, 128, SIZE, 1))
    gain = np.tile(gains(32), 4)
    out["phase_scale"] = (1.0 / gain).astype(np.float32)[None, :]
    for name, sign, scale in (("fwd", -1, 1.0), ("inv", 1, 1.0 / SIZE)):
        lanes = np.kron(np.eye(4), roots(32, 32, 32, sign))
        high, _ = two_parts(np.tile(gain, 2)[:, None] * as_block(lanes) * scale)
        out["inline_" + name] = high
    out["inline_tw_fwd"] = pair_table(np.tile(roots(128, 32, SIZE, -1), (1, 4)) / gain)
    out["inline_tw_inv"] = pair_table(np.tile(roots(128, 32, SIZE, 1), (1, 4)))
    return out


def add(x, y):
    return (x[0] + y[0], x[1] + y[1])


def sub(x, y):
    return (x[0] - y[0], x[1] - y[1])


def times(x, y):
    return (x[0] * y[0] - x[1] * y[1], x[0] * y[1] + x[1] * y[0])


def turn(x, numerator, length, sign):
    eighth = 8 * (numerator % length) * sign % (8 * length)
    if eighth % length:
        angle = sign * 2.0 * math.pi * (numerator % length) / length
        c, s = math.cos(angle), math.sin(angle)
        return (x[0] * c - x[1] * s, x[0] * s + x[1] * c)
    eighth = eighth // length
    r, i = x
    if eighth == 0:
        return x
    if eighth == 1:
        return ((r - i) * HALF, (r + i) * HALF)
    if eighth == 2:
        return (-i, r)
    if eighth == 3:
        return ((r + i) * -HALF, (r - i) * HALF)
    if eighth == 4:
        return (-r, -i)
    if eighth == 5:
        return ((i - r) * HALF, (r + i) * -HALF)
    if eighth == 6:
        return (i, -r)
    return ((r + i) * HALF, (i - r) * HALF)


def dft(x, sign):
    length = len(x)
    if length == 2:
        return [add(x[0], x[1]), sub(x[0], x[1])]
    if length == 4:
        t0, t1 = add(x[0], x[2]), sub(x[0], x[2])
        t2, t3 = add(x[1], x[3]), sub(x[1], x[3])
        r, i = t3
        if sign < 0:
            return [add(t0, t2), (t1[0] + i, t1[1] - r), sub(t0, t2), (t1[0] - i, t1[1] + r)]
        return [add(t0, t2), (t1[0] - i, t1[1] + r), sub(t0, t2), (t1[0] + i, t1[1] - r)]
    first = {8: 2, 16: 4, 32: 8}[length]
    second = length // first
    inner = [dft(x[low::second], sign) for low in range(second)]
    out = [None] * length
    for q in range(first):
        row = [turn(inner[low][q], low * q, length, sign) for low in range(second)]
        for p, value in enumerate(dft(row, sign)):
            out[q + first * p] = value
    return out


def split(value):
    high = value.astype(BF16)
    return high, (value - high.astype(F32)).astype(BF16)


def dot(x, y, dims=((1,), (0,))):
    return lax.dot_general(x, y, (dims, ((), ())), preferred_element_type=F32)


def dot2(value, matrix):
    high, low = split(value)
    return dot(high, matrix[...]) + dot(low, matrix[...])


def pack_kernel(receiver, source, weight, out, raw, sems):
    copies = [pltpu.make_async_copy(weight, raw, sems.at[8])]
    for which, field in enumerate((receiver, source)):
        for part in range(2):
            for freq in range(2):
                rows = pl.ds(freq * 144 + which * 64 + part * 32, 32)
                sem = sems.at[which * 4 + part * 2 + freq]
                copies.append(
                    pltpu.make_async_copy(field.at[part, freq], out.at[:, rows, :], sem)
                )
    for copy in copies:
        copy.start()
    copies[0].wait()
    for freq in range(2):
        value = raw[:, freq]
        high = value >> 7
        code = 1.0 + (value & 127).astype(F32) * (1.0 / 128.0)
        for power in (1, 2, 4, 8, 16, 32):
            code = code * jnp.where((high & power) != 0, 2.0**power, 1.0)
        out[:, freq * 144 + 128 : freq * 144 + 144, :] = code.astype(BF16)
    for copy in copies[1:]:
        copy.wait()


def prepare_kernel(
    omega, slowness, scale, wedge_map, packed, phase, wedges, share, tiles
):
    place = {name: lax.axis_index(name) for name in NAMES}
    device = 0
    for name in EVERY:
        device = device * 2 + place[name]
    step = 2.0 * math.pi / SIZE

    def signed(index):
        index = jnp.where(index >= SIZE // 2, index - SIZE, index)
        return step * index.astype(F32)

    def body(part, carry):
        row = part * 64 + lax.broadcasted_iota(jnp.int32, (64, 128), 0)
        lane = lax.broadcasted_iota(jnp.int32, (64, 128), 1)
        kx = signed((row >> 6) + 16 * ((row >> 3) & 7) + 128 * (lane & 31))
        ky = signed(device * 32 + (row & 7) + 8 * (lane >> 5))
        kx_sq = kx * kx
        ky_sq = ky * ky
        rows = pl.ds(pl.multiple_of(part * 64, 64), 64)
        for freq in range(2):
            for ref in range(2):
                number = omega[freq] * slowness[ref]
                quad = number * number - kx_sq - ky_sq
                root = jnp.sqrt(jnp.abs(quad))
                decay = jnp.exp(-root)
                inside = jnp.maximum(quad, 0.0)
                even = jnp.full_like(quad, 1.0 / math.factorial(22))
                odd = jnp.full_like(quad, 1.0 / math.factorial(23))
                for n in range(10, -1, -1):
                    even = 1.0 / math.factorial(2 * n) - inside * even
                    odd = 1.0 / math.factorial(2 * n + 1) - inside * odd
                real = jnp.where(quad >= 0, even, decay)
                imag = jnp.where(quad >= 0, odd * root, 0.0)
                phase[freq, ref, 0, rows, :] = real * scale[...]
                phase[freq, ref, 1, rows, :] = imag * scale[...]
        return carry

    lax.fori_loop(0, 16, body, 0)
    tiles[0:128, :] = wedge_map[...].astype(F32)
    rows = [tiles[pl.ds(high, 32, stride=4), :] for high in range(4)]
    rows = jnp.concatenate(rows, axis=0).T
    wedges[pl.ds(0, 128, stride=2), :] = rows
    wedges[pl.ds(1, 128, stride=2), :] = rows
    for half in range(2):
        for a in range(32):
            lanes = slice((a % 2) * 128, (a % 2) * 128 + 128)
            block = packed[line_rank(a // 2), half * 144 + 128 : half * 144 + 144, lanes]
            value = block.astype(F32)
            high = jnp.zeros_like(value)
            for power in (32, 16, 8, 4, 2, 1):
                over = value >= 2.0**power
                value = jnp.where(over, value * 2.0**-power, value)
                high = jnp.where(over, high + float(power), high)
            share[a, half * 16 : half * 16 + 16, :] = (high + (value - 1.0)) * (1.0 / 32.0)


def cross_forward_kernel(lines, twist, table, out, matrix, work, turned, ready, sem, sems):
    fetch = pltpu.make_async_copy(table, matrix, sem)
    fetch.start()

    def send(index):
        rows = pl.ds(pl.multiple_of(index * 16, 16), 16)
        return pltpu.make_async_copy(ready.at[index], out.at[:, rows, :], sems.at[index])

    def field(index, carry):
        start = index // 2 * 144 + index % 2 * 64
        for part in range(2):
            for low in range(4):
                values = []
                for high in range(8):
                    a = 4 * high + low
                    lanes = pl.ds((a % 2) * 128, 128)
                    pair = []
                    for side in range(2):
                        row = pl.multiple_of(start + side * 32 + part * 16, 16)
                        value = lines[line_rank(a // 2), pl.ds(row, 16), lanes]
                        pair.append(value.astype(F32))
                    values.append(tuple(pair))
                for q, value in enumerate(dft(values, -1)):
                    r, i = turn(value, low * q, 32, -1)
                    work[q, low, 0, part * 16 : part * 16 + 16, :] = r
                    work[q, low, 1, part * 16 : part * 16 + 16, :] = i

        @pl.when(index == 0)
        def _():
            fetch.wait()

        for pair in range(4):
            real, imag = [], []
            for q in (2 * pair, 2 * pair + 1):
                values = dft([(work[q, low, 0], work[q, low, 1]) for low in range(4)], -1)
                for p, value in enumerate(values):
                    k = q + 8 * p
                    r, i = times(value, (twist[0, k : k + 1, :], twist[1, k : k + 1, :]))
                    real.append(r)
                    imag.append(i)
            both = [jnp.concatenate(real, axis=0), jnp.concatenate(imag, axis=0)]
            high, low = split(jnp.concatenate(both, axis=1))
            value = dot(matrix[...], high, ((1,), (1,))) + dot(matrix[...], low, ((1,), (1,)))
            for side in range(2):
                for half in range(2):
                    turned[pl.ds(side * 8 + pair * 2 + half, 128, stride=24), :] = value[
                        side * 128 : side * 128 + 128, half * 128 : half * 128 + 128
                    ]
        ready[index] = turned[0:3072, :].reshape(128, 24, 128)[:, :16].astype(BF16)
        send(index).start()
        return carry

    lax.fori_loop(0, 4, field, 0, unroll=True)
    for index in range(4):
        send(index).wait()


def inline_kernel(
    lines,
    phase,
    twist,
    twist_inv,
    table,
    table_inv,
    out,
    held,
    matrix,
    matrix_inv,
    shifts,
    work,
    spec,
    term,
    sums,
    sems,
):
    fetch = pltpu.make_async_copy(table, matrix, sems.at[2])
    fetch_inv = pltpu.make_async_copy(table_inv, matrix_inv, sems.at[3])

    def fetch_phase(freq):
        return pltpu.make_async_copy(phase.at[freq], shifts.at[freq], sems.at[freq])

    def fetch_lines(index):
        rows = pl.ds(index * 16, 16)
        return pltpu.make_async_copy(lines.at[:, rows, :], held.at[index], sems.at[4 + index])

    order = [fetch_lines(0), fetch, fetch_lines(1), fetch_phase(0), fetch_inv]
    for copy in order + [fetch_lines(2), fetch_lines(3), fetch_phase(1)]:
        copy.start()
    term[...] = jnp.zeros_like(term)

    def one_freq(freq):
        def forward(which):
            index = freq * 2 + which
            fetch_lines(index).wait()
            for low in range(8):
                values = []
                for high in range(16):
                    value = held[index, every_rank(8 * high + low)].astype(F32)
                    values.append((value[0:8], value[8:16]))
                for q, value in enumerate(dft(values, -1)):
                    r, i = turn(value, low * q, 128, -1)
                    work[q * 8 + low, 0] = r
                    work[q * 8 + low, 1] = i

            if index == 0:
                fetch.wait()
            for part in range(4):
                real, imag = [], []
                for q in range(4 * part, 4 * part + 4):
                    values = [(work[q * 8 + low, 0], work[q * 8 + low, 1]) for low in range(8)]
                    for p, value in enumerate(dft(values, -1)):
                        k = q + 16 * p
                        r, i = times(value, (twist[0, k : k + 1, :], twist[1, k : k + 1, :]))
                        real.append(r)
                        imag.append(i)
                both = [jnp.concatenate(real, axis=0), jnp.concatenate(imag, axis=0)]
                block = slice(part * 256, part * 256 + 256)
                spec[which, block, :] = dot2(jnp.concatenate(both, axis=1), matrix)

        for which in range(2):
            forward(which)
        for part in range(4):
            block = slice(part * 256, part * 256 + 256)
            both = spec[0, block, :] * spec[1, block, :]
            term[block, :] += both[:, 0:128] + both[:, 128:256]

        fetch_phase(freq).wait()

        if freq == 0:
            fetch_inv.wait()

        def inverse(ref):
            for part in range(4):
                block = slice(part * 256, part * 256 + 256)
                value = (spec[0, block, 0:128], spec[0, block, 128:256])
                shift = (shifts[freq, ref, 0, block, :], shifts[freq, ref, 1, block, :])
                turned = jnp.concatenate(times(value, shift), axis=1)
                turned = dot2(turned, matrix_inv)
                for j in range(4):
                    q = 4 * part + j
                    values = []
                    for p in range(8):
                        k = q + 16 * p
                        row = 64 * j + 8 * p
                        value = (turned[row : row + 8, 0:128], turned[row : row + 8, 128:256])
                        values.append(
                            times(value, (twist_inv[0, k : k + 1, :], twist_inv[1, k : k + 1, :]))
                        )
                    for low, value in enumerate(dft(values, 1)):
                        r, i = turn(value, low * q, 128, 1)
                        work[low * 16 + q, 0] = r
                        work[low * 16 + q, 1] = i
            for low in range(8):
                values = [(work[low * 16 + q, 0], work[low * 16 + q, 1]) for q in range(16)]
                for high, value in enumerate(dft(values, 1)):
                    value = jnp.concatenate(value, axis=0).astype(BF16)
                    start = every_rank(8 * high + low) * MESSAGE + freq * 32 + ref * 16
                    out[start : start + 16, :] = value

        for ref in range(2):
            inverse(ref)

    for freq in range(2):
        one_freq(freq)
    total = term[...].reshape(128, 8, 128).sum(axis=1)
    for q in range(16):
        sums[pl.ds(q, 8, stride=16), :] = total[8 * q : 8 * q + 8, :]
    total = sums[0:128, :]
    total = total + pltpu.roll(total, 64, 1)
    total = total + pltpu.roll(total, 32, 1)
    place = lax.broadcasted_iota(jnp.int32, (32, 128), 1) >> 5
    value = total[0:32, :]
    for u in range(1, 4):
        value = jnp.where(place == u, total[32 * u : 32 * u + 32, :], value)
    for v in range(2):
        sums[pl.ds(v, 16, stride=2), :] = value[16 * v : 16 * v + 16, :]
    value = sums[0:32, :].astype(BF16)
    for block in range(DEVICES):
        start = every_rank(block) * MESSAGE + 64
        line = block % GROUP
        out[start : start + 2, :] = value[2 * line : 2 * line + 2, :]


def cross_inverse_kernel(
    lines, wedges, shares, twist, table, out, matrix, flat, work, kept, share, sems
):
    fetch = pltpu.make_async_copy(table, matrix, sems.at[0])
    fetch.start()
    fetch_share = pltpu.make_async_copy(shares, share, sems.at[1])
    fetch_share.start()
    for d in range(DEVICES):
        flat[2 * d : 2 * d + 2, :] = lines[d * MESSAGE + 64 : d * MESSAGE + 66, :].astype(F32)

    def gather(step, totals):
        rows = pl.ds(pl.multiple_of(step * 8, 8), 8)
        value, where = flat[rows, :], wedges[rows, :]
        return tuple(
            total + jnp.where(where == float(w), value, 0.0) for w, total in enumerate(totals)
        )

    zero = jnp.zeros((8, 128), F32)
    totals = lax.fori_loop(0, 32, gather, (zero,) * 8, unroll=8)
    totals = [t[0:2] + t[2:4] + (t[4:6] + t[6:8]) for t in totals]
    for half in range(2):
        value = jnp.concatenate(totals[4 * half : 4 * half + 4], axis=0)
        value = (value * (1.0 / (SIZE * SIZE * math.sqrt(SIZE)))).astype(BF16)
        for group in range(16):
            out[group, 128:136, half * 128 : half * 128 + 128] = value

    fetch.wait()

    def one_freq(freq):
        for ref in range(2):
            if freq == 0 and ref == 1:
                fetch_share.wait()

            for d in range(128):
                rows = pl.ds(d * MESSAGE + freq * 32 + ref * 16, 16)
                flat[24 * d : 24 * d + 16, :] = lines[rows, :].astype(F32)
            for g in range(8):
                pair = [flat[pl.ds(side * 8 + g, 128, stride=24), :] for side in range(2)]
                value = jnp.concatenate([x.T for x in pair], axis=1).astype(BF16)
                value = dot(jnp.concatenate([value, value], axis=1), matrix[...])
                values = []
                for p in range(4):
                    k = g + 8 * p
                    block = value[32 * p : 32 * p + 32, :]
                    block = (block[:, 0:128], block[:, 128:256])
                    values.append(times(block, (twist[0, k : k + 1, :], twist[1, k : k + 1, :])))
                for low, value in enumerate(dft(values, 1)):
                    r, i = turn(value, low * g, 32, 1)
                    work[low, g, 0] = r
                    work[low, g, 1] = i

            def rows16(part, carry):
                start = pl.multiple_of(part * 16, 16)
                rows = pl.ds(start, 16)
                for low in range(4):
                    values = [(work[low, g, 0, rows, :], work[low, g, 1, rows, :]) for g in range(8)]
                    for high, value in enumerate(dft(values, 1)):
                        a = 4 * high + low
                        lanes = slice((a % 2) * 128, (a % 2) * 128 + 128)
                        for side in range(2):
                            rounded = value[side].astype(BF16)
                            if ref == 0:
                                kept[a, side, rows, :] = rounded
                            else:
                                s = share[a, rows, :]
                                first = kept[a, side, rows, :].astype(F32)
                                mixed = first * s + rounded.astype(F32) * (1.0 - s)
                                row = pl.multiple_of(freq * 64 + side * 32 + part * 16, 16)
                                out[line_rank(a // 2), pl.ds(row, 16), lanes] = mixed.astype(BF16)
                return carry

            lax.fori_loop(0, 2, rows16, 0, unroll=True)

    for freq in range(2):
        one_freq(freq)


def unpack_kernel(home, out, angles, coded, turned, wide, sems):
    copies = []
    for part in range(4):
        block = home.at[:, pl.ds(part * 32, 32), :]
        copies.append(pltpu.make_async_copy(block, out.at[part % 2, part // 2], sems.at[part]))
    for copy in copies:
        copy.start()
    place = lax.broadcasted_iota(jnp.int32, (32, 128), 1) >> 5
    for half in range(2):
        rows = home[:, 128:136, half * 128 : half * 128 + 128].astype(F32)
        coded[0:128, :] = rows.reshape(128, 128)
        rows = [coded[pl.ds(r, 16, stride=8), :] for r in range(8)]
        flipped = jnp.concatenate(rows, axis=0).T
        for w in range(4):
            value = pltpu.roll(flipped[0:32], (4 - w) * 32 % 128, 1)
            for u in range(1, 4):
                part = pltpu.roll(flipped[32 * u : 32 * u + 32], (4 + u - w) * 32 % 128, 1)
                value = jnp.where(place == u, part, value)
            turned[pl.ds(half * 4 + w, 32, stride=8), :] = value
    for k in range(32):
        wide[:, k * 128 : k * 128 + 128] = turned[k * 8 : k * 8 + 8, :]
    copies.append(pltpu.make_async_copy(wide, angles, sems.at[4]))
    copies[4].start()
    for copy in copies:
        copy.wait()


FAR = pl.BlockSpec(memory_space=pltpu.HBM)
LOCAL = pl.BlockSpec(memory_space=pltpu.VMEM)
SCALAR = pl.BlockSpec(memory_space=pltpu.SMEM)


def near(value):
    return pltpu.with_memory_space_constraint(value, pltpu.VMEM)


def far(value):
    return pltpu.with_memory_space_constraint(value, pltpu.HBM)


def call(kernel, name, outs, out_specs, in_specs, scratch, mebibytes, args):
    return pl.pallas_call(
        kernel,
        in_specs=in_specs,
        out_specs=out_specs,
        out_shape=outs,
        scratch_shapes=scratch,
        compiler_params=pltpu.CompilerParams(vmem_limit_bytes=mebibytes * 2**20),
        name=name,
    )(*args)


def pack(receiver, source, weight):
    args = (
        far(receiver.reshape(2, 2, GROUP, 32, 256)),
        far(source.reshape(2, 2, GROUP, 32, 256)),
        far(weight.reshape(GROUP, 2, 16, 256)),
    )
    scratch = [pltpu.VMEM((GROUP, 2, 16, 256), jnp.int32), pltpu.SemaphoreType.DMA((9,))]
    outs = pltpu.VMEM((GROUP, 288, 256), BF16)
    return call(pack_kernel, "pack_fields", outs, LOCAL, [FAR] * 3, scratch, 12, args)


def prepare(omega, slowness, wedge_map, packed):
    outs = [
        pltpu.HBM((2, 2, 2, 1024, 128), F32),
        pltpu.VMEM((264, 128), F32),
        pltpu.HBM((32, 32, 128), F32),
    ]
    scale = jnp.asarray(tables()["phase_scale"])
    args = (omega, slowness, scale, wedge_map, near(packed))
    specs = [SCALAR] * 2 + [LOCAL] * 3
    scratch = [pltpu.VMEM((136, 128), F32)]
    return call(prepare_kernel, "prepare", outs, [LOCAL] * 3, specs, scratch, 16, args)


def cross_forward(packed):
    t = tables()
    args = [near(packed), near(jnp.asarray(t["cross_tw_fwd"])), jnp.asarray(t["cross_fwd"])]
    outs = pltpu.HBM((DEVICES, 64, 128), BF16)
    scratch = [
        pltpu.VMEM((256, 256), BF16),
        pltpu.VMEM((8, 4, 2, 32, 128), F32),
        pltpu.VMEM((3096, 128), F32),
        pltpu.VMEM((4, DEVICES, 16, 128), BF16),
        pltpu.SemaphoreType.DMA,
        pltpu.SemaphoreType.DMA((4,)),
    ]
    return call(
        cross_forward_kernel, "crossline_forward", outs, FAR, [LOCAL] * 2 + [FAR], scratch, 16, args
    )


def inline_step(lines, phase):
    t = tables()
    args = [far(lines), far(phase)]
    args += [near(jnp.asarray(t[n])) for n in ("inline_tw_fwd", "inline_tw_inv")]
    args += [jnp.asarray(t[n]) for n in ("inline_fwd", "inline_inv")]
    outs = pltpu.VMEM((DEVICES * MESSAGE, 128), BF16)
    scratch = [
        pltpu.VMEM((4, DEVICES, 16, 128), BF16),
        pltpu.VMEM((256, 256), BF16),
        pltpu.VMEM((256, 256), BF16),
        pltpu.VMEM((2, 2, 2, 1024, 128), F32),
        pltpu.VMEM((128, 2, 8, 128), F32),
        pltpu.VMEM((2, 1024, 256), F32),
        pltpu.VMEM((1024, 128), F32),
        pltpu.VMEM((144, 128), F32),
        pltpu.SemaphoreType.DMA((8,)),
    ]
    specs = [FAR, FAR, LOCAL, LOCAL, FAR, FAR]
    return call(inline_kernel, "inline_step", outs, LOCAL, specs, scratch, 20, args)


def cross_inverse(partial, wedges, share):
    t = tables()
    args = [near(partial), near(wedges), far(share), near(jnp.asarray(t["cross_tw_inv"]))]
    args.append(jnp.asarray(t["cross_inv"]))
    outs = pltpu.VMEM((GROUP, 136, 256), BF16)
    scratch = [
        pltpu.VMEM((512, 256), BF16),
        pltpu.VMEM((3096, 128), F32),
        pltpu.VMEM((4, 8, 2, 32, 128), F32),
        pltpu.VMEM((32, 2, 32, 128), BF16),
        pltpu.VMEM((32, 32, 128), F32),
        pltpu.SemaphoreType.DMA((2,)),
    ]
    return call(
        cross_inverse_kernel, "crossline_inverse", outs, LOCAL, [LOCAL, LOCAL, FAR, LOCAL, FAR], scratch, 16, args
    )


def unpack(home):
    outs = [
        pltpu.HBM((2, 2, GROUP, 32, 256), BF16),
        pltpu.HBM((8, SIZE), F32),
    ]
    scratch = [
        pltpu.VMEM((136, 128), F32),
        pltpu.VMEM((264, 128), F32),
        pltpu.VMEM((8, SIZE), F32),
        pltpu.SemaphoreType.DMA((5,)),
    ]
    specs = [FAR, FAR]
    return call(unpack_kernel, "unpack_fields", outs, specs, [LOCAL], scratch, 12, [near(home)])


def exchange(value, axes):
    return lax.all_to_all(value, axes, 0, 0, tiled=True)


def per_device(receiver, source, weight, omega, slowness, wedge_map):
    packed = exchange(pack(receiver, source, weight), LINE)
    phase, wedges, share = prepare(omega, slowness, wedge_map, packed)
    lines = exchange(cross_forward(packed), EVERY)
    partial = inline_step(lines, phase).reshape(DEVICES, MESSAGE // 2, 2, 128)
    partial = exchange(partial, EVERY).reshape(DEVICES * MESSAGE, 128)
    home = exchange(cross_inverse(partial, wedges, share), LINE)
    mixed, angles = unpack(home)
    return (mixed.reshape(2, 2, 512, 256), angles)


def solution(mesh):
    fine = Mesh(mesh.devices.reshape((2,) * 7), NAMES)
    return jax.shard_map(
        per_device,
        mesh=fine,
        in_specs=(
            P(None, None, ROWS, COLUMNS),
            P(None, None, ROWS, COLUMNS),
            P(ROWS, COLUMNS),
            P(),
            P(),
            P(),
        ),
        out_specs=(P(None, None, ROWS, COLUMNS), P()),
        check_vma=False,
    )
```

```python
import functools
import math

import jax
import jax.numpy as jnp
import ml_dtypes
import numpy as np
from jax import lax
from jax.experimental import pallas as pl
from jax.experimental.pallas import tpu as pltpu
from jax.sharding import Mesh
from jax.sharding import PartitionSpec as P

SIZE = 4096
DEVICES = 128
GROUP = 16
ROWS = ("x_hi", "z_hi", "z_lo")
COLUMNS = ("x_lo", "y_hi", "y_lo", "core")
NAMES = ROWS + COLUMNS
LINE = ("core", "y_lo", "y_hi", "x_lo")
EVERY = ("z_lo", "z_hi", "y_lo", "y_hi", "x_lo", "x_hi", "core")
MESSAGE = 66
BF16 = jnp.bfloat16
F32 = jnp.float32
HALF = math.sqrt(0.5)


def reorder(value, old, new):
    bits = {name: value >> place & 1 for place, name in enumerate(reversed(old))}
    return sum(bits[name] << place for place, name in enumerate(reversed(new)))


def line_rank(block):
    return reorder(block, COLUMNS, LINE)


def every_rank(block):
    return reorder(block, ROWS + LINE, EVERY)


def roots(rows, cols, length, sign):
    turn = np.outer(np.arange(rows), np.arange(cols)) % length
    return np.exp(sign * 2j * np.pi * turn / length)


def as_block(matrix):
    return np.block([[matrix.real, matrix.imag], [-matrix.imag, matrix.real]])


def two_parts(matrix):
    high = matrix.astype(np.float32).astype(ml_dtypes.bfloat16)
    low = (matrix - high.astype(np.float64)).astype(np.float32).astype(ml_dtypes.bfloat16)
    return high, low


def gains(length):
    turns = np.exp(2j * np.pi * np.arange(length) / length)
    factors = np.exp2(np.arange(4096) / 4096)
    best = []
    for row in range(length):
        entries = turns[row * np.arange(length) % length]
        entries = np.concatenate([entries.real, entries.imag])
        scaled = factors[:, None] * entries
        rounded = scaled.astype(np.float32).astype(ml_dtypes.bfloat16).astype(np.float64)
        best.append(factors[(np.square(rounded - scaled).sum(axis=1) / factors**2).argmin()])
    return np.array(best)


def pair_table(values):
    return np.stack([values.real, values.imag]).astype(np.float32)


@functools.lru_cache(None)
def tables():
    out = {}
    high, low = two_parts(as_block(roots(128, 128, 128, -1)).T)
    out["cross_fwd"] = np.concatenate([high, high, low], axis=1)
    high, low = two_parts(as_block(roots(128, 128, 128, 1)) / SIZE)
    out["cross_inv"] = np.concatenate([high, low], axis=0)
    out["cross_tw_fwd"] = pair_table(roots(32, 128, SIZE, -1))
    out["cross_tw_inv"] = pair_table(roots(32, 128, SIZE, 1))
    gain = np.tile(gains(32), 4)
    out["phase_scale"] = (1.0 / gain).astype(np.float32)[None, :]
    for name, sign, scale in (("fwd", -1, 1.0), ("inv", 1, 1.0 / SIZE)):
        lanes = np.kron(np.eye(4), roots(32, 32, 32, sign))
        high, _ = two_parts(np.tile(gain, 2)[:, None] * as_block(lanes) * scale)
        out["inline_" + name] = high
    out["inline_tw_fwd"] = pair_table(np.tile(roots(128, 32, SIZE, -1), (1, 4)) / gain)
    out["inline_tw_inv"] = pair_table(np.tile(roots(128, 32, SIZE, 1), (1, 4)))
    return out


def add(x, y):
    return (x[0] + y[0], x[1] + y[1])


def sub(x, y):
    return (x[0] - y[0], x[1] - y[1])


def times(x, y):
    return (x[0] * y[0] - x[1] * y[1], x[0] * y[1] + x[1] * y[0])


def turn(x, numerator, length, sign):
    eighth = 8 * (numerator % length) * sign % (8 * length)
    if eighth % length:
        angle = sign * 2.0 * math.pi * (numerator % length) / length
        c, s = math.cos(angle), math.sin(angle)
        return (x[0] * c - x[1] * s, x[0] * s + x[1] * c)
    eighth = eighth // length
    r, i = x
    if eighth == 0:
        return x
    if eighth == 1:
        return ((r - i) * HALF, (r + i) * HALF)
    if eighth == 2:
        return (-i, r)
    if eighth == 3:
        return ((r + i) * -HALF, (r - i) * HALF)
    if eighth == 4:
        return (-r, -i)
    if eighth == 5:
        return ((i - r) * HALF, (r + i) * -HALF)
    if eighth == 6:
        return (i, -r)
    return ((r + i) * HALF, (i - r) * HALF)


def dft(x, sign):
    length = len(x)
    if length == 2:
        return [add(x[0], x[1]), sub(x[0], x[1])]
    if length == 4:
        t0, t1 = add(x[0], x[2]), sub(x[0], x[2])
        t2, t3 = add(x[1], x[3]), sub(x[1], x[3])
        r, i = t3
        if sign < 0:
            return [add(t0, t2), (t1[0] + i, t1[1] - r), sub(t0, t2), (t1[0] - i, t1[1] + r)]
        return [add(t0, t2), (t1[0] - i, t1[1] + r), sub(t0, t2), (t1[0] + i, t1[1] - r)]
    first = {8: 2, 16: 4, 32: 8}[length]
    second = length // first
    inner = [dft(x[low::second], sign) for low in range(second)]
    out = [None] * length
    for q in range(first):
        row = [turn(inner[low][q], low * q, length, sign) for low in range(second)]
        for p, value in enumerate(dft(row, sign)):
            out[q + first * p] = value
    return out


def split(value):
    high = value.astype(BF16)
    return high, (value - high.astype(F32)).astype(BF16)


def dot(x, y, dims=((1,), (0,))):
    return lax.dot_general(x, y, (dims, ((), ())), preferred_element_type=F32)


def dot2(value, matrix):
    high, low = split(value)
    return dot(high, matrix[...]) + dot(low, matrix[...])


def pack_kernel(receiver, source, weight, out, raw, sems):
    copies = [pltpu.make_async_copy(weight, raw, sems.at[8])]
    for which, field in enumerate((receiver, source)):
        for part in range(2):
            for freq in range(2):
                rows = pl.ds(freq * 144 + which * 64 + part * 32, 32)
                sem = sems.at[which * 4 + part * 2 + freq]
                copies.append(
                    pltpu.make_async_copy(field.at[part, freq], out.at[:, rows, :], sem)
                )
    for copy in copies:
        copy.start()
    copies[0].wait()
    for freq in range(2):
        value = raw[:, freq]
        high = value >> 7
        code = 1.0 + (value & 127).astype(F32) * (1.0 / 128.0)
        for power in (1, 2, 4, 8, 16, 32):
            code = code * jnp.where((high & power) != 0, 2.0**power, 1.0)
        out[:, freq * 144 + 128 : freq * 144 + 144, :] = code.astype(BF16)
    for copy in copies[1:]:
        copy.wait()


def prepare_kernel(
    omega, slowness, scale, wedge_map, packed, phase, wedges, share, tiles
):
    place = {name: lax.axis_index(name) for name in NAMES}
    device = 0
    for name in EVERY:
        device = device * 2 + place[name]
    step = 2.0 * math.pi / SIZE

    def signed(index):
        index = jnp.where(index >= SIZE // 2, index - SIZE, index)
        return step * index.astype(F32)

    def body(part, carry):
        row = part * 64 + lax.broadcasted_iota(jnp.int32, (64, 128), 0)
        lane = lax.broadcasted_iota(jnp.int32, (64, 128), 1)
        kx = signed((row >> 6) + 16 * ((row >> 3) & 7) + 128 * (lane & 31))
        ky = signed(device * 32 + (row & 7) + 8 * (lane >> 5))
        kx_sq = kx * kx
        ky_sq = ky * ky
        rows = pl.ds(pl.multiple_of(part * 64, 64), 64)
        for freq in range(2):
            for ref in range(2):
                number = omega[freq] * slowness[ref]
                quad = number * number - kx_sq - ky_sq
                root = jnp.sqrt(jnp.abs(quad))
                decay = jnp.exp(-root)
                inside = jnp.maximum(quad, 0.0)
                even = jnp.full_like(quad, 1.0 / math.factorial(22))
                odd = jnp.full_like(quad, 1.0 / math.factorial(23))
                for n in range(10, -1, -1):
                    even = 1.0 / math.factorial(2 * n) - inside * even
                    odd = 1.0 / math.factorial(2 * n + 1) - inside * odd
                real = jnp.where(quad >= 0, even, decay)
                imag = jnp.where(quad >= 0, odd * root, 0.0)
                phase[freq, ref, 0, rows, :] = real * scale[...]
                phase[freq, ref, 1, rows, :] = imag * scale[...]
        return carry

    lax.fori_loop(0, 16, body, 0)
    tiles[0:128, :] = wedge_map[...].astype(F32)
    rows = [tiles[pl.ds(high, 32, stride=4), :] for high in range(4)]
    rows = jnp.concatenate(rows, axis=0).T
    wedges[pl.ds(0, 128, stride=2), :] = rows
    wedges[pl.ds(1, 128, stride=2), :] = rows
    for half in range(2):
        for a in range(32):
            lanes = slice((a % 2) * 128, (a % 2) * 128 + 128)
            block = packed[line_rank(a // 2), half * 144 + 128 : half * 144 + 144, lanes]
            value = block.astype(F32)
            high = jnp.zeros_like(value)
            for power in (32, 16, 8, 4, 2, 1):
                over = value >= 2.0**power
                value = jnp.where(over, value * 2.0**-power, value)
                high = jnp.where(over, high + float(power), high)
            share[a, half * 16 : half * 16 + 16, :] = (high + (value - 1.0)) * (1.0 / 32.0)


def cross_forward_kernel(lines, twist, table, out, matrix, work, turned, ready, sem, sems):
    fetch = pltpu.make_async_copy(table, matrix, sem)
    fetch.start()

    def send(index, half):
        rows = pl.ds(pl.multiple_of(index * 16, 16), 16)
        part = pl.ds(64 * half, 64)
        return pltpu.make_async_copy(ready.at[index, part], out.at[part, rows, :], sems.at[index, half])

    def field(index, carry):
        start = index // 2 * 144 + index % 2 * 64
        for part in range(2):
            for low in range(4):
                values = []
                for high in range(8):
                    a = 4 * high + low
                    lanes = pl.ds((a % 2) * 128, 128)
                    pair = []
                    for side in range(2):
                        row = pl.multiple_of(start + side * 32 + part * 16, 16)
                        value = lines[line_rank(a // 2), pl.ds(row, 16), lanes]
                        pair.append(value.astype(F32))
                    values.append(tuple(pair))
                for q, value in enumerate(dft(values, -1)):
                    r, i = turn(value, low * q, 32, -1)
                    work[q, low, 0, part * 16 : part * 16 + 16, :] = r
                    work[q, low, 1, part * 16 : part * 16 + 16, :] = i

        @pl.when(index == 0)
        def _():
            fetch.wait()

        for pair in range(4):
            real, imag = [], []
            for q in (2 * pair, 2 * pair + 1):
                values = dft([(work[q, low, 0], work[q, low, 1]) for low in range(4)], -1)
                for p, value in enumerate(values):
                    k = q + 8 * p
                    r, i = times(value, (twist[0, k : k + 1, :], twist[1, k : k + 1, :]))
                    real.append(r)
                    imag.append(i)
            both = [jnp.concatenate(real, axis=0), jnp.concatenate(imag, axis=0)]
            high, low = split(jnp.concatenate(both, axis=1))
            parts = jnp.concatenate([high, low, high], axis=1)
            value = dot(matrix[...], parts, ((1,), (1,)))
            for side in range(2):
                for half in range(2):
                    turned[pl.ds(side * 8 + pair * 2 + half, 128, stride=24), :] = value[
                        side * 128 : side * 128 + 128, half * 128 : half * 128 + 128
                    ]
        for half in range(2):
            block = turned[1536 * half : 1536 * half + 1536, :].reshape(64, 24, 128)[:, :16]
            ready[index, 64 * half : 64 * half + 64] = block.astype(BF16)
            send(index, half).start()
        return carry

    lax.fori_loop(0, 4, field, 0, unroll=True)
    for index in range(4):
        send(index, 0).wait()
        send(index, 1).wait()


def inline_kernel(
    lines,
    phase,
    twist,
    twist_inv,
    table,
    table_inv,
    out,
    held,
    matrix,
    matrix_inv,
    shifts,
    work,
    spec,
    term,
    sums,
    sems,
):
    fetch = pltpu.make_async_copy(table, matrix, sems.at[2])
    fetch_inv = pltpu.make_async_copy(table_inv, matrix_inv, sems.at[3])

    def fetch_phase(freq):
        return pltpu.make_async_copy(phase.at[freq], shifts.at[freq], sems.at[freq])

    def fetch_lines(index):
        rows = pl.ds(index * 16, 16)
        return pltpu.make_async_copy(lines.at[:, rows, :], held.at[index], sems.at[4 + index])

    order = [fetch_lines(0), fetch, fetch_lines(1), fetch_phase(0), fetch_inv]
    for copy in order + [fetch_lines(2), fetch_lines(3), fetch_phase(1)]:
        copy.start()
    term[...] = jnp.zeros_like(term)

    def one_freq(freq):
        def forward(which):
            index = freq * 2 + which
            fetch_lines(index).wait()
            for low in range(8):
                values = []
                for high in range(16):
                    value = held[index, every_rank(8 * high + low)].astype(F32)
                    values.append((value[0:8], value[8:16]))
                for q, value in enumerate(dft(values, -1)):
                    r, i = turn(value, low * q, 128, -1)
                    work[q * 8 + low, 0] = r
                    work[q * 8 + low, 1] = i

            if index == 0:
                fetch.wait()
            for part in range(4):
                real, imag = [], []
                for q in range(4 * part, 4 * part + 4):
                    values = [(work[q * 8 + low, 0], work[q * 8 + low, 1]) for low in range(8)]
                    for p, value in enumerate(dft(values, -1)):
                        k = q + 16 * p
                        r, i = times(value, (twist[0, k : k + 1, :], twist[1, k : k + 1, :]))
                        real.append(r)
                        imag.append(i)
                both = [jnp.concatenate(real, axis=0), jnp.concatenate(imag, axis=0)]
                block = slice(part * 256, part * 256 + 256)
                spec[which, block, :] = dot2(jnp.concatenate(both, axis=1), matrix)

        for which in range(2):
            forward(which)
        for part in range(4):
            block = slice(part * 256, part * 256 + 256)
            both = spec[0, block, :] * spec[1, block, :]
            term[block, :] += both[:, 0:128] + both[:, 128:256]

        fetch_phase(freq).wait()

        if freq == 0:
            fetch_inv.wait()

        def inverse(ref):
            for part in range(4):
                block = slice(part * 256, part * 256 + 256)
                value = (spec[0, block, 0:128], spec[0, block, 128:256])
                shift = (shifts[freq, ref, 0, block, :], shifts[freq, ref, 1, block, :])
                turned = jnp.concatenate(times(value, shift), axis=1)
                turned = dot2(turned, matrix_inv)
                for j in range(4):
                    q = 4 * part + j
                    values = []
                    for p in range(8):
                        k = q + 16 * p
                        row = 64 * j + 8 * p
                        value = (turned[row : row + 8, 0:128], turned[row : row + 8, 128:256])
                        values.append(
                            times(value, (twist_inv[0, k : k + 1, :], twist_inv[1, k : k + 1, :]))
                        )
                    for low, value in enumerate(dft(values, 1)):
                        r, i = turn(value, low * q, 128, 1)
                        work[low * 16 + q, 0] = r
                        work[low * 16 + q, 1] = i
            for low in range(8):
                values = [(work[low * 16 + q, 0], work[low * 16 + q, 1]) for q in range(16)]
                for high, value in enumerate(dft(values, 1)):
                    value = jnp.concatenate(value, axis=0).astype(BF16)
                    start = every_rank(8 * high + low) * MESSAGE + freq * 32 + ref * 16
                    out[start : start + 16, :] = value

        for ref in range(2):
            inverse(ref)

    for freq in range(2):
        one_freq(freq)
    total = term[...].reshape(128, 8, 128).sum(axis=1)
    for q in range(16):
        sums[pl.ds(q, 8, stride=16), :] = total[8 * q : 8 * q + 8, :]
    total = sums[0:128, :]
    total = total + pltpu.roll(total, 64, 1)
    total = total + pltpu.roll(total, 32, 1)
    place = lax.broadcasted_iota(jnp.int32, (32, 128), 1) >> 5
    value = total[0:32, :]
    for u in range(1, 4):
        value = jnp.where(place == u, total[32 * u : 32 * u + 32, :], value)
    for v in range(2):
        sums[pl.ds(v, 16, stride=2), :] = value[16 * v : 16 * v + 16, :]
    value = sums[0:32, :].astype(BF16)
    for block in range(DEVICES):
        start = every_rank(block) * MESSAGE + 64
        line = block % GROUP
        out[start : start + 2, :] = value[2 * line : 2 * line + 2, :]


def cross_inverse_kernel(
    lines, wedges, shares, twist, table, out, matrix, flat, work, kept, share, sems
):
    fetch = pltpu.make_async_copy(table, matrix, sems.at[0])
    fetch.start()
    fetch_share = pltpu.make_async_copy(shares, share, sems.at[1])
    fetch_share.start()
    for d in range(DEVICES):
        flat[2 * d : 2 * d + 2, :] = lines[d * MESSAGE + 64 : d * MESSAGE + 66, :].astype(F32)

    def gather(step, totals):
        rows = pl.ds(pl.multiple_of(step * 8, 8), 8)
        value, where = flat[rows, :], wedges[rows, :]
        return tuple(
            total + jnp.where(where == float(w), value, 0.0) for w, total in enumerate(totals)
        )

    zero = jnp.zeros((8, 128), F32)
    totals = lax.fori_loop(0, 32, gather, (zero,) * 8, unroll=8)
    totals = [t[0:2] + t[2:4] + (t[4:6] + t[6:8]) for t in totals]
    for half in range(2):
        value = jnp.concatenate(totals[4 * half : 4 * half + 4], axis=0)
        value = (value * (1.0 / (SIZE * SIZE * math.sqrt(SIZE)))).astype(BF16)
        for group in range(16):
            out[group, 128:136, half * 128 : half * 128 + 128] = value

    fetch.wait()

    def one_freq(freq):
        for ref in range(2):
            if freq == 0 and ref == 1:
                fetch_share.wait()

            for d in range(128):
                rows = pl.ds(d * MESSAGE + freq * 32 + ref * 16, 16)
                flat[24 * d : 24 * d + 16, :] = lines[rows, :].astype(F32)
            for g in range(8):
                pair = [flat[pl.ds(side * 8 + g, 128, stride=24), :] for side in range(2)]
                value = jnp.concatenate([x.T for x in pair], axis=1).astype(BF16)
                value = dot(jnp.concatenate([value, value], axis=1), matrix[...])
                values = []
                for p in range(4):
                    k = g + 8 * p
                    block = value[32 * p : 32 * p + 32, :]
                    block = (block[:, 0:128], block[:, 128:256])
                    values.append(times(block, (twist[0, k : k + 1, :], twist[1, k : k + 1, :])))
                for low, value in enumerate(dft(values, 1)):
                    r, i = turn(value, low * g, 32, 1)
                    work[low, g, 0] = r
                    work[low, g, 1] = i

            def rows16(part, carry):
                start = pl.multiple_of(part * 16, 16)
                rows = pl.ds(start, 16)
                for low in range(4):
                    values = [(work[low, g, 0, rows, :], work[low, g, 1, rows, :]) for g in range(8)]
                    for high, value in enumerate(dft(values, 1)):
                        a = 4 * high + low
                        lanes = slice((a % 2) * 128, (a % 2) * 128 + 128)
                        for side in range(2):
                            rounded = value[side].astype(BF16)
                            if ref == 0:
                                kept[a, side, rows, :] = rounded
                            else:
                                s = share[a, rows, :]
                                first = kept[a, side, rows, :].astype(F32)
                                mixed = first * s + rounded.astype(F32) * (1.0 - s)
                                row = pl.multiple_of(freq * 64 + side * 32 + part * 16, 16)
                                out[line_rank(a // 2), pl.ds(row, 16), lanes] = mixed.astype(BF16)
                return carry

            lax.fori_loop(0, 2, rows16, 0, unroll=True)

    for freq in range(2):
        one_freq(freq)


def unpack_kernel(home, out, angles, coded, turned, wide, sems):
    copies = []
    for part in range(4):
        block = home.at[:, pl.ds(part * 32, 32), :]
        copies.append(pltpu.make_async_copy(block, out.at[part % 2, part // 2], sems.at[part]))
    for copy in copies:
        copy.start()
    place = lax.broadcasted_iota(jnp.int32, (32, 128), 1) >> 5
    for half in range(2):
        rows = home[:, 128:136, half * 128 : half * 128 + 128].astype(F32)
        coded[0:128, :] = rows.reshape(128, 128)
        rows = [coded[pl.ds(r, 16, stride=8), :] for r in range(8)]
        flipped = jnp.concatenate(rows, axis=0).T
        for w in range(4):
            value = pltpu.roll(flipped[0:32], (4 - w) * 32 % 128, 1)
            for u in range(1, 4):
                part = pltpu.roll(flipped[32 * u : 32 * u + 32], (4 + u - w) * 32 % 128, 1)
                value = jnp.where(place == u, part, value)
            turned[pl.ds(half * 4 + w, 32, stride=8), :] = value
    for k in range(32):
        wide[:, k * 128 : k * 128 + 128] = turned[k * 8 : k * 8 + 8, :]
    copies.append(pltpu.make_async_copy(wide, angles, sems.at[4]))
    copies[4].start()
    for copy in copies:
        copy.wait()


FAR = pl.BlockSpec(memory_space=pltpu.HBM)
LOCAL = pl.BlockSpec(memory_space=pltpu.VMEM)
SCALAR = pl.BlockSpec(memory_space=pltpu.SMEM)


def near(value):
    return pltpu.with_memory_space_constraint(value, pltpu.VMEM)


def far(value):
    return pltpu.with_memory_space_constraint(value, pltpu.HBM)


def call(kernel, name, outs, out_specs, in_specs, scratch, mebibytes, args):
    return pl.pallas_call(
        kernel,
        in_specs=in_specs,
        out_specs=out_specs,
        out_shape=outs,
        scratch_shapes=scratch,
        compiler_params=pltpu.CompilerParams(vmem_limit_bytes=mebibytes * 2**20),
        name=name,
    )(*args)


def pack(receiver, source, weight):
    args = (
        far(receiver.reshape(2, 2, GROUP, 32, 256)),
        far(source.reshape(2, 2, GROUP, 32, 256)),
        far(weight.reshape(GROUP, 2, 16, 256)),
    )
    scratch = [pltpu.VMEM((GROUP, 2, 16, 256), jnp.int32), pltpu.SemaphoreType.DMA((9,))]
    outs = pltpu.VMEM((GROUP, 288, 256), BF16)
    return call(pack_kernel, "pack_fields", outs, LOCAL, [FAR] * 3, scratch, 12, args)


def prepare(omega, slowness, wedge_map, packed):
    outs = [
        pltpu.HBM((2, 2, 2, 1024, 128), F32),
        pltpu.VMEM((264, 128), F32),
        pltpu.HBM((32, 32, 128), F32),
    ]
    scale = jnp.asarray(tables()["phase_scale"])
    args = (omega, slowness, scale, wedge_map, near(packed))
    specs = [SCALAR] * 2 + [LOCAL] * 3
    scratch = [pltpu.VMEM((136, 128), F32)]
    return call(prepare_kernel, "prepare", outs, [LOCAL] * 3, specs, scratch, 16, args)


def cross_forward(packed):
    t = tables()
    args = [near(packed), near(jnp.asarray(t["cross_tw_fwd"])), jnp.asarray(t["cross_fwd"])]
    outs = pltpu.HBM((DEVICES, 64, 128), BF16)
    scratch = [
        pltpu.VMEM((256, 768), BF16),
        pltpu.VMEM((8, 4, 2, 32, 128), F32),
        pltpu.VMEM((3096, 128), F32),
        pltpu.VMEM((4, DEVICES, 16, 128), BF16),
        pltpu.SemaphoreType.DMA,
        pltpu.SemaphoreType.DMA((4, 2)),
    ]
    return call(
        cross_forward_kernel, "crossline_forward", outs, FAR, [LOCAL] * 2 + [FAR], scratch, 16, args
    )


def inline_step(lines, phase):
    t = tables()
    args = [far(lines), far(phase)]
    args += [near(jnp.asarray(t[n])) for n in ("inline_tw_fwd", "inline_tw_inv")]
    args += [jnp.asarray(t[n]) for n in ("inline_fwd", "inline_inv")]
    outs = pltpu.VMEM((DEVICES * MESSAGE, 128), BF16)
    scratch = [
        pltpu.VMEM((4, DEVICES, 16, 128), BF16),
        pltpu.VMEM((256, 256), BF16),
        pltpu.VMEM((256, 256), BF16),
        pltpu.VMEM((2, 2, 2, 1024, 128), F32),
        pltpu.VMEM((128, 2, 8, 128), F32),
        pltpu.VMEM((2, 1024, 256), F32),
        pltpu.VMEM((1024, 128), F32),
        pltpu.VMEM((144, 128), F32),
        pltpu.SemaphoreType.DMA((8,)),
    ]
    specs = [FAR, FAR, LOCAL, LOCAL, FAR, FAR]
    return call(inline_kernel, "inline_step", outs, LOCAL, specs, scratch, 20, args)


def cross_inverse(partial, wedges, share):
    t = tables()
    args = [near(partial), near(wedges), far(share), near(jnp.asarray(t["cross_tw_inv"]))]
    args.append(jnp.asarray(t["cross_inv"]))
    outs = pltpu.VMEM((GROUP, 136, 256), BF16)
    scratch = [
        pltpu.VMEM((512, 256), BF16),
        pltpu.VMEM((3096, 128), F32),
        pltpu.VMEM((4, 8, 2, 32, 128), F32),
        pltpu.VMEM((32, 2, 32, 128), BF16),
        pltpu.VMEM((32, 32, 128), F32),
        pltpu.SemaphoreType.DMA((2,)),
    ]
    return call(
        cross_inverse_kernel, "crossline_inverse", outs, LOCAL, [LOCAL, LOCAL, FAR, LOCAL, FAR], scratch, 16, args
    )


def unpack(home):
    outs = [
        pltpu.HBM((2, 2, GROUP, 32, 256), BF16),
        pltpu.HBM((8, SIZE), F32),
    ]
    scratch = [
        pltpu.VMEM((136, 128), F32),
        pltpu.VMEM((264, 128), F32),
        pltpu.VMEM((8, SIZE), F32),
        pltpu.SemaphoreType.DMA((5,)),
    ]
    specs = [FAR, FAR]
    return call(unpack_kernel, "unpack_fields", outs, specs, [LOCAL], scratch, 12, [near(home)])


def exchange(value, axes):
    return lax.all_to_all(value, axes, 0, 0, tiled=True)


def per_device(receiver, source, weight, omega, slowness, wedge_map):
    packed = exchange(pack(receiver, source, weight), LINE)
    phase, wedges, share = prepare(omega, slowness, wedge_map, packed)
    lines = exchange(cross_forward(packed), EVERY)
    partial = inline_step(lines, phase).reshape(DEVICES, MESSAGE // 2, 2, 128)
    partial = exchange(partial, EVERY).reshape(DEVICES * MESSAGE, 128)
    home = exchange(cross_inverse(partial, wedges, share), LINE)
    mixed, angles = unpack(home)
    return (mixed.reshape(2, 2, 512, 256), angles)


def solution(mesh):
    fine = Mesh(mesh.devices.reshape((2,) * 7), NAMES)
    return jax.shard_map(
        per_device,
        mesh=fine,
        in_specs=(
            P(None, None, ROWS, COLUMNS),
            P(None, None, ROWS, COLUMNS),
            P(ROWS, COLUMNS),
            P(),
            P(),
            P(),
        ),
        out_specs=(P(None, None, ROWS, COLUMNS), P()),
        check_vma=False,
    )
```
